32 devices in a mesh: bucket: 4 (over z), seq: 8 (over y, x, core).
Axes of the slice: x: 2, y: 2, z: 4, core: 2. Of those that a mesh axis runs over, the one named last changes fastest.
Arguments:
- frames: bfloat16 [4, 2048, 768], P('bucket', 'seq'), may hold values from -6 to 6
- w_qkv: bfloat16 [2, 768, 2304], replicated, may hold values from -0.21875 to 0.21875
- b_qv: float32 [2, 1536], replicated, may hold values from -3 to 3
- w_out: bfloat16 [2, 768, 768], replicated, may hold values from -0.875 to 0.875
- b_out: float32 [2, 768], replicated, may hold values from -3 to 3
- ln_gain: float32 [2, 2, 768], replicated, may hold values from 0.5 to 1.5
- ln_shift: float32 [2, 2, 768], replicated, may hold values from -3 to 3
- w_up: bfloat16 [2, 768, 3072], replicated, may hold values from -0.21875 to 0.21875
- b_up: float32 [2, 3072], replicated, may hold values from -3 to 3
- w_down: bfloat16 [2, 3072, 768], replicated, may hold values from -0.109375 to 0.109375
- b_down: float32 [2, 768], replicated, may hold values from -3 to 3
- cotangent: bfloat16 [4, 2048, 768], P('bucket', 'seq'), may hold values from -6 to 6
- clip_lengths: int32 [4, 8], P('bucket'), may hold values from 1 to 1917, as said below
- valid_lengths: int32 [4, 8], P('bucket'), may hold values from 1 to 1917, as said below
Outputs:
- activations: bfloat16 [4, 2048, 768], P('bucket', 'seq')
- input_grad: float32 [4, 2048, 768], P('bucket', 'seq')
- grad_w_qkv: float32 [2, 768, 2304], P(None, 'seq')
- grad_b_qv: float32 [2, 1536], P(None, 'seq')
- grad_w_out: float32 [2, 768, 768], P(None, 'seq')
- grad_b_out: float32 [2, 768], P(None, 'seq')
- grad_ln_gain: float32 [2, 2, 768], P(None, None, 'seq')
- grad_ln_shift: float32 [2, 2, 768], P(None, None, 'seq')
- grad_w_up: float32 [2, 768, 3072], P(None, 'seq')
- grad_b_up: float32 [2, 3072], P(None, 'seq')
- grad_w_down: float32 [2, 3072, 768], P(None, 'seq')
- grad_b_down: float32 [2, 768], P(None, 'seq')
The draws below stay inside these ranges and needn't reach their ends.
Inputs may be any that keep to these rules, and one draw needn't show every extreme that they name: `clip_lengths`: the 8 lengths of a bucket sum to 2048; in every bucket one clip has exactly 1917 frames and runs from the first device of seq to the last; the others have at most 33 frames each. `valid_lengths`: at most the clip's length; the longest clip of a bucket has no padding.
All inputs are finite; a program needn't handle non-finite values.
Results may differ from the reference program's by a relative error of at most 0.038.
Values may be sent and summed in bfloat16 or wider, within the bound.
No kernel may reach another device: no remote copies, remote signals or barrier semaphores. Data moves between devices by JAX's collectives and lax.ppermute only.
A program may use at most 256 MiB of HBM per device.

```python
import math
import jax
import jax.numpy as jnp
from jax import lax

D = 768
HEADS = 12
HEAD_DIM = 64
FF = 3072
LAYERS = 2
CLIPS = 8
TOK_DEV = 256
BUCKETS = 4
FRAMES = 2048


def clip_table(key):
    first, second, third = jax.random.split(key, 3)
    short_most = TOK_DEV // CLIPS
    chosen = jax.random.randint(second, (BUCKETS, 1), 0, CLIPS)
    labels = jnp.arange(CLIPS, dtype=jnp.int32)[None, :]
    is_long = labels == chosen
    rank = labels - (labels > chosen).astype(jnp.int32)
    halves = jax.random.randint(first, (BUCKETS, CLIPS), 1, short_most + 1)
    paired = jnp.take_along_axis(halves, rank // 2, axis=1)
    lonely = (rank == CLIPS - 2) & ((CLIPS - 1) % 2 == 1)
    short = jnp.where(rank % 2 == 0, paired, short_most + 1 - paired)
    short = jnp.where(lonely, short_most, short)
    others = jnp.sum(jnp.where(is_long, 0, short), axis=1, keepdims=True)
    lengths = jnp.where(is_long, FRAMES - others, short).astype(jnp.int32)
    padding_most = jnp.where(is_long, 0, lengths // 4)
    padding = jax.random.randint(third, (BUCKETS, CLIPS), 0, padding_most + 1)
    return (lengths, (lengths - padding).astype(jnp.int32))


def draw_clip_lengths(key, part):
    table = clip_table(key)
    return table[0]


def draw_valid_lengths(key, part):
    table = clip_table(key)
    return table[1]


def block_levels(stream_key, extent, shards, low, high):
    loudness = 1.0
    for dim, parts in shards:
        heights = jax.random.uniform(jax.random.fold_in(jax.random.fold_in(stream_key, 6), dim), (parts,), jnp.float32, low / len(shards), high / len(shards))
        loudness = loudness * jnp.repeat(jnp.exp(heights), extent[dim] // parts).reshape((-1,) + (1,) * (len(extent) - 1 - dim))
    return loudness


def bell_draw(key, shape, scale, bound, shards=(), kind=jnp.bfloat16):
    entries = scale * jax.random.normal(key, shape, jnp.float32)
    if shards:
        entries = entries * block_levels(key, shape, shards, -0.22, 0.18)
    return jnp.clip(entries, -bound, bound).astype(kind)


def setup_inputs(seed: int = 0) -> dict:
    splits = jax.random.split(jax.random.key(seed), 15)
    return {
        "frames": bell_draw(splits[0], (BUCKETS, FRAMES, D), 1.0, 6.0, ((0, 4), (1, 8))),
        "w_qkv": bell_draw(splits[1], (LAYERS, D, 3 * D), D ** -0.5, 0.21875),
        "b_qv": bell_draw(splits[2], (LAYERS, 2 * D), 0.5, 3.0, (), jnp.float32),
        "w_out": bell_draw(splits[3], (LAYERS, D, D), (D // 16) ** -0.5, 0.875),
        "b_out": bell_draw(splits[4], (LAYERS, D), 0.5, 3.0, (), jnp.float32),
        "ln_gain": jnp.clip(1.0 + 0.1 * jax.random.normal(splits[5], (LAYERS, 2, D), jnp.float32), 0.5, 1.5),
        "ln_shift": bell_draw(splits[6], (LAYERS, 2, D), 0.5, 3.0, (), jnp.float32),
        "w_up": bell_draw(splits[7], (LAYERS, D, FF), D ** -0.5, 0.21875),
        "b_up": bell_draw(splits[8], (LAYERS, FF), 0.5, 3.0, (), jnp.float32),
        "w_down": bell_draw(splits[9], (LAYERS, FF, D), FF ** -0.5, 0.109375),
        "b_down": bell_draw(splits[10], (LAYERS, D), 0.5, 3.0, (), jnp.float32),
        "cotangent": bell_draw(splits[11], (BUCKETS, FRAMES, D), 1.0, 6.0, ((0, 4), (1, 8))),
        "clip_lengths": draw_clip_lengths(jax.random.fold_in(splits[14], 71), 0),
        "valid_lengths": draw_valid_lengths(jax.random.fold_in(splits[14], 71), 0),
    }


@jax.custom_vjp
def low(v):
    return lax.optimization_barrier(v.astype(jnp.bfloat16)).astype(jnp.float32)

@jax.custom_vjp
def low_back(v):
    return v

def low_keep(v):
    return (low(v), None)

def low_pass(kept, grad):
    return (grad,)

def back_keep(v):
    return (v, None)

def back_low(kept, grad):
    return (low(grad),)
low.defvjp(low_keep, low_pass)
low_back.defvjp(back_keep, back_low)

def clip_tags(lengths, valid, begin, count):
    position = begin + jnp.arange(count, dtype=jnp.int32)
    ends = jnp.cumsum(lengths).astype(jnp.int32)
    starts = ends - lengths
    inside = (position[:, None] >= starts[None, :]) & (position[:, None] < ends[None, :])
    labels = jnp.arange(lengths.shape[0], dtype=jnp.int32)
    segment = lax.optimization_barrier(jnp.sum(jnp.where(inside, labels[None, :], 0), axis=1)).astype(jnp.int32)
    live = jnp.any(inside & (position[:, None] < (starts + valid)[None, :]), axis=1)
    return (segment, jnp.where(live, segment, -1).astype(jnp.int32))

def layer_norm(hidden, gain, shift):
    center = hidden - lax.optimization_barrier(jnp.mean(hidden, axis=-1, keepdims=True))
    spread = lax.optimization_barrier(jnp.mean(center * center, axis=-1, keepdims=True))
    return center * lax.rsqrt(spread + 1e-05) * gain + shift

def attend(queries, keys, values, segment, key_tag):
    scale = HEAD_DIM ** (-0.5)
    block = math.gcd(FRAMES, 512)
    highest = lax.Precision.HIGHEST
    query_heads = queries.reshape(FRAMES, HEADS, HEAD_DIM)
    key_heads = keys.reshape(FRAMES, HEADS, HEAD_DIM)
    value_heads = values.reshape(FRAMES, HEADS, HEAD_DIM)

    def one_block(block_at):
        query_block = lax.dynamic_slice_in_dim(query_heads, block_at * block, block, 0)
        seg_block = lax.dynamic_slice_in_dim(segment, block_at * block, block, 0)
        scores = low_back(jnp.einsum('qhd,khd->hqk', query_block, key_heads, precision=highest) * scale)
        allowed = (seg_block[:, None] == key_tag[None, :])[None]
        probs = low(jax.nn.softmax(jnp.where(allowed, scores, -1e+30), axis=-1))
        result = jnp.einsum('hqk,khd->qhd', probs, value_heads, precision=highest)
        return result.reshape(block, HEADS * HEAD_DIM)
    blocks = lax.map(jax.checkpoint(one_block), jnp.arange(FRAMES // block, dtype=jnp.int32))
    return blocks.reshape(FRAMES, HEADS * HEAD_DIM)

def one_layer(weights, hidden, segment, key_tag):
    w_qkv, b_qv, w_out, b_out, gain, shift, w_up, b_up, w_down, b_down = weights
    highest = lax.Precision.HIGHEST
    inputs = low(hidden)
    projected = jnp.dot(inputs, w_qkv, precision=highest)
    queries = low_back(low(projected[:, :D] + b_qv[:D]))
    keys = low_back(low(projected[:, D:2 * D]))
    values = low_back(low(projected[:, 2 * D:] + b_qv[D:]))
    attended = low_back(low(attend(queries, keys, values, segment, key_tag)))
    branch = low_back(jnp.dot(attended, w_out, precision=highest) + b_out)
    normed = low(layer_norm(inputs + branch, gain[0], shift[0]))
    up_pre = low_back(jnp.dot(normed, w_up, precision=highest) + b_up)
    activated = low(jax.nn.gelu(up_pre, approximate=False))
    down = low_back(jnp.dot(activated, w_down, precision=highest) + b_down)
    return layer_norm(normed + down, gain[1], shift[1])

def forward(params, hidden, segment, key_tag):
    for layer_at in range(LAYERS):
        weights = tuple((array[layer_at] for array in params))
        hidden = one_layer(weights, hidden, segment, key_tag)
    return hidden

def reference(frames, w_qkv, b_qv, w_out, b_out, ln_gain, ln_shift, w_up, b_up, w_down, b_down, cotangent, clip_lengths, valid_lengths):
    params = tuple((array.astype(jnp.float32) for array in (w_qkv, b_qv, w_out, b_out, ln_gain, ln_shift, w_up, b_up, w_down, b_down)))

    def per_bucket(running, item):
        frame_rows, cot_rows, lengths, valid = item
        segment, key_tag = clip_tags(lengths, valid, 0, FRAMES)
        result, pull = jax.vjp(lambda weights, hidden: forward(weights, hidden, segment, key_tag), params, frame_rows.astype(jnp.float32))
        grads, grad_frames = pull(cot_rows.astype(jnp.float32))
        running = jax.tree.map(jnp.add, running, grads)
        return (running, (result.astype(jnp.bfloat16), grad_frames))
    start_grads = jax.tree.map(jnp.zeros_like, params)
    summed, (activations, input_grad) = lax.scan(per_bucket, start_grads, (frames, cotangent, clip_lengths, valid_lengths))
    return (activations, input_grad, summed[0], summed[1], summed[2], summed[3], summed[4], summed[5], summed[6], summed[7], summed[8], summed[9])
```

```python
import functools
import math

import jax
import jax.numpy as jnp
from jax import lax
from jax.experimental import pallas as pl
from jax.experimental.pallas import tpu as pltpu
from jax.sharding import PartitionSpec as P

HEADS = 12
LAYERS = 2
BF = jnp.bfloat16
F32 = jnp.float32
LOW = -1e30
SLACK = 8 * 1024 * 1024


def dot_nn(a, b):
    return lax.dot_general(a, b, (((1,), (0,)), ((), ())), preferred_element_type=F32)


def dot_nt(a, b):
    return lax.dot_general(a, b, (((1,), (1,)), ((), ())), preferred_element_type=F32)


def block_bytes(spec, array):
    lanes = [n for n in spec.block_shape if n is not None]
    lanes[-1] += -lanes[-1] % 128
    return math.prod(lanes) * array.dtype.itemsize


def call(body, name, out_shape, in_specs, out_specs, grid, scratch, flops, args, scalars):
    out_bytes = sum(s.size * s.dtype.itemsize for s in jax.tree.leaves(out_shape))
    need = sum(block_bytes(p, a) for p, a in zip(in_specs, args))
    need += sum(block_bytes(p, a) for p, a in zip(jax.tree.leaves(out_specs), jax.tree.leaves(out_shape)))
    need = 2 * need + sum(math.prod(m.shape) * jnp.dtype(m.dtype).itemsize for m in scratch)
    return pl.pallas_call(
        body,
        name=name,
        out_shape=out_shape,
        grid_spec=pltpu.PrefetchScalarGridSpec(
            num_scalar_prefetch=1,
            grid=grid,
            in_specs=in_specs,
            out_specs=out_specs,
            scratch_shapes=scratch,
        ),
        compiler_params=pltpu.CompilerParams(vmem_limit_bytes=need + SLACK),
        cost_estimate=pl.CostEstimate(
            flops=int(flops), bytes_accessed=int(out_bytes * 3), transcendentals=0
        ),
    )(scalars, *args)


def whole(shape):
    return pl.BlockSpec(shape, lambda i, s: (0,) * len(shape))


def sds(shape, dtype=BF):
    return jax.ShapeDtypeStruct(shape, dtype)


def attend_kernel(layer, chips, first, last, *refs):
    refs = list(refs)
    refs.pop(0)
    if not first:
        qt_in, acc_in, m_in = refs.pop(0), refs.pop(0), refs.pop(0)
    seg_ref, bias_ref, wk_ref, wv_ref = (refs.pop(0) for _ in range(4))
    if first:
        wq_ref = refs.pop(0)
    bias_k = refs.pop(0)
    xs = [refs.pop(0) for _ in range(2 * chips)]
    tags = [refs.pop(0) for _ in range(2 * chips)]
    kvs = [refs.pop(0) for _ in range(chips)]
    if first:
        q_out, qt_out = refs.pop(0), refs.pop(0)
    if last:
        att_ref, ot_ref, lse_ref = refs.pop(0), refs.pop(0), refs.pop(0)
    else:
        acc_out, m_out = refs.pop(0), refs.pop(0)
    s_scr, vt_scr = refs.pop(0), refs.pop(0)
    rows = xs[0].shape[0]
    half = wk_ref.shape[1]
    heads = half // 64
    queries = seg_ref.shape[1]
    high = vt_scr.shape[1]
    pair = 2 * rows
    bias_q = bias_ref[layer : layer + 1, :]
    bias_v = bias_k[layer : layer + 1, :]
    for c in range(chips):
        x = jnp.concatenate([xs[2 * c][...], xs[2 * c + 1][...]], axis=0)
        if first:
            q = (dot_nn(x, wq_ref[...]) + bias_q).astype(BF) * BF(0.125)
            q_out[...] = q
            qt_out[...] = q.T
        kvs[c][:, :half] = dot_nn(x, wk_ref[...]).astype(BF)
        values = (dot_nn(x, wv_ref[...]) + bias_v).astype(BF)
        kvs[c][:, half:] = values
        turned = values.T
        for h in range(heads):
            vt_scr[h, :64, c * pair : (c + 1) * pair] = turned[h * 64 : (h + 1) * 64]
    vt_scr[:, 64:, :] = jnp.ones((heads, high - 64, chips * pair), BF)
    qt = qt_out if first else qt_in
    seg = seg_ref[...]
    outs = []
    if last:
        lse_ref[...] = jnp.zeros_like(lse_ref)
    else:
        m_out[...] = jnp.zeros_like(m_out)
    for h in range(heads):
        qh = qt[h * 64 : (h + 1) * 64, :]
        m8 = None
        for b in range(2 * chips):
            key = slice((b % 2) * rows, (b % 2 + 1) * rows)
            scores = dot_nn(kvs[b // 2][key, h * 64 : (h + 1) * 64], qh)
            ok = jnp.concatenate([tags[b][...]] * (queries // 128), axis=1) == seg
            scores = jnp.where(ok, scores, LOW)
            s_scr[h % 2, b * rows : (b + 1) * rows, :] = scores
            top = jnp.max(scores.reshape(rows // 8, 8, queries), axis=0)
            m8 = top if m8 is None else jnp.maximum(m8, top)
        m = jnp.max(m8, axis=0, keepdims=True)
        if not first:
            m_old = m_in[h : h + 1, :]
            m = jnp.maximum(m, m_old)
        acc = jnp.zeros((high, queries), F32)
        for b in range(2 * chips):
            probs = jnp.exp(s_scr[h % 2, b * rows : (b + 1) * rows, :] - m).astype(BF)
            acc = acc + dot_nn(vt_scr[h, :, b * rows : (b + 1) * rows], probs)
        if not first:
            acc = acc + acc_in[h] * jnp.exp(m_old - m)
        if last:
            total = acc[64:65]
            out = acc[:64] / total
            ot_ref[h * 64 : (h + 1) * 64, :] = out
            lse_ref[h : h + 1, :] = m + jnp.log(total)
            outs.append(out.astype(BF))
        else:
            acc_out[h] = acc
            m_out[h : h + 1, :] = m
    if last:
        att_ref[...] = jnp.concatenate(outs, axis=0).T


def tag_specs(tag_ids, rows):
    return [pl.BlockSpec((None, rows, 128), lambda i, s, r=r: (r, 0, 0)) for r in tag_ids]


def attend_call(layer, scal, state, seg_row, w_qkv, b_qv, xs, tags, tag_ids, last=False):
    first = not state
    rows, width = xs[0].shape
    half = width // 2
    heads = half // 64
    queries = 2 * rows
    chips = len(xs) // 2
    high = 80
    stat = sds((8, queries), F32)
    out_shape = tuple(sds((2 * rows, width)) for _ in range(chips))
    if first:
        out_shape += (sds((queries, half)), sds((half, queries)))
    if last:
        out_shape += (sds((queries, half)), sds((half, queries), F32), stat)
    else:
        out_shape += (sds((heads, high, queries), F32), stat)

    def weight(part):
        return pl.BlockSpec((None, width, half), lambda i, s: (layer, 0, 2 * part + s[0] % 2))

    def bias(part):
        return pl.BlockSpec((LAYERS, half), lambda i, s: (0, 2 * part + s[0] % 2))

    specs = [whole(a.shape) for a in state] + [whole(seg_row.shape), bias(0), weight(1), weight(2)]
    args = tuple(state) + (seg_row, b_qv, w_qkv, w_qkv)
    if first:
        specs.append(weight(0))
        args += (w_qkv,)
    specs += [bias(1)] + [whole(x.shape) for x in xs] + tag_specs(tag_ids, rows)
    args += (b_qv,) + tuple(xs) + (tags,) * len(xs)
    return call(
        functools.partial(attend_kernel, layer, chips, first, last),
        "attend",
        out_shape,
        specs,
        tuple(whole(o.shape) for o in out_shape),
        (1,),
        [
            pltpu.VMEM((2, chips * 2 * rows, queries), F32),
            pltpu.VMEM((heads, high, chips * 2 * rows), BF),
        ],
        chips * 12 * 4 * queries * half * rows,
        args,
        scal,
    )


def attend_back_kernel(blocks, adds, first, last, *refs):
    refs = list(refs)
    refs.pop(0)
    if first:
        b_m, b_o, w_out, ot_ref = (refs.pop(0) for _ in range(4))
    else:
        do_in, dot_in, corr_in, dq_in = (refs.pop(0) for _ in range(4))
    q, qt, lse_ref, seg_ref = (refs.pop(0) for _ in range(4))
    kvs = [refs.pop(0) for _ in range(blocks)]
    more = [refs.pop(0) for _ in range(blocks)] if adds else None
    tags = [refs.pop(0) for _ in range(blocks)]
    outs = [refs.pop(0) for _ in range(blocks)]
    if first:
        do_out, dot_out, corr_out, dq_out = (refs.pop(0) for _ in range(4))
    else:
        dq_out = refs.pop(0)
    dqt_scr = refs.pop(0)
    rows, width = kvs[0].shape
    half = width // 2
    heads = half // 64
    seg = seg_ref[...]
    queries = seg.shape[1]
    if first:
        branch = jnp.concatenate([b_m[...], b_o[...]], axis=0)
        grad_att = dot_nt(branch, w_out[...]).astype(BF)
        do_out[...] = grad_att
        turned = grad_att.T
        dot_out[...] = turned
        wide = turned.astype(F32) * ot_ref[...]
        corr_out[...] = jnp.zeros_like(corr_out)
        for h in range(heads):
            corr_out[h : h + 1, :] = jnp.sum(wide[h * 64 : (h + 1) * 64], axis=0, keepdims=True)
        do, dot, corr = do_out, dot_out, corr_out
    else:
        do, dot, corr = do_in, dot_in, corr_in
    for b in range(blocks):
        kt = kvs[b][:, :half].T
        ok = jnp.concatenate([tags[b][...]] * (queries // 128), axis=1) == seg
        dks, dvs = [], []
        for h in range(heads):
            sl = slice(h * 64, (h + 1) * 64)
            vl = slice(half + h * 64, half + (h + 1) * 64)
            scores = dot_nn(kvs[b][:, sl], qt[sl, :])
            grad = dot_nn(kvs[b][:, vl], dot[sl, :])
            probs = jnp.exp(jnp.where(ok, scores - lse_ref[h : h + 1, :], LOW))
            grad = (probs * (grad - corr[h : h + 1, :])).astype(BF)
            probs = probs.astype(BF)
            term = dot_nn(kt[sl], grad)
            if b == 0:
                if first:
                    dqt_scr[sl, :] = term
                else:
                    dqt_scr[sl, :] = dq_in[sl, :] + term
            else:
                dqt_scr[sl, :] += term
            dks.append(dot_nn(grad, q[:, sl]))
            dvs.append(dot_nn(probs, do[:, sl]))
        result = jnp.concatenate(dks + dvs, axis=1)
        if adds:
            result = result + more[b][...].astype(F32)
        outs[b][...] = result.astype(BF)
    if last:
        dq_out[...] = (dqt_scr[...] * 0.125).astype(BF).T
    else:
        dq_out[...] = dqt_scr[...]


def attend_back_call(layer, scal, state, w_out, shared, kvs, adds, tags, tag_ids, last=False):
    first = w_out is not None
    rows = kvs[0].shape[0] // 2
    width = kvs[0].shape[1]
    half = width // 2
    queries = 2 * rows
    blocks = len(kvs)
    out_shape = tuple(sds((rows, width)) for _ in range(blocks))
    if first:
        out_shape += (sds((queries, half)), sds((half, queries)), sds((8, queries), F32))
    out_shape += (sds((queries, half)) if last else sds((half, queries), F32),)
    args, specs = tuple(state), [whole(a.shape) for a in state]
    if first:
        args = args[:2] + (w_out,) + args[2:]
        specs.insert(
            2, pl.BlockSpec((None, half, width), lambda i, s: (layer, s[0] % 2, 0))
        )
    args += tuple(shared) + tuple(kvs) + tuple(adds or ())
    specs += [whole(a.shape) for a in shared]
    specs += [pl.BlockSpec((rows, width), lambda i, s, r=r: (r % 2, 0)) for r in tag_ids]
    specs += [whole(a.shape) for a in adds or ()] + tag_specs(tag_ids, rows)
    return call(
        functools.partial(attend_back_kernel, blocks, adds is not None, first, last),
        "attend_back",
        out_shape,
        specs,
        tuple(whole(o.shape) for o in out_shape),
        (1,),
        [pltpu.VMEM((half, queries), F32)],
        10 * 4 * queries * half * rows * blocks,
        args + (tags,) * blocks,
        scal,
    )


def normalize(hidden):
    center = hidden - jnp.mean(hidden, axis=-1, keepdims=True)
    spread = lax.rsqrt(jnp.mean(center * center, axis=-1, keepdims=True) + 1e-05)
    return center * spread, spread


def normalize_back(grad, unit, spread, gain):
    scaled = grad * gain
    mean = jnp.mean(scaled, axis=-1, keepdims=True)
    along = jnp.mean(scaled * unit, axis=-1, keepdims=True)
    return spread * (scaled - mean - unit * along)


def gauss(up):
    size = jnp.abs(up)
    bell = jnp.exp(-0.5 * up * up)
    t = 1.0 / (1.0 + 0.23164189 * size)
    poly = 0.5307027145 * t - 0.7265760135
    poly = poly * t + 0.7107068705
    poly = poly * t - 0.142248368
    poly = poly * t + 0.127414796
    tail = poly * t * bell
    return jnp.where(up < 0, tail, 1.0 - tail), bell


def ffn_kernel(
    layer, s, x, att, oatt, w_out, b_out, gain, shift, w_up, b_up, w_down, b_down,
    unit1, rs1, normed, act, slope, unit2, rs2, y, total,
):
    n = pl.program_id(0)
    rows = x.shape[0]
    half = att.shape[1]
    core = s[0] % 2

    @pl.when(n == 0)
    def _():
        mine = pl.multiple_of(core * half, 128)
        other = pl.multiple_of((1 - core) * half, 128)
        branch = dot_nn(att[:rows], w_out[pl.ds(mine, half), :])
        branch = branch + dot_nn(oatt[rows:], w_out[pl.ds(other, half), :])
        first = x[...].astype(F32) + branch + b_out[layer : layer + 1, :]
        unit, spread = normalize(first)
        unit1[...] = unit
        rs1[...] = jnp.broadcast_to(spread, rs1.shape)
        low = (unit * gain[layer, 0:1, :] + shift[layer, 0:1, :]).astype(BF)
        normed[...] = low
        total[...] = low.astype(F32) + b_down[layer : layer + 1, :]

    up = dot_nn(normed[...], w_up[...]) + b_up[layer : layer + 1, :]
    phi, bell = gauss(up)
    low = (up * phi).astype(BF)
    act[...] = low
    slope[...] = (phi + up * (0.3989422804014327 * bell)).astype(BF)
    total[...] += dot_nn(low, w_down[...])

    @pl.when(n == pl.num_programs(0) - 1)
    def _():
        unit, spread = normalize(total[...])
        unit2[...] = unit
        rs2[...] = jnp.broadcast_to(spread, rs2.shape)
        y[...] = (unit * gain[layer, 1:2, :] + shift[layer, 1:2, :]).astype(BF)


def ffn_call(layer, scal, x, att, oatt, w_out, b_out, gain, shift, w_up, b_up, w_down, b_down):
    rows, width = x.shape
    wide = w_up.shape[2]
    steps = wide // width
    vec = sds((rows, 128), F32)
    out_shape = (
        sds((rows, width), F32), vec, sds((rows, width)), sds((rows, wide)), sds((rows, wide)),
        sds((rows, width), F32), vec, sds((rows, width)),
    )
    strip = pl.BlockSpec((rows, width), lambda n, s: (0, n))
    return call(
        functools.partial(ffn_kernel, layer),
        "ffn",
        out_shape,
        [
            whole(x.shape), whole(att.shape), whole(oatt.shape),
            pl.BlockSpec((None, width, width), lambda n, s: (layer, 0, 0)),
            whole(b_out.shape), whole(gain.shape), whole(shift.shape),
            pl.BlockSpec((None, width, width), lambda n, s: (layer, 0, n)),
            pl.BlockSpec((LAYERS, width), lambda n, s: (0, n)),
            pl.BlockSpec((None, width, width), lambda n, s: (layer, n, 0)),
            whole(b_down.shape),
        ],
        (
            whole((rows, width)), whole((rows, 128)), whole((rows, width)), strip, strip,
            whole((rows, width)), whole((rows, 128)), whole((rows, width)),
        ),
        (steps,),
        [pltpu.VMEM((rows, width), F32)],
        4 * rows * width * wide + 2 * rows * width * width,
        (x, att, oatt, w_out, b_out, gain, shift, w_up, b_up, w_down, b_down),
        scal,
    )


def ffn_back_kernel(
    layer, s, gy, unit2, rs2, slope, unit1, rs1, gain, w_up, w_down,
    d_down, d_up, d_branch, d_first, sums, total,
):
    n = pl.program_id(0)

    @pl.when(n == 0)
    def _():
        grad = gy[...].astype(F32)
        unit = unit2[...]
        second = normalize_back(grad, unit, rs2[:, 0:1], gain[layer, 1:2, :])
        sums[...] = jnp.zeros_like(sums)
        sums[1:2, :] = jnp.sum(grad * unit, axis=0, keepdims=True)
        sums[3:4, :] = jnp.sum(grad, axis=0, keepdims=True)
        total[...] = second
        low = second.astype(BF)
        d_down[...] = low
        sums[5:6, :] = jnp.sum(low.astype(F32), axis=0, keepdims=True)

    low = (dot_nt(d_down[...], w_down[...]) * slope[...].astype(F32)).astype(BF)
    d_up[...] = low
    sums[pl.ds(6 + n, 1), :] = jnp.sum(low.astype(F32), axis=0, keepdims=True)
    total[...] += dot_nt(low, w_up[...])

    @pl.when(n == pl.num_programs(0) - 1)
    def _():
        grad = total[...]
        unit = unit1[...]
        first = normalize_back(grad, unit, rs1[:, 0:1], gain[layer, 0:1, :])
        sums[0:1, :] = jnp.sum(grad * unit, axis=0, keepdims=True)
        sums[2:3, :] = jnp.sum(grad, axis=0, keepdims=True)
        d_first[...] = first
        low = first.astype(BF)
        d_branch[...] = low
        sums[4:5, :] = jnp.sum(low.astype(F32), axis=0, keepdims=True)


def ffn_back_call(layer, scal, gy, unit2, rs2, slope, unit1, rs1, gain, w_up, w_down):
    rows, width = gy.shape
    wide = w_up.shape[2]
    steps = wide // width
    low = sds((rows, width))
    out_shape = (low, sds((rows, wide)), low, sds((rows, width), F32), sds((16, width), F32))
    strip = pl.BlockSpec((rows, width), lambda n, s: (0, n))
    out_specs = [whole(o.shape) for o in out_shape]
    out_specs[1] = strip
    return call(
        functools.partial(ffn_back_kernel, layer),
        "ffn_back",
        out_shape,
        [
            whole(gy.shape), whole(unit2.shape), whole(rs2.shape), strip,
            whole(unit1.shape), whole(rs1.shape), whole(gain.shape),
            pl.BlockSpec((None, width, width), lambda n, s: (layer, 0, n)),
            pl.BlockSpec((None, width, width), lambda n, s: (layer, n, 0)),
        ],
        tuple(out_specs),
        (steps,),
        [pltpu.VMEM((rows, width), F32)],
        4 * rows * width * wide,
        (gy, unit2, rs2, slope, unit1, rs1, gain, w_up, w_down),
        scal,
    )


def input_back_kernel(s, d_first, dq, dkv, odq, odkv, w, gx):
    rows = d_first.shape[0]
    half = dq.shape[1]
    width = 2 * half
    core = s[0] % 2
    result = d_first[...]
    for at, q_part, kv_part in (
        (core * half, dq[:rows], dkv),
        ((1 - core) * half, odq[rows:], odkv),
    ):
        for i, part in enumerate((q_part, kv_part[:, :half], kv_part[:, half:])):
            columns = pl.ds(pl.multiple_of(i * width + at, 128), half)
            result = result + dot_nt(part, w[:, columns])
    gx[...] = result


def input_back_call(layer, scal, d_first, dq, dkv, odq, odkv, w_qkv):
    rows, width = d_first.shape
    strip = pl.BlockSpec((rows, 256), lambda n, s: (0, n))
    return call(
        input_back_kernel,
        "input_back",
        sds((rows, width), F32),
        [
            strip, whole(dq.shape), whole(dkv.shape), whole(odq.shape), whole(odkv.shape),
            pl.BlockSpec((None, 256, 3 * width), lambda n, s: (layer, n, 0)),
        ],
        strip,
        (width // 256,),
        [],
        6 * rows * width * width,
        (d_first, dq, dkv, odq, odkv, w_qkv),
        scal,
    )


def gather_rows(s, turned, picked, order):
    chip, core = s[0] // 2, s[0] % 2
    share = picked.shape[0] // len(order)
    for at, step in enumerate(order):
        begin = pl.multiple_of((chip ^ step) * (2 * share) + core * share, 32)
        picked[at * share : (at + 1) * share, :] = turned[pl.ds(begin, share), :]


def up_grad_kernel(s, x_m, x_o, g_m, g_o, keep, send, turned, picked):
    rows = x_m.shape[0]

    @pl.when(pl.program_id(0) == 0)
    def _():
        turned[:, :rows] = x_m[...].T
        turned[:, rows:] = x_o[...].T
        gather_rows(s, turned, picked, (0, 2, 1, 3))

    grad = dot_nn(picked[:, :rows], g_m[...]) + dot_nn(picked[:, rows:], g_o[...])
    share = picked.shape[0] // 4
    for at in range(2):
        keep[at] = grad[at * share : (at + 1) * share].astype(BF)
        send[at] = grad[(2 + at) * share : (3 + at) * share].astype(BF)


def up_grad_call(scal, x_m, x_o, g_m, g_o):
    rows, width = x_m.shape
    wide = g_m.shape[1]
    steps = wide // width
    share = width // 8
    out = sds((2, steps * share, width))
    strip = pl.BlockSpec((rows, width), lambda n, s: (0, n))
    block = pl.BlockSpec((2, share, width), lambda n, s: (0, n, 0))
    return call(
        up_grad_kernel,
        "up_grad",
        (out, out),
        [whole(x_m.shape), whole(x_o.shape), strip, strip],
        (block, block),
        (steps,),
        [pltpu.VMEM((width, 2 * rows), BF), pltpu.VMEM((width // 2, 2 * rows), BF)],
        2 * rows * width * wide,
        (x_m, x_o, g_m, g_o),
        scal,
    )


def down_grad_kernel(s, a_m, a_o, g_m, g_o, keep, send):
    n = pl.program_id(0)
    grad = dot_nn(a_m[...].T, g_m[...]) + dot_nn(a_o[...].T, g_o[...])
    grad = grad.astype(BF)

    @pl.when(n < 2)
    def _():
        keep[...] = grad

    @pl.when(n >= 2)
    def _():
        send[...] = grad


def down_grad_call(scal, a_m, a_o, g_m, g_o):
    rows, wide = a_m.shape
    width = g_m.shape[1]
    share = wide // 8
    out = sds((2, share, width))
    picked = pl.BlockSpec((rows, share), lambda n, s: (0, 2 * ((s[0] // 2) ^ n) + s[0] % 2))
    return call(
        down_grad_kernel,
        "down_grad",
        (out, out),
        [picked, picked, whole(g_m.shape), whole(g_o.shape)],
        (
            pl.BlockSpec((None, share, width), lambda n, s: (jnp.minimum(n, 1), 0, 0)),
            pl.BlockSpec((None, share, width), lambda n, s: (jnp.maximum(n - 2, 0), 0, 0)),
        ),
        (4,),
        [],
        2 * rows * width * wide,
        (a_m, a_o, g_m, g_o),
        scal,
    )


def out_grad_kernel(
    s, x_m, x_o, dq, dkv_m, dkv_r, odq, odkv_m, odkv_r, att, oatt, b_m, b_o, sums_m, sums_o,
    keep_a, send_a, keep_b, send_b, turned, picked,
):
    rows, width = x_m.shape
    half = width // 2
    core = s[0] % 2
    share = width // 8
    mine = pl.ds(pl.multiple_of(core * half, 128), half)
    other = pl.ds(pl.multiple_of((1 - core) * half, 128), half)
    turned[:, :rows] = x_m[...].T
    turned[:, rows:] = x_o[...].T
    gather_rows(s, turned, picked, (0, 2, 1, 3))
    left_m, left_o = picked[:, :rows], picked[:, rows:]

    def put(refs, order, at, grad, columns):
        for j in range(4):
            place = order.index(j)
            ref = refs[place // 2]
            ref[place % 2, at * share : (at + 1) * share, columns] = grad[
                (0, 2, 1, 3).index(j) * share : ((0, 2, 1, 3).index(j) + 1) * share
            ].astype(BF)

    first, second = (0, 2, 1, 3), (0, 1, 2, 3)
    refs_a, refs_b = (keep_a, send_a), (keep_b, send_b)
    for at, refs, order, place in (
        (0, refs_a, first, 0),
        (1, refs_a, first, 1),
        (2, refs_b, second, 0),
    ):
        if at == 0:
            pairs = ((dq[:rows], dq[rows:]), (odq[rows:], odq[:rows]))
        else:
            cut = slice((at - 1) * half, at * half)
            pairs = ((dkv_m[:, cut], dkv_r[:, cut]), (odkv_r[:, cut], odkv_m[:, cut]))
        for columns, (mine_rows, other_rows) in zip((mine, other), pairs):
            grad = dot_nn(left_m, mine_rows) + dot_nn(left_o, other_rows)
            put(refs, order, place, grad, columns)
    turned[mine, :] = att[...].T
    turned[other, :rows] = oatt[rows:].T
    turned[other, rows:] = oatt[:rows].T
    gather_rows(s, turned, picked, (0, 2, 1, 3))
    grad = dot_nn(picked[:, :rows], b_m[...]) + dot_nn(picked[:, rows:], b_o[...])
    put(refs_b, second, 1, grad, slice(0, width))
    small = (sums_m[...] + sums_o[...]).astype(BF)
    for ref in (keep_a, send_a, keep_b, send_b):
        for at in range(2):
            ref[at, 2 * share :, :] = small
    for row, parts in ((10, (dq[...], odq[...])), (11, (dkv_m[:, half:], dkv_r[:, half:], odkv_m[:, half:], odkv_r[:, half:]))):
        count = len(parts) // 2
        for columns, group in ((mine, parts[:count]), (other, parts[count:])):
            line = sum(jnp.sum(p.astype(F32), axis=0, keepdims=True) for p in group).astype(BF)
            for ref in (keep_a, send_a, keep_b, send_b):
                for at in range(2):
                    ref[at, 2 * share + row : 2 * share + row + 1, columns] = line


def out_grad_call(scal, *args):
    rows, width = args[0].shape
    share = width // 8
    out = sds((2, 2 * share + 16, width))
    return call(
        out_grad_kernel,
        "out_grad",
        (out,) * 4,
        [whole(a.shape) for a in args],
        (whole(out.shape),) * 4,
        (1,),
        [pltpu.VMEM((width, 2 * rows), BF), pltpu.VMEM((width // 2, 2 * rows), BF)],
        8 * rows * width * width,
        args,
        scal,
    )


def over_core(array):
    return lax.ppermute(array, "seq", [(i, i ^ 1) for i in range(8)])


def over_x(array):
    return lax.ppermute(array, "seq", [(i, i ^ 2) for i in range(8)])


def over_y(array):
    return lax.ppermute(array, "seq", [(i, i ^ 4) for i in range(8)])


def over_bucket(array, pairs):
    return lax.ppermute(array, "bucket", pairs)


def scatter_sum(keep_a, send_a, keep_b, send_b):
    got_a, got_b = over_x(send_a), over_y(send_b)
    pass_a = over_y(keep_a[1] + got_a[1])
    pass_b = over_x(keep_b[1] + got_b[1])
    return keep_a[0] + got_a[0] + pass_a, keep_b[0] + got_b[0] + pass_b


def bucket_sum(part_a, part_b):
    place = lax.axis_index("bucket")
    outer = (place == 0) | (place == 3)
    near = [(0, 1), (1, 0), (2, 3), (3, 2)]
    far = [(0, 3), (3, 0), (1, 2), (2, 1)]
    mine = jnp.where(outer, part_a, part_b) + over_bucket(jnp.where(outer, part_b, part_a), near)
    mine = mine + over_bucket(mine, far)
    other = over_bucket(mine, near)
    return jnp.where(outer, mine, other), jnp.where(outer, other, mine)


def fast_local(
    frames, w_qkv, b_qv, w_out, b_out, ln_gain, ln_shift, w_up, b_up, w_down, b_down,
    cotangent, clip_lengths, valid_lengths,
):
    rows, width = frames.shape[1:]
    place = lax.axis_index("seq")
    scal = place.astype(jnp.int32)[None]
    blocks = place ^ jnp.arange(8, dtype=jnp.int32)
    position = (blocks[:, None] * rows + jnp.arange(rows, dtype=jnp.int32)[None]).reshape(-1)
    ends = jnp.cumsum(clip_lengths[0])
    starts = ends - clip_lengths[0]
    inside = (position[:, None] >= starts) & (position[:, None] < ends)
    segment = jnp.sum(jnp.where(inside, jnp.arange(ends.shape[0], dtype=jnp.int32), 0), axis=1)
    live = jnp.any(inside & (position[:, None] < starts + valid_lengths[0]), axis=1)
    tags = jnp.where(live, segment, -1).reshape(8, rows, 1)
    tags = jnp.broadcast_to(tags, (8, rows, 128))
    seg_row = segment[: 2 * rows][None]

    x = frames[0]
    saved = []
    for layer in range(LAYERS):
        attend = functools.partial(attend_call, layer, scal)
        x_r, x_x, x_y = over_core(x), over_x(x), over_y(x)
        x_d = over_y(x_x)
        x_xr, x_yr, x_dr = over_core(x_x), over_core(x_y), over_core(x_d)
        kv, q, qt, acc, top = attend((), seg_row, w_qkv, b_qv, (x, x_r), tags, (0, 1))
        kv_x, kv_y, acc, top = attend(
            (qt, acc, top), seg_row, w_qkv, b_qv, (x_x, x_xr, x_y, x_yr), tags, (2, 3, 4, 5)
        )
        kv_d, att, ot, lse = attend(
            (qt, acc, top), seg_row, w_qkv, b_qv, (x_d, x_dr), tags, (6, 7), last=True
        )
        oatt = over_core(att)
        unit1, rs1, normed, act, slope, unit2, rs2, y = ffn_call(
            layer, scal, x, att, oatt, w_out, b_out, ln_gain, ln_shift, w_up, b_up, w_down, b_down
        )
        saved.append(
            (x, x_r, q, qt, kv, kv_x, kv_y, kv_d, att, oatt, ot, lse)
            + (unit1, rs1, normed, over_core(normed), act, over_core(act), slope, unit2, rs2)
        )
        x = y
    activations = x[None]

    grad = cotangent[0]
    ffn_parts, att_parts = [None] * LAYERS, [None] * LAYERS
    for layer in reversed(range(LAYERS)):
        x, x_r, q, qt, kv, kv_x, kv_y, kv_d, att, oatt, ot, lse = saved[layer][:12]
        unit1, rs1, normed, o_normed, act, o_act, slope, unit2, rs2 = saved[layer][12:]
        d_down, d_up, d_branch, d_first, sums = ffn_back_call(
            layer, scal, grad, unit2, rs2, slope, unit1, rs1, ln_gain, w_up, w_down
        )
        o_branch = over_core(d_branch)
        o_up, o_down, o_sums = over_core(d_up), over_core(d_down), over_core(sums)
        keep_a, send_a = up_grad_call(scal, normed, o_normed, d_up, o_up)
        keep_b, send_b = down_grad_call(scal, act, o_act, d_down, o_down)
        ffn_parts[layer] = scatter_sum(keep_a, send_a, keep_b, send_b)
        back = functools.partial(attend_back_call, layer, scal)
        common = (q, qt, lse, seg_row)
        g_dm, g_dr, do, dot, corr, dq = back(
            (d_branch, o_branch, ot), w_out, common, (kv_d, kv_d), None, tags, (6, 7)
        )
        g_dm, g_dr = over_x(g_dm), over_y(g_dr)
        g_xm, g_yr, dq = back(
            (do, dot, corr, dq), None, common, (kv_x, kv_y), None, tags, (2, 5)
        )
        g_xm, g_yr = over_x(g_xm), over_y(g_yr)
        g_ym, g_xr, dq = back(
            (do, dot, corr, dq), None, common, (kv_y, kv_x), (g_dm, g_dr), tags, (4, 3)
        )
        g_ym, g_xr = over_y(g_ym), over_x(g_xr)
        g_m, g_r, dq = back(
            (do, dot, corr, dq), None, common, (kv, kv), (g_xm, g_yr), tags, (0, 1), last=True
        )
        g_m, g_r = g_m + g_ym, g_r + g_xr
        odq, o_m, o_r = over_core(dq), over_core(g_m), over_core(g_r)
        grad = input_back_call(layer, scal, d_first, dq, g_m, odq, o_r, w_qkv)
        att_parts[layer] = scatter_sum(
            *out_grad_call(
                scal, x, x_r, dq, g_m, g_r, odq, o_m, o_r, att, oatt, d_branch, o_branch,
                sums, o_sums,
            )
        )

    share = width // 8
    for layer in range(LAYERS):
        ffn_parts[layer] = bucket_sum(*ffn_parts[layer])
        att_parts[layer] = bucket_sum(*att_parts[layer])

    def both(make):
        return jnp.stack([make(layer).astype(F32) for layer in range(LAYERS)])

    small = both(lambda l: att_parts[l][0][2 * share :])

    def own(array, axis):
        size = array.shape[axis] // 8
        return lax.dynamic_slice_in_dim(array, place * size, size, axis)

    def beside(array):
        parts = array.shape[0] // share
        return array.reshape(parts, share, width).transpose(1, 0, 2).reshape(share, -1)

    return (
        activations,
        grad[None],
        both(
            lambda l: jnp.concatenate(
                [beside(att_parts[l][0][: 2 * share]), att_parts[l][1][:share]], axis=1
            )
        ),
        own(small[:, 10:12].reshape(LAYERS, -1), 1),
        both(lambda l: att_parts[l][1][share : 2 * share]),
        own(small[:, 4], 1),
        own(small[:, 0:2], 2),
        own(small[:, 2:4], 2),
        both(lambda l: beside(ffn_parts[l][0])),
        own(small[:, 6:10].reshape(LAYERS, -1), 1),
        both(lambda l: ffn_parts[l][1]),
        own(small[:, 5], 1),
    )


def clip_tags(lengths, valid, begin, count):
    position = begin + jnp.arange(count, dtype=jnp.int32)
    ends = jnp.cumsum(lengths)
    starts = ends - lengths
    inside = (position[:, None] >= starts[None, :]) & (position[:, None] < ends[None, :])
    labels = jnp.arange(lengths.shape[0], dtype=jnp.int32)
    segment = jnp.sum(jnp.where(inside, labels[None, :], 0), axis=1)
    live = jnp.any(inside & (position[:, None] < (starts + valid)[None, :]), axis=1)
    return (segment, jnp.where(live, segment, -1))


def layer_norm(hidden, gain, shift):
    center = hidden - jnp.mean(hidden, axis=-1, keepdims=True)
    spread = jnp.mean(center * center, axis=-1, keepdims=True)
    return center * lax.rsqrt(spread + 1e-05) * gain + shift


def exact_gelu(hidden):
    return jax.nn.gelu(hidden, approximate=False)


def split_heads(matrix):
    return matrix.reshape(matrix.shape[0], HEADS, -1)


def pair_terms(
    query_heads,
    grad_heads,
    log_total,
    correction,
    query_seg,
    key_heads,
    value_heads,
    key_tag,
    scale,
):
    scores = (
        jnp.einsum("qhd,khd->hqk", query_heads, key_heads, preferred_element_type=jnp.float32)
        * scale
    )
    allowed = (query_seg[:, None] == key_tag[None, :])[None]
    scores = jnp.where(allowed, scores, -1e30)
    probs = jnp.where(allowed, jnp.exp(scores - log_total[..., None]), 0.0)
    grad_probs = jnp.einsum(
        "qhd,khd->hqk", grad_heads, value_heads, preferred_element_type=jnp.float32
    )
    grad_scores = (probs * (grad_probs - correction[..., None])).astype(jnp.bfloat16)
    return (probs.astype(jnp.bfloat16), grad_scores)


def forward_layer(hidden, weights, query_seg, lengths, valid):
    w_qkv, b_qv, w_out, b_out, gain, shift, w_up, b_up, w_down, b_down = weights
    rows, width = hidden.shape
    scale = (width // HEADS) ** (-0.5)
    inputs = hidden.astype(jnp.bfloat16)
    projected = jnp.dot(inputs, w_qkv, preferred_element_type=jnp.float32)
    queries = (projected[:, :width] + b_qv[:width]).astype(jnp.bfloat16)
    keys = projected[:, width : 2 * width].astype(jnp.bfloat16)
    values = (projected[:, 2 * width :] + b_qv[width:]).astype(jnp.bfloat16)
    query_heads = split_heads(queries)
    initial = (
        jnp.full((HEADS, rows), -1e30, jnp.float32),
        jnp.zeros((HEADS, rows), jnp.float32),
        jnp.zeros((HEADS, rows, width // HEADS), jnp.float32),
    )
    key_piece = lax.all_gather(keys, "seq", axis=0, tiled=True)
    value_piece = lax.all_gather(values, "seq", axis=0, tiled=True)
    count = key_piece.shape[0] // rows
    key_blocks = key_piece.reshape(count, rows, HEADS, -1)
    value_blocks = value_piece.reshape(count, rows, HEADS, -1)

    def fold_inner(state, item):
        key_heads, value_heads, block_at = item
        _, block_tag = clip_tags(lengths, valid, block_at * rows, rows)
        running, denominator, weighted = state
        scores = (
            jnp.einsum("qhd,khd->hqk", query_heads, key_heads, preferred_element_type=jnp.float32)
            * scale
        )
        allowed = (query_seg[:, None] == block_tag[None, :])[None]
        scores = jnp.where(allowed, scores, -1e30)
        raised = jnp.maximum(running, jnp.max(scores, axis=-1))
        block_probs = jnp.where(allowed, jnp.exp(scores - raised[..., None]), 0.0)
        factor = jnp.exp(running - raised)
        denominator = denominator * factor + jnp.sum(block_probs, axis=-1)
        weighted = weighted * factor[..., None] + jnp.einsum(
            "hqk,khd->hqd",
            block_probs.astype(jnp.bfloat16),
            value_heads,
            preferred_element_type=jnp.float32,
        )
        return ((raised, denominator, weighted), None)

    state, _ = lax.scan(
        fold_inner, initial, (key_blocks, value_blocks, jnp.arange(count, dtype=jnp.int32))
    )
    running, denominator, weighted = state
    attended = (weighted / denominator[..., None]).transpose(1, 0, 2).reshape(rows, width)
    log_total = running + jnp.log(denominator)
    attended_low = attended.astype(jnp.bfloat16)
    branch = jnp.dot(attended_low, w_out, preferred_element_type=jnp.float32) + b_out
    first_sum = inputs.astype(jnp.float32) + branch
    normed = layer_norm(first_sum, gain[0], shift[0]).astype(jnp.bfloat16)
    up_pre = jnp.dot(normed, w_up, preferred_element_type=jnp.float32) + b_up
    activated = exact_gelu(up_pre).astype(jnp.bfloat16)
    second_sum = (
        normed.astype(jnp.float32)
        + jnp.dot(activated, w_down, preferred_element_type=jnp.float32)
        + b_down
    )
    output = layer_norm(second_sum, gain[1], shift[1])
    kept = (
        inputs,
        queries,
        keys,
        values,
        attended,
        attended_low,
        log_total,
        None,
        first_sum,
        normed,
        up_pre,
        activated,
        second_sum,
    )
    return (output, kept)


def attention_grads(kept, grad_att, query_seg, lengths, valid):
    (
        inputs,
        queries,
        keys,
        values,
        attended,
        attended_low,
        log_total,
        gathered,
        first_sum,
        normed,
        up_pre,
        activated,
        second_sum,
    ) = kept
    rows, width = queries.shape
    scale = (width // HEADS) ** (-0.5)
    query_heads = split_heads(queries)
    grad_heads = split_heads(grad_att)
    correction = jnp.sum(grad_heads.astype(jnp.float32) * split_heads(attended), axis=-1).T
    key_all, value_all = (
        lax.all_gather(keys, "seq", axis=0, tiled=True),
        lax.all_gather(values, "seq", axis=0, tiled=True),
    )
    count = key_all.shape[0] // rows
    key_blocks = key_all.reshape(count, rows, HEADS, -1)
    value_blocks = value_all.reshape(count, rows, HEADS, -1)
    block_ids = jnp.arange(count, dtype=jnp.int32)
    zero_heads = jnp.zeros((rows, HEADS, width // HEADS), jnp.float32)

    def attention_inner(acc, item):
        key_heads, value_heads, block_at = item
        _, block_tag = clip_tags(lengths, valid, block_at * rows, rows)
        probs, grad_scores = pair_terms(
            query_heads,
            grad_heads,
            log_total,
            correction,
            query_seg,
            key_heads,
            value_heads,
            block_tag,
            scale,
        )
        acc = (
            acc
            + jnp.einsum("hqk,khd->qhd", grad_scores, key_heads, preferred_element_type=jnp.float32)
            * scale
        )
        key_term = (
            jnp.einsum("hqk,qhd->khd", grad_scores, query_heads, preferred_element_type=jnp.float32)
            * scale
        )
        value_term = jnp.einsum(
            "hqk,qhd->khd", probs, grad_heads, preferred_element_type=jnp.float32
        )
        return (
            acc,
            jnp.concatenate(
                [key_term.reshape(rows, width), value_term.reshape(rows, width)], axis=1
            ),
        )

    grad_query, terms = lax.scan(attention_inner, zero_heads, (key_blocks, value_blocks, block_ids))
    summed = lax.psum_scatter(
        terms.reshape(count * rows, 2 * width).astype(jnp.bfloat16),
        "seq",
        scatter_dimension=0,
        tiled=True,
    ).astype(jnp.float32)
    grad_key = summed[:, :width]
    grad_value = summed[:, width:]
    return (grad_query.reshape(rows, width), grad_key, grad_value)


def backward_layer(grad_out, kept, weights, query_seg, lengths, valid):
    w_qkv, b_qv, w_out, b_out, gain, shift, w_up, b_up, w_down, b_down = weights
    (
        inputs,
        queries,
        keys,
        values,
        attended,
        attended_low,
        log_total,
        gathered,
        first_sum,
        normed,
        up_pre,
        activated,
        second_sum,
    ) = kept
    _, pull_second = jax.vjp(layer_norm, second_sum, gain[1], shift[1])
    grad_second, gain_second, shift_second = pull_second(grad_out)
    grad_down = grad_second.astype(jnp.bfloat16)
    sum_down = jnp.sum(grad_down, axis=0, dtype=jnp.float32)
    weight_down = jnp.einsum("rf,rd->fd", activated, grad_down, preferred_element_type=jnp.float32)
    grad_activated = jnp.einsum("rd,fd->rf", grad_down, w_down, preferred_element_type=jnp.float32)
    _, pull_gelu = jax.vjp(exact_gelu, up_pre)
    grad_up = pull_gelu(grad_activated)[0].astype(jnp.bfloat16)
    sum_up = jnp.sum(grad_up, axis=0, dtype=jnp.float32)
    weight_up = jnp.einsum("rd,rf->df", normed, grad_up, preferred_element_type=jnp.float32)
    grad_normed = grad_second + jnp.einsum(
        "rf,df->rd", grad_up, w_up, preferred_element_type=jnp.float32
    )
    _, pull_first = jax.vjp(layer_norm, first_sum, gain[0], shift[0])
    grad_first, gain_first, shift_first = pull_first(grad_normed)
    grad_branch = grad_first.astype(jnp.bfloat16)
    sum_out = jnp.sum(grad_branch, axis=0, dtype=jnp.float32)
    weight_out = jnp.einsum(
        "re,rd->ed", attended_low, grad_branch, preferred_element_type=jnp.float32
    )
    grad_att = jnp.einsum(
        "rd,ed->re", grad_branch, w_out, preferred_element_type=jnp.float32
    ).astype(jnp.bfloat16)
    grad_query, grad_key, grad_value = attention_grads(kept, grad_att, query_seg, lengths, valid)
    grad_proj = jnp.concatenate(
        [
            grad_query.astype(jnp.bfloat16),
            grad_key.astype(jnp.bfloat16),
            grad_value.astype(jnp.bfloat16),
        ],
        axis=1,
    )
    width = inputs.shape[1]
    sum_qv = jnp.concatenate(
        [
            jnp.sum(grad_proj[:, :width], axis=0, dtype=jnp.float32),
            jnp.sum(grad_proj[:, 2 * width :], axis=0, dtype=jnp.float32),
        ]
    )
    weight_qkv = jnp.einsum("rd,re->de", inputs, grad_proj, preferred_element_type=jnp.float32)
    grad_input = grad_first + jnp.einsum(
        "re,de->rd", grad_proj, w_qkv, preferred_element_type=jnp.float32
    )
    gains = jnp.stack([gain_first, gain_second])
    shifts = jnp.stack([shift_first, shift_second])
    return (
        grad_input,
        (
            weight_qkv,
            sum_qv,
            weight_out,
            sum_out,
            gains,
            shifts,
            weight_up,
            sum_up,
            weight_down,
            sum_down,
        ),
    )


def local(
    frames,
    w_qkv,
    b_qv,
    w_out,
    b_out,
    ln_gain,
    ln_shift,
    w_up,
    b_up,
    w_down,
    b_down,
    cotangent,
    clip_lengths,
    valid_lengths,
):
    rows = frames.shape[1]
    lengths = clip_lengths[0]
    valid = valid_lengths[0]
    offset = lax.axis_index("seq") * rows
    query_seg, key_tag = clip_tags(lengths, valid, offset, rows)
    layer_weights = [
        tuple(
            (
                array[layer_at]
                for array in (
                    w_qkv,
                    b_qv,
                    w_out,
                    b_out,
                    ln_gain,
                    ln_shift,
                    w_up,
                    b_up,
                    w_down,
                    b_down,
                )
            )
        )
        for layer_at in range(LAYERS)
    ]
    hidden = frames[0].astype(jnp.float32)
    saved = []
    for layer_at in range(LAYERS):
        hidden, kept = forward_layer(hidden, layer_weights[layer_at], query_seg, lengths, valid)
        saved.append(kept)
    activations = hidden.astype(jnp.bfloat16)[None]
    grad_hidden = cotangent[0].astype(jnp.float32)
    per_layer = [None] * LAYERS
    for layer_at in reversed(range(LAYERS)):
        grad_hidden, per_layer[layer_at] = backward_layer(
            grad_hidden, saved[layer_at], layer_weights[layer_at], query_seg, lengths, valid
        )
    stacked = [
        jnp.stack([per_layer[layer_at][member] for layer_at in range(LAYERS)])
        for member in range(10)
    ]
    g_wqkv, g_bqv, g_wout, g_bout, g_gain, g_shift, g_wup, g_bup, g_wdown, g_bdown = stacked
    shares = (
        lax.psum_scatter(
            g_wqkv.astype(jnp.bfloat16), "seq", scatter_dimension=1, tiled=True
        ).astype(jnp.float32),
        lax.psum_scatter(g_bqv.astype(jnp.bfloat16), "seq", scatter_dimension=1, tiled=True).astype(
            jnp.float32
        ),
        lax.psum_scatter(
            g_wout.astype(jnp.bfloat16), "seq", scatter_dimension=1, tiled=True
        ).astype(jnp.float32),
        lax.psum_scatter(
            g_bout.astype(jnp.bfloat16), "seq", scatter_dimension=1, tiled=True
        ).astype(jnp.float32),
        lax.psum_scatter(
            g_gain.astype(jnp.bfloat16), "seq", scatter_dimension=2, tiled=True
        ).astype(jnp.float32),
        lax.psum_scatter(
            g_shift.astype(jnp.bfloat16), "seq", scatter_dimension=2, tiled=True
        ).astype(jnp.float32),
        lax.psum_scatter(g_wup.astype(jnp.bfloat16), "seq", scatter_dimension=1, tiled=True).astype(
            jnp.float32
        ),
        lax.psum_scatter(g_bup.astype(jnp.bfloat16), "seq", scatter_dimension=1, tiled=True).astype(
            jnp.float32
        ),
        lax.psum_scatter(
            g_wdown.astype(jnp.bfloat16), "seq", scatter_dimension=1, tiled=True
        ).astype(jnp.float32),
        lax.psum_scatter(
            g_bdown.astype(jnp.bfloat16), "seq", scatter_dimension=1, tiled=True
        ).astype(jnp.float32),
    )
    s_wqkv, s_bqv, s_wout, s_bout, s_gain, s_shift, s_wup, s_bup, s_wdown, s_bdown = shares
    totals = (
        lax.psum(s_wqkv.astype(jnp.bfloat16), "bucket").astype(jnp.float32),
        lax.psum(s_bqv.astype(jnp.bfloat16), "bucket").astype(jnp.float32),
        lax.psum(s_wout.astype(jnp.bfloat16), "bucket").astype(jnp.float32),
        lax.psum(s_bout.astype(jnp.bfloat16), "bucket").astype(jnp.float32),
        lax.psum(s_gain.astype(jnp.bfloat16), "bucket").astype(jnp.float32),
        lax.psum(s_shift.astype(jnp.bfloat16), "bucket").astype(jnp.float32),
        lax.psum(s_wup.astype(jnp.bfloat16), "bucket").astype(jnp.float32),
        lax.psum(s_bup.astype(jnp.bfloat16), "bucket").astype(jnp.float32),
        lax.psum(s_wdown.astype(jnp.bfloat16), "bucket").astype(jnp.float32),
        lax.psum(s_bdown.astype(jnp.bfloat16), "bucket").astype(jnp.float32),
    )
    return (
        activations,
        grad_hidden[None],
        totals[0],
        totals[1],
        totals[2],
        totals[3],
        totals[4],
        totals[5],
        totals[6],
        totals[7],
        totals[8],
        totals[9],
    )


def solution(mesh):
    placed = (
        P("bucket", "seq", None),
        P(),
        P(),
        P(),
        P(),
        P(),
        P(),
        P(),
        P(),
        P(),
        P(),
        P("bucket", "seq", None),
        P("bucket", None),
        P("bucket", None),
    )
    chips_2x2 = mesh.shape["seq"] == 8 and mesh.shape["bucket"] == 4
    return jax.shard_map(
        fast_local if chips_2x2 else local,
        mesh=mesh,
        in_specs=placed,
        out_specs=(
            P("bucket", "seq", None),
            P("bucket", "seq", None),
            P(None, "seq", None),
            P(None, "seq"),
            P(None, "seq", None),
            P(None, "seq"),
            P(None, None, "seq"),
            P(None, None, "seq"),
            P(None, "seq", None),
            P(None, "seq"),
            P(None, "seq", None),
            P(None, "seq"),
        ),
        check_vma=False,
    )
```

```python
import functools
import math

import jax
import jax.numpy as jnp
from jax import lax
from jax.experimental import pallas as pl
from jax.experimental.pallas import tpu as pltpu
from jax.sharding import PartitionSpec as P

HEADS = 12
LAYERS = 2
NEAR = [(0, 1), (1, 0), (2, 3), (3, 2)]
FAR = [(0, 3), (3, 0), (1, 2), (2, 1)]
BF = jnp.bfloat16
F32 = jnp.float32
LOW = -1e30
SLACK = 6 * 1024 * 1024


def dot_nn(a, b):
    return lax.dot_general(a, b, (((1,), (0,)), ((), ())), preferred_element_type=F32)


def dot_nt(a, b):
    return lax.dot_general(a, b, (((1,), (1,)), ((), ())), preferred_element_type=F32)


def block_bytes(spec, array):
    if spec.block_shape is None:
        return 0
    lanes = [n for n in spec.block_shape if n is not None]
    lanes[-1] += -lanes[-1] % 128
    return math.prod(lanes) * array.dtype.itemsize


def call(body, name, out_shape, in_specs, out_specs, grid, scratch, flops, args, scalars, after=()):
    args = tuple(
        stored(a) if p.memory_space == pltpu.HBM else a for p, a in zip(in_specs, args)
    )
    count = len(args)

    def run(scal, *refs):
        body(scal, *refs[:count], *refs[count + len(after) :])

    need = sum(block_bytes(p, a) for p, a in zip(in_specs, args))
    need += sum(block_bytes(p, a) for p, a in zip(jax.tree.leaves(out_specs), jax.tree.leaves(out_shape)))
    need = need + sum(
        math.prod(m.shape) * jnp.dtype(m.dtype).itemsize for m in scratch if m.memory_space == pltpu.VMEM
    )
    return pl.pallas_call(
        run,
        name=name,
        out_shape=out_shape,
        grid_spec=pltpu.PrefetchScalarGridSpec(
            num_scalar_prefetch=1,
            grid=grid,
            in_specs=list(in_specs) + [pl.BlockSpec(memory_space=pl.ANY)] * len(after),
            out_specs=out_specs,
            scratch_shapes=scratch,
        ),
        compiler_params=pltpu.CompilerParams(vmem_limit_bytes=need + SLACK),
        cost_estimate=pl.CostEstimate(
            flops=int(flops), bytes_accessed=1 + int(flops / 400), transcendentals=0
        ),
    )(scalars, *args, *after)


def whole(shape):
    return pl.BlockSpec(shape, lambda i, s: (0,) * len(shape))


def kept(shape, dtype=BF):
    return pltpu.HBM(shape, dtype)


def near(shape, dtype=BF):
    return pltpu.VMEM(shape, dtype)


def held(array):
    return pltpu.with_memory_space_constraint(array, pltpu.VMEM)


def stored(array):
    return pltpu.with_memory_space_constraint(array, pltpu.HBM)


def gate(arrays, after, space=pltpu.VMEM):
    anywhere = pl.BlockSpec(memory_space=pl.ANY)
    count = len(arrays)

    def body(*refs):
        pass

    return pl.pallas_call(
        body,
        name="gate",
        out_shape=tuple(sds(a.shape, a.dtype) for a in arrays),
        in_specs=[anywhere] * (count + len(after)),
        out_specs=(anywhere,) * count,
        input_output_aliases={i: i for i in range(count)},
        compiler_params=pltpu.CompilerParams(vmem_limit_bytes=1024 * 1024),
        cost_estimate=pl.CostEstimate(flops=1, bytes_accessed=1, transcendentals=0),
    )(*(pltpu.with_memory_space_constraint(a, space) for a in arrays), *after)


def far():
    return pl.BlockSpec(memory_space=pltpu.HBM)


def fetch(pairs, sems):
    copies = [pltpu.make_async_copy(src, dst, sems.at[i]) for i, (src, dst) in enumerate(pairs)]
    for copy in copies:
        copy.start()
    return copies


def sds(shape, dtype=BF):
    return jax.ShapeDtypeStruct(shape, dtype)


def attend_kernel(layer, chips, first, last, *refs):
    refs = list(refs)
    core = refs.pop(0)[0] % 2
    if not first:
        qt, w_kv, acc_in, m_in = (refs.pop(0) for _ in range(4))
    seg_ref, bias_ref, bias_k, w_ref = (refs.pop(0) for _ in range(4))
    xs = [refs.pop(0) for _ in range(2 * chips)]
    tags = [refs.pop(0) for _ in range(2 * chips)]
    kv_outs = [refs.pop(0) for _ in range(chips)]
    if first:
        q_out, qt, w_kv = (refs.pop(0) for _ in range(3))
    if last:
        att_ref, ot_ref, lse_ref = refs.pop(0), refs.pop(0), refs.pop(0)
    else:
        acc_out, m_out = refs.pop(0), refs.pop(0)
    s_scr, vt_scr, kvs, out_sems = (refs.pop(0) for _ in range(4))
    rows, width = xs[0].shape
    half = width // 2
    heads = half // 64
    queries = seg_ref.shape[1]
    high = vt_scr.shape[1]
    pair = 2 * rows
    leaving = []

    def leave(src, dst):
        copy = pltpu.make_async_copy(src, dst, out_sems.at[len(leaving)])
        copy.start()
        leaving.append(copy)

    if first:
        w_scr, q_scr, sems = (refs.pop(0) for _ in range(3))
        begin = [pl.multiple_of(width * i + core * half, 128) for i in range(3)]
        places = (w_scr, w_kv.at[0], w_kv.at[1])
        copies = fetch(
            [(w_ref.at[layer, :, pl.ds(begin[i], half)], places[i]) for i in range(3)], sems
        )
    if last:
        ot_scr = refs.pop(0)
    bias_q = bias_ref[layer : layer + 1, :]
    bias_v = bias_k[layer : layer + 1, :]
    for c in range(chips):
        x = jnp.concatenate([xs[2 * c][...], xs[2 * c + 1][...]], axis=0)
        if first:
            copies.pop(0).wait()
            q = (dot_nn(x, w_scr[...]) + bias_q).astype(BF) * BF(0.125)
            q_scr[...] = q
            qt[...] = q.T
            leave(q_scr, q_out)
            copies.pop(0).wait()
            copies.pop(0).wait()
        kvs[c, :, :half] = dot_nn(x, w_kv[0]).astype(BF)
        values = (dot_nn(x, w_kv[1]) + bias_v).astype(BF)
        kvs[c, :, half:] = values
        leave(kvs.at[c], kv_outs[c])
        turned = values.T
        for h in range(heads):
            vt_scr[h, :64, c * pair : (c + 1) * pair] = turned[h * 64 : (h + 1) * 64]
    vt_scr[:, 64:, :] = jnp.ones((heads, high - 64, chips * pair), BF)
    seg = seg_ref[...]
    outs = []
    if last:
        lse_ref[...] = jnp.zeros_like(lse_ref)
    else:
        m_out[...] = jnp.zeros_like(m_out)
    for h in range(heads):
        qh = qt[h * 64 : (h + 1) * 64, :]
        m8 = None
        for b in range(2 * chips):
            key = slice((b % 2) * rows, (b % 2 + 1) * rows)
            scores = dot_nn(kvs[b // 2, key, h * 64 : (h + 1) * 64], qh)
            ok = jnp.concatenate([tags[b][...]] * (queries // 128), axis=1) == seg
            scores = jnp.where(ok, scores, LOW)
            s_scr[h % 2, b * rows : (b + 1) * rows, :] = scores
            top = jnp.max(scores.reshape(rows // 8, 8, queries), axis=0)
            m8 = top if m8 is None else jnp.maximum(m8, top)
        m = jnp.max(m8, axis=0, keepdims=True)
        if not first:
            m_old = m_in[h : h + 1, :]
            m = jnp.maximum(m, m_old)
        acc = jnp.zeros((high, queries), F32)
        for b in range(2 * chips):
            probs = jnp.exp(s_scr[h % 2, b * rows : (b + 1) * rows, :] - m).astype(BF)
            acc = acc + dot_nn(vt_scr[h, :, b * rows : (b + 1) * rows], probs)
        if not first:
            acc = acc + acc_in[h] * jnp.exp(m_old - m)
        if last:
            total = acc[64:65]
            out = acc[:64] / total
            ot_scr[h * 64 : (h + 1) * 64, :] = out
            strip = pl.ds(h * 64, 64)
            leave(ot_scr.at[strip], ot_ref.at[strip])
            lse_ref[h : h + 1, :] = m + jnp.log(total)
            outs.append(out.astype(BF))
        else:
            acc_out[h] = acc
            m_out[h : h + 1, :] = m
    if last:
        att_ref[...] = jnp.concatenate(outs, axis=0).T
    for copy in leaving:
        copy.wait()


def tag_specs(tag_ids, rows):
    return [pl.BlockSpec((None, rows, 128), lambda i, s, r=r: (r, 0, 0)) for r in tag_ids]


def attend_call(layer, scal, state, seg_row, w_qkv, b_qv, xs, tags, tag_ids, last=False, after=()):
    first = not state
    rows, width = xs[0].shape
    half = width // 2
    heads = half // 64
    queries = 2 * rows
    chips = len(xs) // 2
    high = 80
    out_shape = tuple(kept((2 * rows, width)) for _ in range(chips))
    if first:
        out_shape += (kept((queries, half)), near((half, queries)), near((2, width, half)))
    if last:
        out_shape += (sds((queries, half)), kept((half, queries), F32), sds((8, queries), F32))
    else:
        out_shape += (near((heads, high, queries), F32), near((8, queries), F32))
    out_specs = [whole(o.shape) for o in out_shape]
    for i in range(chips + first):
        out_specs[i] = far()
    if last:
        out_specs[chips + 1] = far()

    def bias(part):
        return pl.BlockSpec((LAYERS, half), lambda i, s: (0, 2 * part + s[0] % 2))

    state = tuple(held(a) for a in state)
    specs = [whole(a.shape) for a in state]
    specs += [whole(seg_row.shape), bias(0), bias(1), far()]
    specs += [whole(x.shape) for x in xs] + tag_specs(tag_ids, rows)
    args = state + (seg_row, b_qv, b_qv, w_qkv) + tuple(xs) + (tags,) * len(xs)
    scratch = [
        pltpu.VMEM((2, chips * 2 * rows, queries), F32),
        pltpu.VMEM((heads, high, chips * 2 * rows), BF),
        pltpu.VMEM((chips, 2 * rows, width), BF),
        pltpu.SemaphoreType.DMA((chips + heads,)),
    ]
    if first:
        scratch += [
            pltpu.VMEM((width, half), BF),
            pltpu.VMEM((queries, half), BF),
            pltpu.SemaphoreType.DMA((3,)),
        ]
    if last:
        scratch.append(pltpu.VMEM((half, queries), F32))
    return call(
        functools.partial(attend_kernel, layer, chips, first, last),
        "attend",
        out_shape,
        specs,
        tuple(out_specs),
        (1,),
        scratch,
        chips * 12 * 4 * queries * half * rows,
        args,
        scal,
        after,
    )


def attend_back_kernel(sides, adds, first, last, *refs):
    refs = list(refs)
    refs.pop(0)
    blocks = len(sides)
    if first:
        b_m, b_o, w_out, ot_ref, q = (refs.pop(0) for _ in range(5))
    else:
        do, dot, corr, q, qt, dq_in = (refs.pop(0) for _ in range(6))
    lse_ref, seg_ref = (refs.pop(0) for _ in range(2))
    kvs = [refs.pop(0) for _ in range(blocks)]
    more = [refs.pop(0) for _ in range(blocks)] if adds else None
    tags = [refs.pop(0) for _ in range(blocks)]
    outs = [refs.pop(0) for _ in range(blocks)]
    if first:
        do, dot, corr, q_out, qt, dq_out = (refs.pop(0) for _ in range(6))
    else:
        dq_out = refs.pop(0)
    dqt_scr, kv_scr, sems = (refs.pop(0) for _ in range(3))
    rows, width = kv_scr.shape[1:]
    copies = fetch(
        [(kvs[b].at[pl.ds(sides[b] * rows, rows)], kv_scr.at[b]) for b in range(blocks)], sems
    )
    half = width // 2
    heads = half // 64
    seg = seg_ref[...]
    queries = seg.shape[1]
    if first:
        branch = jnp.concatenate([b_m[...], b_o[...]], axis=0)
        grad_att = dot_nt(branch, w_out[...]).astype(BF)
        do[...] = grad_att
        turned = grad_att.T
        dot[...] = turned
        wide = turned.astype(F32) * ot_ref[...]
        corr[...] = jnp.zeros_like(corr)
        for h in range(heads):
            corr[h : h + 1, :] = jnp.sum(wide[h * 64 : (h + 1) * 64], axis=0, keepdims=True)
        q_out[...] = q[...]
        qt[...] = q[...].T
    for b in range(blocks):
        copies[b].wait()
        kt = kv_scr[b, :, :half].T
        ok = jnp.concatenate([tags[b][...]] * (queries // 128), axis=1) == seg
        dks, dvs = [], []
        for h in range(heads):
            sl = slice(h * 64, (h + 1) * 64)
            vl = slice(half + h * 64, half + (h + 1) * 64)
            scores = dot_nn(kv_scr[b, :, sl], qt[sl, :])
            grad = dot_nn(kv_scr[b, :, vl], dot[sl, :])
            probs = jnp.exp(jnp.where(ok, scores - lse_ref[h : h + 1, :], LOW))
            grad = (probs * (grad - corr[h : h + 1, :])).astype(BF)
            probs = probs.astype(BF)
            term = dot_nn(kt[sl], grad)
            if b == 0:
                if first:
                    dqt_scr[sl, :] = term
                else:
                    dqt_scr[sl, :] = dq_in[sl, :] + term
            else:
                dqt_scr[sl, :] += term
            dks.append(dot_nn(grad, q[:, sl]))
            dvs.append(dot_nn(probs, do[:, sl]))
        result = jnp.concatenate(dks + dvs, axis=1)
        if adds:
            result = result + more[b][...].astype(F32)
        outs[b][...] = result.astype(BF)
    if last:
        dq_out[...] = (dqt_scr[...] * 0.125).astype(BF).T
    else:
        dq_out[...] = dqt_scr[...]


def attend_back_call(layer, scal, state, w_out, shared, kvs, adds, tags, tag_ids, last=False, after=()):
    first = w_out is not None
    rows = kvs[0].shape[0] // 2
    width = kvs[0].shape[1]
    half = width // 2
    queries = 2 * rows
    blocks = len(kvs)
    out_shape = tuple(sds((rows, width)) for _ in range(blocks))
    if first:
        tall, flat = near((queries, half)), near((half, queries))
        out_shape += (tall, flat, near((8, queries), F32), tall, flat)
    else:
        state = tuple(held(a) for a in state)
    out_shape += (sds((queries, half)) if last else near((half, queries), F32),)
    args, specs = tuple(state), [whole(a.shape) for a in state]
    if first:
        args = args[:2] + (w_out,) + args[2:]
        specs.insert(
            2, pl.BlockSpec((None, half, width), lambda i, s: (layer, s[0] % 2, 0))
        )
    args += tuple(shared) + tuple(kvs) + tuple(adds or ())
    specs += [whole(a.shape) for a in shared] + [far()] * blocks
    specs += [whole(a.shape) for a in adds or ()] + tag_specs(tag_ids, rows)
    sides = [r % 2 for r in tag_ids]
    return call(
        functools.partial(attend_back_kernel, sides, adds is not None, first, last),
        "attend_back",
        out_shape,
        specs,
        tuple(whole(o.shape) for o in out_shape),
        (1,),
        [
            pltpu.VMEM((half, queries), F32),
            pltpu.VMEM((blocks, rows, width), BF),
            pltpu.SemaphoreType.DMA((blocks,)),
        ],
        1,
        args + (tags,) * blocks,
        scal,
        after,
    )


def normalize(hidden):
    center = hidden - jnp.mean(hidden, axis=-1, keepdims=True)
    spread = lax.rsqrt(jnp.mean(center * center, axis=-1, keepdims=True) + 1e-05)
    return center * spread, spread


def normalize_back(grad, unit, spread, gain):
    scaled = grad * gain
    mean = jnp.mean(scaled, axis=-1, keepdims=True)
    along = jnp.mean(scaled * unit, axis=-1, keepdims=True)
    return spread * (scaled - mean - unit * along)


def gauss(up):
    size = jnp.abs(up)
    bell = jnp.exp(-0.5 * up * up)
    t = 1.0 / (1.0 + 0.23164189 * size)
    poly = 0.5307027145 * t - 0.7265760135
    poly = poly * t + 0.7107068705
    poly = poly * t - 0.142248368
    poly = poly * t + 0.127414796
    tail = poly * t * bell
    return jnp.where(up < 0, tail, 1.0 - tail), bell


def ffn_kernel(
    layer, s, x, att, oatt, b_out, gain, shift, b_up, b_down, w_out, w_up, w_down,
    unit1, rs1, normed, act, slope, unit2, rs2, y, kept_scr, unit_scr, kept_sems, out_scr,
    up_scr, down_scr, sems,
):
    rows, width = x.shape
    half = att.shape[1]
    core = s[0] % 2
    steps = up_scr.shape[0]
    pairs = [(w_out.at[layer], out_scr)]
    for n in range(steps):
        strip = pl.ds(n * width, width)
        pairs += [(w_up.at[layer, :, strip], up_scr.at[n]), (w_down.at[layer, strip], down_scr.at[n])]
    copies = fetch(pairs, sems)
    copies[0].wait()
    mine = pl.multiple_of(core * half, 128)
    other = pl.multiple_of((1 - core) * half, 128)
    branch = dot_nn(att[:rows], out_scr[pl.ds(mine, half), :])
    branch = branch + dot_nn(oatt[rows:], out_scr[pl.ds(other, half), :])
    first = x[...].astype(F32) + branch + b_out[layer : layer + 1, :]
    unit, spread = normalize(first)
    unit_scr[0] = unit
    leaving = [pltpu.make_async_copy(unit_scr.at[0], unit1, kept_sems.at[2 * steps])]
    leaving[0].start()
    rs1[...] = jnp.broadcast_to(spread, rs1.shape)
    low = (unit * gain[layer, 0:1, :] + shift[layer, 0:1, :]).astype(BF)
    normed[...] = low
    total = low.astype(F32) + b_down[layer : layer + 1, :]
    for n in range(steps):
        strip = slice(n * width, (n + 1) * width)
        copies[1 + 2 * n].wait()
        up = dot_nn(normed[...], up_scr[n]) + b_up[layer : layer + 1, strip]
        phi, bell = gauss(up)
        low = (up * phi).astype(BF)
        kept_scr[0, :, strip] = low
        kept_scr[1, :, strip] = (phi + up * (0.3989422804014327 * bell)).astype(BF)
        for i, ref in enumerate((act, slope)):
            copy = pltpu.make_async_copy(
                kept_scr.at[i, :, strip], ref.at[:, strip], kept_sems.at[2 * n + i]
            )
            copy.start()
            leaving.append(copy)
        copies[2 + 2 * n].wait()
        total = total + dot_nn(low, down_scr[n])
    unit, spread = normalize(total)
    unit_scr[1] = unit
    leaving.append(pltpu.make_async_copy(unit_scr.at[1], unit2, kept_sems.at[2 * steps + 1]))
    leaving[-1].start()
    rs2[...] = jnp.broadcast_to(spread, rs2.shape)
    y[...] = (unit * gain[layer, 1:2, :] + shift[layer, 1:2, :]).astype(BF)
    for copy in leaving:
        copy.wait()


def ffn_call(
    layer, scal, x, att, oatt, w_out, b_out, gain, shift, w_up, b_up, w_down, b_down, after=()
):
    rows, width = x.shape
    wide = w_up.shape[2]
    steps = wide // width
    vec = sds((rows, 128), F32)
    out_shape = (
        kept((rows, width), F32), vec, sds((rows, width)), kept((rows, wide)), kept((rows, wide)),
        kept((rows, width), F32), vec, sds((rows, width)),
    )
    out_specs = [whole(o.shape) for o in out_shape]
    for i in (0, 3, 4, 5):
        out_specs[i] = far()
    arrays = (x, att, oatt, b_out, gain, shift, b_up, b_down)
    return call(
        functools.partial(ffn_kernel, layer),
        "ffn",
        out_shape,
        [whole(a.shape) for a in arrays] + [far()] * 3,
        tuple(out_specs),
        (1,),
        [
            pltpu.VMEM((2, rows, wide), BF),
            pltpu.VMEM((2, rows, width), F32),
            pltpu.SemaphoreType.DMA((2 * steps + 2,)),
            pltpu.VMEM((width, width), BF),
            pltpu.VMEM((steps, width, width), BF),
            pltpu.VMEM((steps, width, width), BF),
            pltpu.SemaphoreType.DMA((1 + 2 * steps,)),
        ],
        4 * rows * width * wide + 2 * rows * width * width,
        arrays + (w_out, w_up, w_down),
        scal,
        after,
    )


def ffn_back_kernel(
    layer, s, gy, unit2, rs2, slope, unit1, rs1, gain, w_up, w_down,
    d_down, d_up, d_branch, d_first, sums, up_scr, down_scr, sems,
):
    steps = up_scr.shape[0]
    width = gy.shape[1]
    pairs = []
    for n in range(steps):
        strip = pl.ds(n * width, width)
        pairs += [(w_down.at[layer, strip], down_scr.at[n]), (w_up.at[layer, :, strip], up_scr.at[n])]
    copies = fetch(pairs, sems)
    grad = gy[...].astype(F32)
    unit = unit2[...]
    total = normalize_back(grad, unit, rs2[:, 0:1], gain[layer, 1:2, :])
    sums[...] = jnp.zeros_like(sums)
    sums[1:2, :] = jnp.sum(grad * unit, axis=0, keepdims=True)
    sums[3:4, :] = jnp.sum(grad, axis=0, keepdims=True)
    low = total.astype(BF)
    d_down[...] = low
    sums[5:6, :] = jnp.sum(low.astype(F32), axis=0, keepdims=True)
    for n in range(steps):
        strip = slice(n * width, (n + 1) * width)
        copies[2 * n].wait()
        low = (dot_nt(d_down[...], down_scr[n]) * slope[:, strip].astype(F32)).astype(BF)
        d_up[:, strip] = low
        sums[6 + n : 7 + n, :] = jnp.sum(low.astype(F32), axis=0, keepdims=True)
        copies[2 * n + 1].wait()
        total = total + dot_nt(low, up_scr[n])
    unit = unit1[...]
    first = normalize_back(total, unit, rs1[:, 0:1], gain[layer, 0:1, :])
    sums[0:1, :] = jnp.sum(total * unit, axis=0, keepdims=True)
    sums[2:3, :] = jnp.sum(total, axis=0, keepdims=True)
    d_first[...] = first
    low = first.astype(BF)
    d_branch[...] = low
    sums[4:5, :] = jnp.sum(low.astype(F32), axis=0, keepdims=True)


def ffn_back_call(layer, scal, gy, unit2, rs2, slope, unit1, rs1, gain, w_up, w_down, after=()):
    rows, width = gy.shape
    wide = w_up.shape[2]
    steps = wide // width
    low = sds((rows, width))
    out_shape = (low, sds((rows, wide)), low, sds((rows, width), F32), sds((16, width), F32))
    arrays = (gy, unit2, rs2, slope, unit1, rs1, gain)
    return call(
        functools.partial(ffn_back_kernel, layer),
        "ffn_back",
        out_shape,
        [whole(a.shape) for a in arrays] + [far()] * 2,
        tuple(whole(o.shape) for o in out_shape),
        (1,),
        [
            pltpu.VMEM((steps, width, width), BF),
            pltpu.VMEM((steps, width, width), BF),
            pltpu.SemaphoreType.DMA((2 * steps,)),
        ],
        1,
        arrays + (w_up, w_down),
        scal,
        after,
    )


def input_back_kernel(layer, s, d_first, dq, dkv, odq, odkv, w, gx, w_scr, sems):
    rows, width = d_first.shape
    half = width // 2
    core = s[0] % 2
    steps = w_scr.shape[0]
    tall = width // steps
    copies = fetch([(w.at[layer, pl.ds(n * tall, tall)], w_scr.at[n]) for n in range(steps)], sems)
    for n in range(steps):
        copies[n].wait()
        strip = slice(n * tall, (n + 1) * tall)
        result = d_first[:, strip]
        for at, q_part, kv_part in (
            (core * half, dq[:rows], dkv),
            ((1 - core) * half, odq[rows:], odkv),
        ):
            for i, part in enumerate((q_part, kv_part[:, :half], kv_part[:, half:])):
                columns = pl.ds(pl.multiple_of(i * width + at, 128), half)
                result = result + dot_nt(part, w_scr[n, :, columns])
        gx[:, strip] = result


def input_back_call(layer, scal, d_first, dq, dkv, odq, odkv, w_qkv, after=()):
    rows, width = d_first.shape
    arrays = (d_first, dq, dkv, odq, odkv)
    return call(
        functools.partial(input_back_kernel, layer),
        "input_back",
        sds((rows, width), F32),
        [whole(a.shape) for a in arrays] + [far()],
        whole((rows, width)),
        (1,),
        [pltpu.VMEM((3, width // 3, 3 * width), BF), pltpu.SemaphoreType.DMA((3,))],
        1,
        arrays + (w_qkv,),
        scal,
        after,
    )


def gather_rows(s, turned, picked, order):
    chip, core = s[0] // 2, s[0] % 2
    share = picked.shape[0] // 4
    for at in range(4):
        place = at if order is None else chip ^ order[at]
        begin = pl.multiple_of(place * (2 * share) + core * share, 32)
        picked[at * share : (at + 1) * share, :] = turned[pl.ds(begin, share), :]


def up_grad_kernel(s, x_m, x_o, g_m, g_o, keep, send, turned, picked):
    rows = x_m.shape[0]

    @pl.when(pl.program_id(0) == 0)
    def _():
        turned[:, :rows] = x_m[...].T
        turned[:, rows:] = x_o[...].T
        gather_rows(s, turned, picked, (0, 2, 1, 3))

    grad = dot_nn(picked[:, :rows], g_m[...]) + dot_nn(picked[:, rows:], g_o[...])
    share = picked.shape[0] // 4
    for at in range(2):
        keep[at] = grad[at * share : (at + 1) * share].astype(BF)
        send[at] = grad[(2 + at) * share : (3 + at) * share].astype(BF)


def up_grad_call(scal, x_m, x_o, g_m, g_o, after=()):
    rows, width = x_m.shape
    wide = g_m.shape[1]
    steps = wide // width
    share = width // 8
    out = sds((2, steps * share, width))
    strip = pl.BlockSpec((rows, width), lambda n, s: (0, n))
    block = pl.BlockSpec((2, share, width), lambda n, s: (0, n, 0))
    return call(
        up_grad_kernel,
        "up_grad",
        (out, out),
        [whole(x_m.shape), whole(x_o.shape), strip, strip],
        (block, block),
        (steps,),
        [pltpu.VMEM((width, 2 * rows), BF), pltpu.VMEM((width // 2, 2 * rows), BF)],
        1,
        (x_m, x_o, g_m, g_o),
        scal,
        after,
    )


def down_grad_kernel(s, a_m, a_o, g_m, g_o, keep, send):
    n = pl.program_id(0)
    grad = dot_nn(a_m[...].T, g_m[...]) + dot_nn(a_o[...].T, g_o[...])
    grad = grad.astype(BF)

    @pl.when(n < 2)
    def _():
        keep[...] = grad

    @pl.when(n >= 2)
    def _():
        send[...] = grad


def down_grad_call(scal, a_m, a_o, g_m, g_o, after=()):
    rows, wide = a_m.shape
    width = g_m.shape[1]
    share = wide // 8
    out = sds((2, share, width))
    picked = pl.BlockSpec((rows, share), lambda n, s: (0, 2 * ((s[0] // 2) ^ n) + s[0] % 2))
    return call(
        down_grad_kernel,
        "down_grad",
        (out, out),
        [picked, picked, whole(g_m.shape), whole(g_o.shape)],
        (
            pl.BlockSpec((None, share, width), lambda n, s: (jnp.minimum(n, 1), 0, 0)),
            pl.BlockSpec((None, share, width), lambda n, s: (jnp.maximum(n - 2, 0), 0, 0)),
        ),
        (4,),
        [],
        1,
        (a_m, a_o, g_m, g_o),
        scal,
        after,
    )


def ffn_grad_kernel(s, x_m, x_o, u_m, u_o, a_m, a_o, d_m, d_o, final, out, sems, turned, picked):
    rows, width = x_m.shape
    turned[:, :rows] = x_m[...].T
    turned[:, rows:] = x_o[...].T
    gather_rows(s, turned, picked, None)
    share = picked.shape[0] // 4
    tall = 4 * share
    core = s[0] % 2
    for n in range(u_m.shape[1] // width):
        strip = slice(n * width, (n + 1) * width)
        grad = dot_nn(picked[:, :rows], u_m[:, strip]) + dot_nn(picked[:, rows:], u_o[:, strip])
        for at in range(4):
            out[n, at, :share, :] = grad[at * share : (at + 1) * share].astype(BF)
    copies = []
    for at in range(4):
        columns = pl.ds(pl.multiple_of((2 * at + core) * tall, 128), tall)
        grad = dot_nn(a_m[:, columns].T, d_m[...]) + dot_nn(a_o[:, columns].T, d_o[...])
        for n in range(4):
            out[n, at, share:, :] = grad[n * share : (n + 1) * share].astype(BF)
        copies.append(pltpu.make_async_copy(out.at[:, at], final.at[:, at], sems.at[at]))
        copies[-1].start()
    for copy in copies:
        copy.wait()


def ffn_grad_call(scal, *args, after=()):
    rows, width = args[0].shape
    wide = args[2].shape[1]
    out = kept((4, 4, width // 4, width))
    return call(
        ffn_grad_kernel,
        "ffn_grad",
        out,
        [whole(a.shape) for a in args],
        far(),
        (1,),
        [
            pltpu.VMEM(out.shape, BF),
            pltpu.SemaphoreType.DMA((4,)),
            pltpu.VMEM((width, 2 * rows), BF),
            pltpu.VMEM((width // 2, 2 * rows), BF),
        ],
        1,
        args,
        scal,
        after,
    )


def out_grad_kernel(
    absolute, s, x_m, x_o, dq, dkv_m, dkv_r, odq, odkv_m, odkv_r, att, oatt, b_m, b_o, sums_m,
    sums_o, *refs,
):
    turned, picked = refs[-2:]
    if absolute:
        tops = [refs[0].at[at] for at in range(4)]
        places_a = places_b = tops
        skip = 2 * (x_m.shape[1] // 8)
    else:
        keep_a, send_a, keep_b, send_b = refs[:4]
        places_a = [keep_a.at[0], keep_a.at[1], send_a.at[0], send_a.at[1]]
        places_b = [keep_b.at[0], send_b.at[0], keep_b.at[1], send_b.at[1]]
        skip = 0
    rows, width = x_m.shape
    half = width // 2
    core = s[0] % 2
    share = width // 8
    mine = pl.ds(pl.multiple_of(core * half, 128), half)
    other = pl.ds(pl.multiple_of((1 - core) * half, 128), half)
    turned[:, :rows] = x_m[...].T
    turned[:, rows:] = x_o[...].T
    order = None if absolute else (0, 2, 1, 3)
    gather_rows(s, turned, picked, order)
    left_m, left_o = picked[:, :rows], picked[:, rows:]

    def put(places, begin, grad, columns):
        for at in range(4):
            part = grad[at * share : (at + 1) * share].astype(BF)
            places[at][begin : begin + share, columns] = part

    for at, places, begin in ((0, places_a, 0), (1, places_a, share), (2, places_b, skip)):
        if at == 0:
            pairs = ((dq[:rows], dq[rows:]), (odq[rows:], odq[:rows]))
        else:
            cut = slice((at - 1) * half, at * half)
            pairs = ((dkv_m[:, cut], dkv_r[:, cut]), (odkv_r[:, cut], odkv_m[:, cut]))
        for columns, (mine_rows, other_rows) in zip((mine, other), pairs):
            grad = dot_nn(left_m, mine_rows) + dot_nn(left_o, other_rows)
            put(places, begin, grad, columns)
    turned[mine, :] = att[...].T
    turned[other, :rows] = oatt[rows:].T
    turned[other, rows:] = oatt[:rows].T
    gather_rows(s, turned, picked, order)
    grad = dot_nn(picked[:, :rows], b_m[...]) + dot_nn(picked[:, rows:], b_o[...])
    put(places_b, skip + share, grad, slice(0, width))
    small = (sums_m[...] + sums_o[...]).astype(BF)
    begin = skip + 2 * share
    ends = places_b if absolute else places_a + places_b
    for ref in ends:
        ref[begin:, :] = small
    value = [ref[:, half:] for ref in (dkv_m, dkv_r, odkv_m, odkv_r)]
    for row, parts in ((10, (dq[...], odq[...])), (11, value)):
        count = len(parts) // 2
        for columns, group in ((mine, parts[:count]), (other, parts[count:])):
            line = sum(jnp.sum(p.astype(F32), axis=0, keepdims=True) for p in group).astype(BF)
            for ref in ends:
                ref[begin + row : begin + row + 1, columns] = line


def out_grad_call(scal, absolute, *args, after=()):
    rows, width = args[0].shape
    share = width // 8
    if absolute:
        outs = (kept((4, 4 * share + 16, width)),)
    else:
        outs = (sds((2, 2 * share + 16, width)),) * 4
    return call(
        functools.partial(out_grad_kernel, absolute),
        "out_grad",
        outs,
        [whole(a.shape) for a in args],
        tuple(whole(o.shape) for o in outs),
        (1,),
        [pltpu.VMEM((width, 2 * rows), BF), pltpu.VMEM((width // 2, 2 * rows), BF)],
        1,
        args,
        scal,
        after,
    )


def over_core(array):
    return lax.ppermute(array, "seq", [(i, i ^ 1) for i in range(8)])


def over_x(array):
    return lax.ppermute(array, "seq", [(i, i ^ 2) for i in range(8)])


def over_y(array):
    return lax.ppermute(array, "seq", [(i, i ^ 4) for i in range(8)])


def over_bucket(array, pairs):
    return lax.ppermute(array, "bucket", pairs)


def sum_kernel(s, *refs):
    pairs, out = refs[:-1], refs[-1]
    total = pairs[0][...].astype(F32)
    for ref in pairs[1:]:
        total = total + ref[...].astype(F32)
    out[...] = total.astype(BF)


def sum_call(scal, parts, after=()):
    specs, args = [], []
    for part in parts:
        if isinstance(part, tuple):
            array, at = part
            rows, width = array.shape[1:]
            specs.append(pl.BlockSpec((None, rows, width), lambda i, s, at=at: (at, 0, 0)))
            args.append(array)
        else:
            rows, width = part.shape
            specs.append(whole(part.shape))
            args.append(part)
    return call(
        sum_kernel, "sum", sds((rows, width)), specs, whole((rows, width)), (1,), [],
        1, tuple(args), scal, after,
    )


def join_kernel(s, first, second, more, out):
    out[0] = first[...]
    out[1] = (second[...].astype(F32) + more[...].astype(F32)).astype(BF)


def join_call(scal, first, second, more, after=()):
    rows, width = first.shape
    return call(
        join_kernel, "join", sds((2, rows, width)), [whole(first.shape)] * 3,
        whole((2, rows, width)), (1,), [], 1, (first, second, more), scal, after,
    )


def scatter_call(parts):
    flat = parts.reshape(-1, parts.shape[-1])
    return lax.psum_scatter(
        flat, "seq", scatter_dimension=0, tiled=True,
        axis_index_groups=[[0, 2, 4, 6], [1, 3, 5, 7]],
    )


def over_buckets_first(parts):
    flat = parts.reshape(-1, parts.shape[-1])
    return lax.psum_scatter(flat, "bucket", scatter_dimension=0, tiled=True)


def over_buckets(array, order):
    return lax.psum(array, "bucket", axis_index_groups=[list(order)])


def sort_kernel(s, *refs):
    mine, other = refs[-2:]
    outer = (s[0] == 0) | (s[0] == 3)

    def write(first, second):
        begin = 0
        for at in range(0, len(refs) - 2, 6):
            halves = [refs[at : at + 3], refs[at + 3 : at + 6]]
            size = halves[0][0].shape[0]
            for out, half in ((mine, halves[first]), (other, halves[second])):
                total = sum(ref[...].astype(F32) for ref in half)
                out[begin : begin + size, :] = total.astype(BF)
            begin += size

    @pl.when(outer)
    def _():
        write(0, 1)

    @pl.when(jnp.logical_not(outer))
    def _():
        write(1, 0)


def bucket_start(zscal, groups, after):
    args, specs, total = (), [], 0
    for keep_a, keep_b, got_a, got_b, pass_a, pass_b in groups:
        rows, width = pass_a.shape
        top = pl.BlockSpec((None, rows, width), lambda i, s: (0, 0, 0))
        args += (keep_a, got_a, pass_a, keep_b, got_b, pass_b)
        specs += [top, top, whole((rows, width))] * 2
        total += rows
    flat = (total, width)
    mine, other = call(
        sort_kernel, "sort", (sds(flat),) * 2, specs, (whole(flat),) * 2, (1,), [], 1, args, zscal,
        after,
    )
    return mine, over_bucket(other, NEAR)


def bucket_middle(scal, mine, got, after):
    mine = sum_call(scal, (mine, got), after)
    return mine, over_bucket(mine, FAR)


def bucket_last(scal, mine, got, after):
    mine = sum_call(scal, (mine, got), after)
    return mine, over_bucket(mine, NEAR)


def bucket_end(mine, other):
    place = lax.axis_index("bucket")
    outer = (place == 0) | (place == 3)
    return jnp.where(outer, mine, other), jnp.where(outer, other, mine)


def phase_one(keep_a, send_a, keep_b, send_b):
    return keep_a, keep_b, over_x(send_a), over_y(send_b)


def phase_two(scal, keep_a, keep_b, got_a, got_b, after):
    pass_a = sum_call(scal, ((keep_a, 1), (got_a, 1)), after)
    pass_b = sum_call(scal, ((keep_b, 1), (got_b, 1)), (pass_a,))
    return keep_a, keep_b, got_a, got_b, over_y(pass_a), over_x(pass_b), (pass_b,)


def phase_end(scal, keep_a, keep_b, got_a, got_b, pass_a, pass_b, after):
    own_a = sum_call(scal, ((keep_a, 0), (got_a, 0), pass_a), after)
    own_b = sum_call(scal, ((keep_b, 0), (got_b, 0), pass_b), (own_a,))
    return own_a, own_b


def fast_local(
    frames, w_qkv, b_qv, w_out, b_out, ln_gain, ln_shift, w_up, b_up, w_down, b_down,
    cotangent, clip_lengths, valid_lengths,
):
    rows, width = frames.shape[1:]
    place = lax.axis_index("seq")
    scal = place.astype(jnp.int32)[None]
    zscal = lax.axis_index("bucket").astype(jnp.int32)[None]
    blocks = place ^ jnp.arange(8, dtype=jnp.int32)
    position = (blocks[:, None] * rows + jnp.arange(rows, dtype=jnp.int32)[None]).reshape(-1)
    ends = jnp.cumsum(clip_lengths[0])
    starts = ends - clip_lengths[0]
    inside = (position[:, None] >= starts) & (position[:, None] < ends)
    segment = jnp.sum(jnp.where(inside, jnp.arange(ends.shape[0], dtype=jnp.int32), 0), axis=1)
    live = jnp.any(inside & (position[:, None] < starts + valid_lengths[0]), axis=1)
    tags = jnp.where(live, segment, -1).reshape(8, rows, 1)
    tags = jnp.broadcast_to(tags, (8, rows, 128))
    seg_row = segment[: 2 * rows][None]

    x = frames[0]
    saved = []
    before = ()
    for layer in range(LAYERS):
        attend = functools.partial(attend_call, layer, scal)
        x_r, x_x, x_y = over_core(x), over_x(x), over_y(x)
        kv, q, qt, w_kv, acc, top = attend((), seg_row, w_qkv, b_qv, (x, x_r), tags, (0, 1))
        x_x, x_y = gate((x_x, x_y), (top,))
        x_d = over_y(x_x)
        x_xr, x_yr = over_core(x_x), over_core(x_y)
        kv_x, kv_y, acc, top = attend(
            (qt, w_kv, acc, top), seg_row, w_qkv, b_qv, (x_x, x_xr, x_y, x_yr), tags, (2, 3, 4, 5),
            after=before,
        )
        (x_d,) = gate((x_d,), (top,))
        x_dr = over_core(x_d)
        kv_d, att, ot, lse = attend(
            (qt, w_kv, acc, top), seg_row, w_qkv, b_qv, (x_d, x_dr), tags, (6, 7), last=True
        )
        oatt = over_core(att)
        unit1, rs1, normed, act, slope, unit2, rs2, y = ffn_call(
            layer, scal, x, att, oatt, w_out, b_out, ln_gain, ln_shift, w_up, b_up, w_down, b_down
        )
        before = (over_core(normed), over_core(act))
        saved.append(
            (x, x_r, q, kv, kv_x, kv_y, kv_d, att, oatt, ot, lse)
            + (unit1, rs1, normed, act, slope, unit2, rs2) + before
        )
        x = y
    activations = x[None]

    grad = cotangent[0]
    done = ()
    for layer in reversed(range(LAYERS)):
        top_layer = layer == LAYERS - 1
        x, x_r, q, kv, kv_x, kv_y, kv_d, att, oatt, ot, lse = saved[layer][:11]
        unit1, rs1, normed, act, slope, unit2, rs2, o_normed, o_act = saved[layer][11:]
        normed, act, o_normed, o_act = (stored(a) for a in (normed, act, o_normed, o_act))
        slope, unit1, unit2 = (stored(a) for a in (slope, unit1, unit2))
        d_down, d_up, d_branch, d_first, sums = ffn_back_call(
            layer, scal, grad, unit2, rs2, slope, unit1, rs1, ln_gain, w_up, w_down, done
        )
        o_branch = over_core(d_branch)
        o_up, o_down, o_sums = over_core(d_up), over_core(d_down), over_core(sums)
        done = before if top_layer else ()
        if not top_layer:
            late = phase_two(scal, *late, (sums,))
            parts = out_grad_call(scal, False, *out_args, after=late[-1])
            done = parts[:1]
            middle = phase_one(*parts)
        back = functools.partial(attend_back_call, layer, scal)
        common = (lse, seg_row)
        g_dm, g_dr, *state, dq = back(
            (d_branch, o_branch, ot, q), w_out, common, (kv_d, kv_d), None, tags, (6, 7), after=done
        )
        g_dm, g_dr = over_x(g_dm), over_y(g_dr)
        done = (o_up, o_down, o_sums) + (() if top_layer else late[4:6])
        g_xm, g_xr, g_ym, g_yr, dq = back(
            (*state, dq), None, common, (kv_x, kv_x, kv_y, kv_y), None, tags, (2, 3, 4, 5),
            after=done,
        )
        done = (dq,)
        if not top_layer:
            middle = phase_two(scal, *middle, done)
            done = middle[-1]
        g_x = join_call(scal, g_xm, g_xr, g_dr, done)
        g_y = join_call(scal, g_yr, g_ym, g_dm, (g_x,))
        done = (g_y,)
        g_x, g_y = over_x(g_x), over_y(g_y)
        keep_a, send_a = up_grad_call(scal, normed, o_normed, d_up, o_up, after=done)
        done = (keep_a,)
        if not top_layer:
            early = bucket_start(zscal, (late[:-1], middle[:-1]), done)
            done = early[:1]
        keep_b, send_b = down_grad_call(scal, act, o_act, d_down, o_down, after=done)
        done = (keep_b,)
        late = phase_one(keep_a, send_a, keep_b, send_b)
        g_m, g_r, dq = back(
            (*state, dq), None, common, (kv, kv), None, tags, (0, 1), last=True, after=done
        )
        odq = over_core(dq)
        g_r = sum_call(scal, (g_r, (g_x, 1), (g_y, 0)), (dq,))
        o_r = over_core(g_r)
        g_m = sum_call(scal, (g_m, (g_x, 0), (g_y, 1)), (g_r,))
        o_m = over_core(g_m)
        done = (o_m,)
        grad = input_back_call(layer, scal, d_first, dq, g_m, odq, o_r, w_qkv, after=done)
        done = (grad,)
        out_args = (
            stored(x), stored(x_r), dq, g_m, g_r, odq, o_m, o_r, stored(att), stored(oatt),
            stored(d_branch), stored(o_branch), sums, o_sums,
        )
    early = bucket_middle(scal, *early, done)
    parts = out_grad_call(scal, False, *out_args, after=early[:1])
    last = phase_one(*parts)
    late = phase_two(scal, *late, parts[:1])
    last = phase_two(scal, *last, late[-1])
    early = bucket_last(scal, *early, last[-1])
    late = bucket_start(zscal, (late[:-1],), early[:1])
    last = bucket_start(zscal, (last[:-1],), late[:1])
    late = bucket_middle(scal, *late, last[:1])
    last = bucket_middle(scal, *last, late[:1])
    late = bucket_last(scal, *late, last[:1])
    last = bucket_last(scal, *last, late[:1])
    early, ffn_0, att_0 = (bucket_end(*pair) for pair in (early, late, last))
    half = width // 2
    ffn_parts = (ffn_0, [part[:half] for part in early])
    att_parts = (att_0, [part[half:] for part in early])

    share = width // 8

    def both(make):
        return jnp.stack([make(layer).astype(F32) for layer in range(LAYERS)])

    small = both(lambda l: att_parts[l][0][2 * share :])

    def own(array, axis):
        size = array.shape[axis] // 8
        return lax.dynamic_slice_in_dim(array, place * size, size, axis)

    def beside(array):
        parts = array.shape[0] // share
        return array.reshape(parts, share, width).transpose(1, 0, 2).reshape(share, -1)

    return (
        activations,
        grad[None],
        both(
            lambda l: jnp.concatenate(
                [beside(att_parts[l][0][: 2 * share]), att_parts[l][1][:share]], axis=1
            )
        ),
        own(small[:, 10:12].reshape(LAYERS, -1), 1),
        both(lambda l: att_parts[l][1][share : 2 * share]),
        own(small[:, 4], 1),
        own(small[:, 0:2], 2),
        own(small[:, 2:4], 2),
        both(lambda l: beside(ffn_parts[l][0])),
        own(small[:, 6:10].reshape(LAYERS, -1), 1),
        both(lambda l: ffn_parts[l][1]),
        own(small[:, 5], 1),
    )


def clip_tags(lengths, valid, begin, count):
    position = begin + jnp.arange(count, dtype=jnp.int32)
    ends = jnp.cumsum(lengths)
    starts = ends - lengths
    inside = (position[:, None] >= starts[None, :]) & (position[:, None] < ends[None, :])
    labels = jnp.arange(lengths.shape[0], dtype=jnp.int32)
    segment = jnp.sum(jnp.where(inside, labels[None, :], 0), axis=1)
    live = jnp.any(inside & (position[:, None] < (starts + valid)[None, :]), axis=1)
    return (segment, jnp.where(live, segment, -1))


def layer_norm(hidden, gain, shift):
    center = hidden - jnp.mean(hidden, axis=-1, keepdims=True)
    spread = jnp.mean(center * center, axis=-1, keepdims=True)
    return center * lax.rsqrt(spread + 1e-05) * gain + shift


def exact_gelu(hidden):
    return jax.nn.gelu(hidden, approximate=False)


def split_heads(matrix):
    return matrix.reshape(matrix.shape[0], HEADS, -1)


def pair_terms(
    query_heads,
    grad_heads,
    log_total,
    correction,
    query_seg,
    key_heads,
    value_heads,
    key_tag,
    scale,
):
    scores = (
        jnp.einsum("qhd,khd->hqk", query_heads, key_heads, preferred_element_type=jnp.float32)
        * scale
    )
    allowed = (query_seg[:, None] == key_tag[None, :])[None]
    scores = jnp.where(allowed, scores, -1e30)
    probs = jnp.where(allowed, jnp.exp(scores - log_total[..., None]), 0.0)
    grad_probs = jnp.einsum(
        "qhd,khd->hqk", grad_heads, value_heads, preferred_element_type=jnp.float32
    )
    grad_scores = (probs * (grad_probs - correction[..., None])).astype(jnp.bfloat16)
    return (probs.astype(jnp.bfloat16), grad_scores)


def forward_layer(hidden, weights, query_seg, lengths, valid):
    w_qkv, b_qv, w_out, b_out, gain, shift, w_up, b_up, w_down, b_down = weights
    rows, width = hidden.shape
    scale = (width // HEADS) ** (-0.5)
    inputs = hidden.astype(jnp.bfloat16)
    projected = jnp.dot(inputs, w_qkv, preferred_element_type=jnp.float32)
    queries = (projected[:, :width] + b_qv[:width]).astype(jnp.bfloat16)
    keys = projected[:, width : 2 * width].astype(jnp.bfloat16)
    values = (projected[:, 2 * width :] + b_qv[width:]).astype(jnp.bfloat16)
    query_heads = split_heads(queries)
    initial = (
        jnp.full((HEADS, rows), -1e30, jnp.float32),
        jnp.zeros((HEADS, rows), jnp.float32),
        jnp.zeros((HEADS, rows, width // HEADS), jnp.float32),
    )
    key_piece = lax.all_gather(keys, "seq", axis=0, tiled=True)
    value_piece = lax.all_gather(values, "seq", axis=0, tiled=True)
    count = key_piece.shape[0] // rows
    key_blocks = key_piece.reshape(count, rows, HEADS, -1)
    value_blocks = value_piece.reshape(count, rows, HEADS, -1)

    def fold_inner(state, item):
        key_heads, value_heads, block_at = item
        _, block_tag = clip_tags(lengths, valid, block_at * rows, rows)
        running, denominator, weighted = state
        scores = (
            jnp.einsum("qhd,khd->hqk", query_heads, key_heads, preferred_element_type=jnp.float32)
            * scale
        )
        allowed = (query_seg[:, None] == block_tag[None, :])[None]
        scores = jnp.where(allowed, scores, -1e30)
        raised = jnp.maximum(running, jnp.max(scores, axis=-1))
        block_probs = jnp.where(allowed, jnp.exp(scores - raised[..., None]), 0.0)
        factor = jnp.exp(running - raised)
        denominator = denominator * factor + jnp.sum(block_probs, axis=-1)
        weighted = weighted * factor[..., None] + jnp.einsum(
            "hqk,khd->hqd",
            block_probs.astype(jnp.bfloat16),
            value_heads,
            preferred_element_type=jnp.float32,
        )
        return ((raised, denominator, weighted), None)

    state, _ = lax.scan(
        fold_inner, initial, (key_blocks, value_blocks, jnp.arange(count, dtype=jnp.int32))
    )
    running, denominator, weighted = state
    attended = (weighted / denominator[..., None]).transpose(1, 0, 2).reshape(rows, width)
    log_total = running + jnp.log(denominator)
    attended_low = attended.astype(jnp.bfloat16)
    branch = jnp.dot(attended_low, w_out, preferred_element_type=jnp.float32) + b_out
    first_sum = inputs.astype(jnp.float32) + branch
    normed = layer_norm(first_sum, gain[0], shift[0]).astype(jnp.bfloat16)
    up_pre = jnp.dot(normed, w_up, preferred_element_type=jnp.float32) + b_up
    activated = exact_gelu(up_pre).astype(jnp.bfloat16)
    second_sum = (
        normed.astype(jnp.float32)
        + jnp.dot(activated, w_down, preferred_element_type=jnp.float32)
        + b_down
    )
    output = layer_norm(second_sum, gain[1], shift[1])
    kept = (
        inputs,
        queries,
        keys,
        values,
        attended,
        attended_low,
        log_total,
        None,
        first_sum,
        normed,
        up_pre,
        activated,
        second_sum,
    )
    return (output, kept)


def attention_grads(kept, grad_att, query_seg, lengths, valid):
    (
        inputs,
        queries,
        keys,
        values,
        attended,
        attended_low,
        log_total,
        gathered,
        first_sum,
        normed,
        up_pre,
        activated,
        second_sum,
    ) = kept
    rows, width = queries.shape
    scale = (width // HEADS) ** (-0.5)
    query_heads = split_heads(queries)
    grad_heads = split_heads(grad_att)
    correction = jnp.sum(grad_heads.astype(jnp.float32) * split_heads(attended), axis=-1).T
    key_all, value_all = (
        lax.all_gather(keys, "seq", axis=0, tiled=True),
        lax.all_gather(values, "seq", axis=0, tiled=True),
    )
    count = key_all.shape[0] // rows
    key_blocks = key_all.reshape(count, rows, HEADS, -1)
    value_blocks = value_all.reshape(count, rows, HEADS, -1)
    block_ids = jnp.arange(count, dtype=jnp.int32)
    zero_heads = jnp.zeros((rows, HEADS, width // HEADS), jnp.float32)

    def attention_inner(acc, item):
        key_heads, value_heads, block_at = item
        _, block_tag = clip_tags(lengths, valid, block_at * rows, rows)
        probs, grad_scores = pair_terms(
            query_heads,
            grad_heads,
            log_total,
            correction,
            query_seg,
            key_heads,
            value_heads,
            block_tag,
            scale,
        )
        acc = (
            acc
            + jnp.einsum("hqk,khd->qhd", grad_scores, key_heads, preferred_element_type=jnp.float32)
            * scale
        )
        key_term = (
            jnp.einsum("hqk,qhd->khd", grad_scores, query_heads, preferred_element_type=jnp.float32)
            * scale
        )
        value_term = jnp.einsum(
            "hqk,qhd->khd", probs, grad_heads, preferred_element_type=jnp.float32
        )
        return (
            acc,
            jnp.concatenate(
                [key_term.reshape(rows, width), value_term.reshape(rows, width)], axis=1
            ),
        )

    grad_query, terms = lax.scan(attention_inner, zero_heads, (key_blocks, value_blocks, block_ids))
    summed = lax.psum_scatter(
        terms.reshape(count * rows, 2 * width).astype(jnp.bfloat16),
        "seq",
        scatter_dimension=0,
        tiled=True,
    ).astype(jnp.float32)
    grad_key = summed[:, :width]
    grad_value = summed[:, width:]
    return (grad_query.reshape(rows, width), grad_key, grad_value)


def backward_layer(grad_out, kept, weights, query_seg, lengths, valid):
    w_qkv, b_qv, w_out, b_out, gain, shift, w_up, b_up, w_down, b_down = weights
    (
        inputs,
        queries,
        keys,
        values,
        attended,
        attended_low,
        log_total,
        gathered,
        first_sum,
        normed,
        up_pre,
        activated,
        second_sum,
    ) = kept
    _, pull_second = jax.vjp(layer_norm, second_sum, gain[1], shift[1])
    grad_second, gain_second, shift_second = pull_second(grad_out)
    grad_down = grad_second.astype(jnp.bfloat16)
    sum_down = jnp.sum(grad_down, axis=0, dtype=jnp.float32)
    weight_down = jnp.einsum("rf,rd->fd", activated, grad_down, preferred_element_type=jnp.float32)
    grad_activated = jnp.einsum("rd,fd->rf", grad_down, w_down, preferred_element_type=jnp.float32)
    _, pull_gelu = jax.vjp(exact_gelu, up_pre)
    grad_up = pull_gelu(grad_activated)[0].astype(jnp.bfloat16)
    sum_up = jnp.sum(grad_up, axis=0, dtype=jnp.float32)
    weight_up = jnp.einsum("rd,rf->df", normed, grad_up, preferred_element_type=jnp.float32)
    grad_normed = grad_second + jnp.einsum(
        "rf,df->rd", grad_up, w_up, preferred_element_type=jnp.float32
    )
    _, pull_first = jax.vjp(layer_norm, first_sum, gain[0], shift[0])
    grad_first, gain_first, shift_first = pull_first(grad_normed)
    grad_branch = grad_first.astype(jnp.bfloat16)
    sum_out = jnp.sum(grad_branch, axis=0, dtype=jnp.float32)
    weight_out = jnp.einsum(
        "re,rd->ed", attended_low, grad_branch, preferred_element_type=jnp.float32
    )
    grad_att = jnp.einsum(
        "rd,ed->re", grad_branch, w_out, preferred_element_type=jnp.float32
    ).astype(jnp.bfloat16)
    grad_query, grad_key, grad_value = attention_grads(kept, grad_att, query_seg, lengths, valid)
    grad_proj = jnp.concatenate(
        [
            grad_query.astype(jnp.bfloat16),
            grad_key.astype(jnp.bfloat16),
            grad_value.astype(jnp.bfloat16),
        ],
        axis=1,
    )
    width = inputs.shape[1]
    sum_qv = jnp.concatenate(
        [
            jnp.sum(grad_proj[:, :width], axis=0, dtype=jnp.float32),
            jnp.sum(grad_proj[:, 2 * width :], axis=0, dtype=jnp.float32),
        ]
    )
    weight_qkv = jnp.einsum("rd,re->de", inputs, grad_proj, preferred_element_type=jnp.float32)
    grad_input = grad_first + jnp.einsum(
        "re,de->rd", grad_proj, w_qkv, preferred_element_type=jnp.float32
    )
    gains = jnp.stack([gain_first, gain_second])
    shifts = jnp.stack([shift_first, shift_second])
    return (
        grad_input,
        (
            weight_qkv,
            sum_qv,
            weight_out,
            sum_out,
            gains,
            shifts,
            weight_up,
            sum_up,
            weight_down,
            sum_down,
        ),
    )


def local(
    frames,
    w_qkv,
    b_qv,
    w_out,
    b_out,
    ln_gain,
    ln_shift,
    w_up,
    b_up,
    w_down,
    b_down,
    cotangent,
    clip_lengths,
    valid_lengths,
):
    rows = frames.shape[1]
    lengths = clip_lengths[0]
    valid = valid_lengths[0]
    offset = lax.axis_index("seq") * rows
    query_seg, key_tag = clip_tags(lengths, valid, offset, rows)
    layer_weights = [
        tuple(
            (
                array[layer_at]
                for array in (
                    w_qkv,
                    b_qv,
                    w_out,
                    b_out,
                    ln_gain,
                    ln_shift,
                    w_up,
                    b_up,
                    w_down,
                    b_down,
                )
            )
        )
        for layer_at in range(LAYERS)
    ]
    hidden = frames[0].astype(jnp.float32)
    saved = []
    for layer_at in range(LAYERS):
        hidden, kept = forward_layer(hidden, layer_weights[layer_at], query_seg, lengths, valid)
        saved.append(kept)
    activations = hidden.astype(jnp.bfloat16)[None]
    grad_hidden = cotangent[0].astype(jnp.float32)
    per_layer = [None] * LAYERS
    for layer_at in reversed(range(LAYERS)):
        grad_hidden, per_layer[layer_at] = backward_layer(
            grad_hidden, saved[layer_at], layer_weights[layer_at], query_seg, lengths, valid
        )
    stacked = [
        jnp.stack([per_layer[layer_at][member] for layer_at in range(LAYERS)])
        for member in range(10)
    ]
    g_wqkv, g_bqv, g_wout, g_bout, g_gain, g_shift, g_wup, g_bup, g_wdown, g_bdown = stacked
    shares = (
        lax.psum_scatter(
            g_wqkv.astype(jnp.bfloat16), "seq", scatter_dimension=1, tiled=True
        ).astype(jnp.float32),
        lax.psum_scatter(g_bqv.astype(jnp.bfloat16), "seq", scatter_dimension=1, tiled=True).astype(
            jnp.float32
        ),
        lax.psum_scatter(
            g_wout.astype(jnp.bfloat16), "seq", scatter_dimension=1, tiled=True
        ).astype(jnp.float32),
        lax.psum_scatter(
            g_bout.astype(jnp.bfloat16), "seq", scatter_dimension=1, tiled=True
        ).astype(jnp.float32),
        lax.psum_scatter(
            g_gain.astype(jnp.bfloat16), "seq", scatter_dimension=2, tiled=True
        ).astype(jnp.float32),
        lax.psum_scatter(
            g_shift.astype(jnp.bfloat16), "seq", scatter_dimension=2, tiled=True
        ).astype(jnp.float32),
        lax.psum_scatter(g_wup.astype(jnp.bfloat16), "seq", scatter_dimension=1, tiled=True).astype(
            jnp.float32
        ),
        lax.psum_scatter(g_bup.astype(jnp.bfloat16), "seq", scatter_dimension=1, tiled=True).astype(
            jnp.float32
        ),
        lax.psum_scatter(
            g_wdown.astype(jnp.bfloat16), "seq", scatter_dimension=1, tiled=True
        ).astype(jnp.float32),
        lax.psum_scatter(
            g_bdown.astype(jnp.bfloat16), "seq", scatter_dimension=1, tiled=True
        ).astype(jnp.float32),
    )
    s_wqkv, s_bqv, s_wout, s_bout, s_gain, s_shift, s_wup, s_bup, s_wdown, s_bdown = shares
    totals = (
        lax.psum(s_wqkv.astype(jnp.bfloat16), "bucket").astype(jnp.float32),
        lax.psum(s_bqv.astype(jnp.bfloat16), "bucket").astype(jnp.float32),
        lax.psum(s_wout.astype(jnp.bfloat16), "bucket").astype(jnp.float32),
        lax.psum(s_bout.astype(jnp.bfloat16), "bucket").astype(jnp.float32),
        lax.psum(s_gain.astype(jnp.bfloat16), "bucket").astype(jnp.float32),
        lax.psum(s_shift.astype(jnp.bfloat16), "bucket").astype(jnp.float32),
        lax.psum(s_wup.astype(jnp.bfloat16), "bucket").astype(jnp.float32),
        lax.psum(s_bup.astype(jnp.bfloat16), "bucket").astype(jnp.float32),
        lax.psum(s_wdown.astype(jnp.bfloat16), "bucket").astype(jnp.float32),
        lax.psum(s_bdown.astype(jnp.bfloat16), "bucket").astype(jnp.float32),
    )
    return (
        activations,
        grad_hidden[None],
        totals[0],
        totals[1],
        totals[2],
        totals[3],
        totals[4],
        totals[5],
        totals[6],
        totals[7],
        totals[8],
        totals[9],
    )


def solution(mesh):
    placed = (
        P("bucket", "seq", None),
        P(),
        P(),
        P(),
        P(),
        P(),
        P(),
        P(),
        P(),
        P(),
        P(),
        P("bucket", "seq", None),
        P("bucket", None),
        P("bucket", None),
    )
    chips_2x2 = mesh.shape["seq"] == 8 and mesh.shape["bucket"] == 4
    return jax.shard_map(
        fast_local if chips_2x2 else local,
        mesh=mesh,
        in_specs=placed,
        out_specs=(
            P("bucket", "seq", None),
            P("bucket", "seq", None),
            P(None, "seq", None),
            P(None, "seq"),
            P(None, "seq", None),
            P(None, "seq"),
            P(None, None, "seq"),
            P(None, None, "seq"),
            P(None, "seq", None),
            P(None, "seq"),
            P(None, "seq", None),
            P(None, "seq"),
        ),
        check_vma=False,
    )
```

```python
import functools
import math

import jax
import jax.numpy as jnp
from jax import lax
from jax.experimental import pallas as pl
from jax.experimental.pallas import tpu as pltpu
from jax.sharding import PartitionSpec as P

HEADS = 12
LAYERS = 2
NEAR = [(0, 1), (1, 0), (2, 3), (3, 2)]
FAR = [(0, 3), (3, 0), (1, 2), (2, 1)]
BF = jnp.bfloat16
F32 = jnp.float32
LOW = -1e30
SLACK = 6 * 1024 * 1024


def dot_nn(a, b):
    return lax.dot_general(a, b, (((1,), (0,)), ((), ())), preferred_element_type=F32)


def dot_nt(a, b):
    return lax.dot_general(a, b, (((1,), (1,)), ((), ())), preferred_element_type=F32)


def block_bytes(spec, array):
    if spec.block_shape is None:
        return 0
    lanes = [n for n in spec.block_shape if n is not None]
    lanes[-1] += -lanes[-1] % 128
    return math.prod(lanes) * array.dtype.itemsize


def call(body, name, out_shape, in_specs, out_specs, grid, scratch, flops, args, scalars, after=()):
    args = tuple(
        stored(a) if p.memory_space == pltpu.HBM else a for p, a in zip(in_specs, args)
    )
    count = len(args)

    def run(scal, *refs):
        body(scal, *refs[:count], *refs[count + len(after) :])

    need = sum(block_bytes(p, a) for p, a in zip(in_specs, args))
    need += sum(block_bytes(p, a) for p, a in zip(jax.tree.leaves(out_specs), jax.tree.leaves(out_shape)))
    need = need + sum(
        math.prod(m.shape) * jnp.dtype(m.dtype).itemsize for m in scratch if m.memory_space == pltpu.VMEM
    )
    return pl.pallas_call(
        run,
        name=name,
        out_shape=out_shape,
        grid_spec=pltpu.PrefetchScalarGridSpec(
            num_scalar_prefetch=1,
            grid=grid,
            in_specs=list(in_specs) + [pl.BlockSpec(memory_space=pl.ANY)] * len(after),
            out_specs=out_specs,
            scratch_shapes=scratch,
        ),
        compiler_params=pltpu.CompilerParams(vmem_limit_bytes=need + SLACK),
        cost_estimate=pl.CostEstimate(
            flops=int(flops), bytes_accessed=1 + int(flops / 400), transcendentals=0
        ),
    )(scalars, *args, *after)


def whole(shape):
    return pl.BlockSpec(shape, lambda i, s: (0,) * len(shape))


def kept(shape, dtype=BF):
    return pltpu.HBM(shape, dtype)


def near(shape, dtype=BF):
    return pltpu.VMEM(shape, dtype)


def held(array):
    return pltpu.with_memory_space_constraint(array, pltpu.VMEM)


def stored(array):
    return pltpu.with_memory_space_constraint(array, pltpu.HBM)


def gate(arrays, after, space=pltpu.VMEM):
    anywhere = pl.BlockSpec(memory_space=pl.ANY)
    count = len(arrays)

    def body(*refs):
        pass

    return pl.pallas_call(
        body,
        name="gate",
        out_shape=tuple(sds(a.shape, a.dtype) for a in arrays),
        in_specs=[anywhere] * (count + len(after)),
        out_specs=(anywhere,) * count,
        input_output_aliases={i: i for i in range(count)},
        compiler_params=pltpu.CompilerParams(vmem_limit_bytes=1024 * 1024),
        cost_estimate=pl.CostEstimate(flops=1, bytes_accessed=1, transcendentals=0),
    )(*(pltpu.with_memory_space_constraint(a, space) for a in arrays), *after)


def far():
    return pl.BlockSpec(memory_space=pltpu.HBM)


def fetch(pairs, sems):
    copies = [pltpu.make_async_copy(src, dst, sems.at[i]) for i, (src, dst) in enumerate(pairs)]
    for copy in copies:
        copy.start()
    return copies


def sds(shape, dtype=BF):
    return jax.ShapeDtypeStruct(shape, dtype)


def attend_kernel(layer, chips, first, last, *refs):
    refs = list(refs)
    core = refs.pop(0)[0] % 2
    if not first:
        qt, w_all, acc_in, m_in = (refs.pop(0) for _ in range(4))
    seg_ref, bias_ref, bias_k, w_ref = (refs.pop(0) for _ in range(4))
    xs = [refs.pop(0) for _ in range(2 * chips)]
    tags = [refs.pop(0) for _ in range(2 * chips)]
    kv_outs = [refs.pop(0) for _ in range(chips)]
    q_outs = [refs.pop(0) for _ in range(chips)]
    if first:
        qt, w_all = (refs.pop(0) for _ in range(2))
    if last:
        att_ref = refs.pop(0)
    else:
        acc_out, m_out = refs.pop(0), refs.pop(0)
    s_scr, vt_scr, kvs, qs, out_sems = (refs.pop(0) for _ in range(5))
    rows, width = xs[0].shape
    half = width // 2
    heads = half // 64
    queries = seg_ref.shape[1]
    high = vt_scr.shape[1]
    pair = 2 * rows
    leaving = []

    def leave(src, dst):
        copy = pltpu.make_async_copy(src, dst, out_sems.at[len(leaving)])
        copy.start()
        leaving.append(copy)

    if first:
        sems = refs.pop(0)
        begin = [pl.multiple_of(width * i + core * half, 128) for i in range(3)]
        copies = fetch(
            [(w_ref.at[layer, :, pl.ds(begin[i], half)], w_all.at[i]) for i in range(3)], sems
        )
    bias_q = bias_ref[layer : layer + 1, :]
    bias_v = bias_k[layer : layer + 1, :]
    for c in range(chips):
        x = jnp.concatenate([xs[2 * c][...], xs[2 * c + 1][...]], axis=0)
        if first:
            copies.pop(0).wait()
        q = (dot_nn(x, w_all[0]) + bias_q).astype(BF) * BF(0.125)
        qs[c] = q
        leave(qs.at[c], q_outs[c])
        if first:
            qt[...] = q.T
            copies.pop(0).wait()
            copies.pop(0).wait()
        kvs[c, :, :half] = dot_nn(x, w_all[1]).astype(BF)
        values = (dot_nn(x, w_all[2]) + bias_v).astype(BF)
        kvs[c, :, half:] = values
        leave(kvs.at[c], kv_outs[c])
        turned = values.T
        for h in range(heads):
            vt_scr[h, :64, c * pair : (c + 1) * pair] = turned[h * 64 : (h + 1) * 64]
    vt_scr[:, 64:, :] = jnp.ones((heads, high - 64, chips * pair), BF)
    seg = seg_ref[...]
    outs, lses = [], []
    if not last:
        m_out[...] = jnp.zeros_like(m_out)
    for h in range(heads):
        qh = qt[h * 64 : (h + 1) * 64, :]
        m8 = None
        for b in range(2 * chips):
            key = slice((b % 2) * rows, (b % 2 + 1) * rows)
            scores = dot_nn(kvs[b // 2, key, h * 64 : (h + 1) * 64], qh)
            ok = jnp.concatenate([tags[b][...]] * (queries // 128), axis=1) == seg
            scores = jnp.where(ok, scores, LOW)
            s_scr[h % 2, b * rows : (b + 1) * rows, :] = scores
            top = jnp.max(scores.reshape(rows // 8, 8, queries), axis=0)
            m8 = top if m8 is None else jnp.maximum(m8, top)
        m = jnp.max(m8, axis=0, keepdims=True)
        if not first:
            m_old = m_in[h : h + 1, :]
            m = jnp.maximum(m, m_old)
        acc = jnp.zeros((high, queries), F32)
        for b in range(2 * chips):
            probs = jnp.exp(s_scr[h % 2, b * rows : (b + 1) * rows, :] - m).astype(BF)
            acc = acc + dot_nn(vt_scr[h, :, b * rows : (b + 1) * rows], probs)
        if not first:
            acc = acc + acc_in[h] * jnp.exp(m_old - m)
        if last:
            total = acc[64:65]
            outs.append((acc[:64] / total).astype(BF))
            lses.append(m + jnp.log(total))
        else:
            acc_out[h] = acc
            m_out[h : h + 1, :] = m
    if last:
        lse = jnp.concatenate(lses, axis=0)
        top = lse.astype(BF).astype(F32)
        rest = jnp.zeros((128 - 2 * heads, queries), F32)
        tail = jnp.concatenate([top, lse - top, rest], axis=0)
        att_ref[:, :half] = jnp.concatenate(outs, axis=0).T
        att_ref[:, half:] = tail.T.astype(BF)
    for copy in leaving:
        copy.wait()


def tag_specs(tag_ids, rows):
    return [pl.BlockSpec((None, rows, 128), lambda i, s, r=r: (r, 0, 0)) for r in tag_ids]


def attend_call(layer, scal, state, seg_row, w_qkv, b_qv, xs, tags, tag_ids, last=False, after=()):
    first = not state
    rows, width = xs[0].shape
    half = width // 2
    heads = half // 64
    queries = 2 * rows
    chips = len(xs) // 2
    high = 80
    out_shape = tuple(kept((2 * rows, width)) for _ in range(chips))
    out_shape += tuple(kept((2 * rows, half)) for _ in range(chips))
    if first:
        out_shape += (near((half, queries)), near((3, width, half)))
    if last:
        out_shape += (sds((queries, half + 128)),)
    else:
        out_shape += (near((heads, high, queries), F32), near((8, queries), F32))
    out_specs = [whole(o.shape) for o in out_shape]
    for i in range(2 * chips):
        out_specs[i] = far()

    def bias(part):
        return pl.BlockSpec((LAYERS, half), lambda i, s: (0, 2 * part + s[0] % 2))

    state = tuple(held(a) for a in state)
    specs = [whole(a.shape) for a in state]
    specs += [whole(seg_row.shape), bias(0), bias(1), far()]
    specs += [whole(x.shape) for x in xs] + tag_specs(tag_ids, rows)
    args = state + (seg_row, b_qv, b_qv, w_qkv) + tuple(xs) + (tags,) * len(xs)
    scratch = [
        pltpu.VMEM((2, chips * 2 * rows, queries), F32),
        pltpu.VMEM((heads, high, chips * 2 * rows), BF),
        pltpu.VMEM((chips, 2 * rows, width), BF),
        pltpu.VMEM((chips, 2 * rows, half), BF),
        pltpu.SemaphoreType.DMA((2 * chips,)),
    ]
    if first:
        scratch.append(pltpu.SemaphoreType.DMA((3,)))
    return call(
        functools.partial(attend_kernel, layer, chips, first, last),
        "attend",
        out_shape,
        specs,
        tuple(out_specs),
        (1,),
        scratch,
        chips * 12 * 4 * queries * half * rows,
        args,
        scal,
        after,
    )


def back_queries(core, ext_m, ext_r, w_out, turned_scr):
    rows, wide = ext_m.shape
    width = wide - 128
    ext = jnp.concatenate([ext_m[...], ext_r[...]], axis=0)
    grad = dot_nt(ext[:, :width], w_out).astype(BF)
    turned_scr[...] = ext[:, width:].T.astype(F32)
    part = turned_scr[pl.ds(pl.multiple_of(core * 64, 64), 64), :]
    heads = width // 128
    lse = part[:heads] + part[heads : 2 * heads]
    corr = part[2 * heads : 3 * heads] + part[3 * heads : 4 * heads]
    return grad, grad.T, lse, corr


def pair_terms_kernel(keys, values, qt, dot, lse, corr, ok):
    scores = dot_nn(keys, qt)
    grad = dot_nn(values, dot)
    probs = jnp.exp(jnp.where(ok, scores - lse, LOW))
    return probs.astype(BF), (probs * (grad - corr)).astype(BF)


def back_own_kernel(
    layer, s, ext_m, ext_r, q, seg_ref, kv, tag_m, tag_r, w_ref,
    w_out, qt, dot, stats, dq, dkv, kv_out, tag_out, turned_scr, sems,
):
    core = s[0] % 2
    rows = ext_m.shape[0]
    half = q.shape[1]
    heads = half // 64
    queries = 2 * rows
    (copy,) = fetch(
        [(w_ref.at[layer, pl.ds(pl.multiple_of(core * half, 128), half)], w_out)], sems
    )
    kv_out[...] = kv[...]
    tag_out[0] = tag_m[...]
    tag_out[1] = tag_r[...]
    qt[...] = q[...].T
    copy.wait()
    do, turned, lse, corr = back_queries(core, ext_m, ext_r, w_out[...], turned_scr)
    dot[...] = turned
    stats[...] = jnp.zeros_like(stats)
    stats[:heads, :] = lse
    stats[8 : 8 + heads, :] = corr
    seg = seg_ref[...]
    for b in range(2):
        key = slice(b * rows, (b + 1) * rows)
        kt = kv[key, :half].T
        ok = jnp.concatenate([tag_out[b]] * (queries // 128), axis=1) == seg
        for h in range(heads):
            sl = slice(h * 64, (h + 1) * 64)
            vl = slice(half + h * 64, half + (h + 1) * 64)
            probs, grad = pair_terms_kernel(
                kv[key, sl], kv[key, vl], qt[sl, :], dot[sl, :], lse[h : h + 1],
                corr[h : h + 1], ok,
            )
            term = dot_nn(kt[sl], grad)
            if b == 0:
                dq[sl, :] = term
            else:
                dq[sl, :] += term
            dkv[key, sl] = dot_nn(grad, q[:, sl])
            dkv[key, vl] = dot_nn(probs, do[:, sl])


def back_own_call(layer, scal, ext_m, ext_r, q, seg_rows, kv, tags, w_out, after=()):
    rows = ext_m.shape[0]
    queries, half = q.shape
    width = 2 * half
    out_shape = (
        near((half, width)), near((half, queries)), near((half, queries)),
        near((16, queries), F32), near((half, queries), F32), near((queries, width), F32),
        near((queries, width)), near((2, rows, 128), jnp.int32),
    )
    return call(
        functools.partial(back_own_kernel, layer),
        "back_own",
        out_shape,
        [whole(ext_m.shape), whole(ext_r.shape), whole(q.shape), seg_spec(queries, 0), whole(kv.shape)]
        + tag_specs((0, 1), rows) + [far()],
        tuple(whole(o.shape) for o in out_shape),
        (1,),
        [pltpu.VMEM((128, queries), F32), pltpu.SemaphoreType.DMA((1,))],
        1,
        (ext_m, ext_r, q, seg_rows, kv, tags, tags, w_out),
        scal,
        after,
    )


def seg_spec(queries, at):
    return pl.BlockSpec((1, queries), lambda i, s: (0, at))


def back_dq_kernel(chips, last, s, *refs):
    refs = list(refs)
    qt, dot, stats, dq_in, seg_ref = (refs.pop(0) for _ in range(5))
    kvs = [refs.pop(0) for _ in range(chips)]
    tags = [refs.pop(0) for _ in range(2 * chips)]
    dq_out, dq_scr, kv_scr, sems = refs
    copies = fetch([(kvs[c], kv_scr.at[c]) for c in range(chips)], sems)
    rows = tags[0].shape[0]
    half, queries = qt.shape
    heads = half // 64
    seg = seg_ref[...]
    dq_scr[...] = dq_in[...]
    for c in range(chips):
        copies[c].wait()
        for b in range(2):
            key = slice(b * rows, (b + 1) * rows)
            kt = kv_scr[c, key, :half].T
            ok = jnp.concatenate([tags[2 * c + b][...]] * (queries // 128), axis=1) == seg
            for h in range(heads):
                sl = slice(h * 64, (h + 1) * 64)
                vl = slice(half + h * 64, half + (h + 1) * 64)
                _, grad = pair_terms_kernel(
                    kv_scr[c, key, sl], kv_scr[c, key, vl], qt[sl, :], dot[sl, :],
                    stats[h : h + 1, :], stats[8 + h : 9 + h, :], ok,
                )
                dq_scr[sl, :] += dot_nn(kt[sl], grad)
    if last:
        dq_out[...] = (dq_scr[...] * 0.125).astype(BF).T
    else:
        dq_out[...] = dq_scr[...]


def back_dq_call(scal, qt, dot, stats, dq, seg_rows, kvs, tags, tag_ids, last, after=()):
    half, queries = qt.shape
    rows = queries // 2
    chips = len(kvs)
    state = tuple(held(a) for a in (qt, dot, stats, dq))
    out = sds((queries, half)) if last else near((half, queries), F32)
    return call(
        functools.partial(back_dq_kernel, chips, last),
        "back_dq",
        out,
        [whole(a.shape) for a in state] + [seg_spec(queries, 0)] + [far()] * chips
        + tag_specs(tag_ids, rows),
        whole(out.shape),
        (1,),
        [
            pltpu.VMEM((half, queries), F32),
            pltpu.VMEM((chips, queries, 2 * half), BF),
            pltpu.SemaphoreType.DMA((chips,)),
        ],
        1,
        state + (seg_rows,) + tuple(kvs) + (tags,) * (2 * chips),
        scal,
        after,
    )


def back_dkv_kernel(chips, last, s, *refs):
    refs = list(refs)
    w_out, kv, tag, dkv_in = (refs.pop(0) for _ in range(4))
    exts = [refs.pop(0) for _ in range(2 * chips)]
    qs = [refs.pop(0) for _ in range(chips)]
    segs = [refs.pop(0) for _ in range(chips)]
    if last:
        out_m, out_r = refs.pop(0), refs.pop(0)
    else:
        dkv_out = refs.pop(0)
    dkv, q_scr, turned_scr, sems = refs
    copies = fetch([(qs[c], q_scr.at[c]) for c in range(chips)], sems)
    core = s[0] % 2
    rows = exts[0].shape[0]
    half, width = w_out.shape
    heads = half // 64
    queries = 2 * rows
    dkv[...] = dkv_in[...]
    for c in range(chips):
        do, dot, lse, corr = back_queries(
            core, exts[2 * c], exts[2 * c + 1], w_out[...], turned_scr
        )
        copies[c].wait()
        q = q_scr[c]
        qt = q.T
        seg = segs[c][...]
        for b in range(2):
            key = slice(b * rows, (b + 1) * rows)
            ok = jnp.concatenate([tag[b]] * (queries // 128), axis=1) == seg
            for h in range(heads):
                sl = slice(h * 64, (h + 1) * 64)
                vl = slice(half + h * 64, half + (h + 1) * 64)
                probs, grad = pair_terms_kernel(
                    kv[key, sl], kv[key, vl], qt[sl], dot[sl], lse[h : h + 1], corr[h : h + 1], ok
                )
                dkv[key, sl] += dot_nn(grad, q[:, sl])
                dkv[key, vl] += dot_nn(probs, do[:, sl])
    if last:
        out_m[...] = dkv[:rows, :].astype(BF)
        out_r[...] = dkv[rows:, :].astype(BF)
    else:
        dkv_out[...] = dkv[...]


def back_dkv_call(scal, w_out, kv, tag, dkv, exts, qs, seg_rows, seg_ids, last, after=()):
    queries, width = kv.shape
    rows, half = queries // 2, width // 2
    chips = len(qs)
    state = tuple(held(a) for a in (w_out, kv, tag, dkv))
    flat = sds((rows, width))
    out_shape = (flat, flat) if last else (near((queries, width), F32),)
    return call(
        functools.partial(back_dkv_kernel, chips, last),
        "back_dkv",
        out_shape,
        [whole(a.shape) for a in state] + [whole(e.shape) for e in exts] + [far()] * chips
        + [seg_spec(queries, at) for at in seg_ids],
        tuple(whole(o.shape) for o in out_shape),
        (1,),
        [
            pltpu.VMEM((queries, width), F32),
            pltpu.VMEM((chips, queries, half), BF),
            pltpu.VMEM((128, queries), F32),
            pltpu.SemaphoreType.DMA((chips,)),
        ],
        1,
        state + tuple(exts) + tuple(qs) + (seg_rows,) * chips,
        scal,
        after,
    )


def normalize(hidden):
    center = hidden - jnp.mean(hidden, axis=-1, keepdims=True)
    spread = lax.rsqrt(jnp.mean(center * center, axis=-1, keepdims=True) + 1e-05)
    return center * spread, spread


def normalize_back(grad, unit, spread, gain):
    scaled = grad * gain
    mean = jnp.mean(scaled, axis=-1, keepdims=True)
    along = jnp.mean(scaled * unit, axis=-1, keepdims=True)
    return spread * (scaled - mean - unit * along)


def gauss(up):
    size = jnp.abs(up)
    bell = jnp.exp(-0.5 * up * up)
    t = 1.0 / (1.0 + 0.23164189 * size)
    poly = 0.5307027145 * t - 0.7265760135
    poly = poly * t + 0.7107068705
    poly = poly * t - 0.142248368
    poly = poly * t + 0.127414796
    tail = poly * t * bell
    return jnp.where(up < 0, tail, 1.0 - tail), bell


def ffn_kernel(
    layer, s, x, att, oatt, b_out, gain, shift, b_up, b_down, w_out, w_up, w_down,
    unit1, rs1, normed, act, slope, unit2, rs2, y, kept_scr, unit_scr, kept_sems, out_scr,
    up_scr, down_scr, sems,
):
    rows, width = x.shape
    half = width // 2
    core = s[0] % 2
    steps = up_scr.shape[0]
    pairs = [(w_out.at[layer], out_scr)]
    for n in range(steps):
        strip = pl.ds(n * width, width)
        pairs += [(w_up.at[layer, :, strip], up_scr.at[n]), (w_down.at[layer, strip], down_scr.at[n])]
    copies = fetch(pairs, sems)
    copies[0].wait()
    mine = pl.multiple_of(core * half, 128)
    other = pl.multiple_of((1 - core) * half, 128)
    branch = dot_nn(att[:rows, :half], out_scr[pl.ds(mine, half), :])
    branch = branch + dot_nn(oatt[rows:, :half], out_scr[pl.ds(other, half), :])
    first = x[...].astype(F32) + branch + b_out[layer : layer + 1, :]
    unit, spread = normalize(first)
    unit_scr[0] = unit
    leaving = [pltpu.make_async_copy(unit_scr.at[0], unit1, kept_sems.at[2 * steps])]
    leaving[0].start()
    rs1[...] = jnp.broadcast_to(spread, rs1.shape)
    low = (unit * gain[layer, 0:1, :] + shift[layer, 0:1, :]).astype(BF)
    normed[...] = low
    total = low.astype(F32) + b_down[layer : layer + 1, :]
    for n in range(steps):
        strip = slice(n * width, (n + 1) * width)
        copies[1 + 2 * n].wait()
        up = dot_nn(normed[...], up_scr[n]) + b_up[layer : layer + 1, strip]
        phi, bell = gauss(up)
        low = (up * phi).astype(BF)
        kept_scr[0, :, strip] = low
        kept_scr[1, :, strip] = (phi + up * (0.3989422804014327 * bell)).astype(BF)
        for i, ref in enumerate((act, slope)):
            copy = pltpu.make_async_copy(
                kept_scr.at[i, :, strip], ref.at[:, strip], kept_sems.at[2 * n + i]
            )
            copy.start()
            leaving.append(copy)
        copies[2 + 2 * n].wait()
        total = total + dot_nn(low, down_scr[n])
    unit, spread = normalize(total)
    unit_scr[1] = unit
    leaving.append(pltpu.make_async_copy(unit_scr.at[1], unit2, kept_sems.at[2 * steps + 1]))
    leaving[-1].start()
    rs2[...] = jnp.broadcast_to(spread, rs2.shape)
    y[...] = (unit * gain[layer, 1:2, :] + shift[layer, 1:2, :]).astype(BF)
    for copy in leaving:
        copy.wait()


def ffn_call(
    layer, scal, x, att, oatt, w_out, b_out, gain, shift, w_up, b_up, w_down, b_down, after=()
):
    rows, width = x.shape
    wide = w_up.shape[2]
    steps = wide // width
    vec = sds((rows, 128), F32)
    out_shape = (
        kept((rows, width), F32), vec, sds((rows, width)), kept((rows, wide)), kept((rows, wide)),
        kept((rows, width), F32), vec, sds((rows, width)),
    )
    out_specs = [whole(o.shape) for o in out_shape]
    for i in (0, 3, 4, 5):
        out_specs[i] = far()
    arrays = (x, att, oatt, b_out, gain, shift, b_up, b_down)
    return call(
        functools.partial(ffn_kernel, layer),
        "ffn",
        out_shape,
        [whole(a.shape) for a in arrays] + [far()] * 3,
        tuple(out_specs),
        (1,),
        [
            pltpu.VMEM((2, rows, wide), BF),
            pltpu.VMEM((2, rows, width), F32),
            pltpu.SemaphoreType.DMA((2 * steps + 2,)),
            pltpu.VMEM((width, width), BF),
            pltpu.VMEM((steps, width, width), BF),
            pltpu.VMEM((steps, width, width), BF),
            pltpu.SemaphoreType.DMA((1 + 2 * steps,)),
        ],
        4 * rows * width * wide + 2 * rows * width * width,
        arrays + (w_out, w_up, w_down),
        scal,
        after,
    )


def ffn_back_kernel(
    layer, s, gy, unit2, rs2, slope, unit1, rs1, gain, att, oatt, w_up, w_down, w_out,
    d_down, d_up, d_up_more, d_branch, d_first, sums, up_scr, down_scr, out_scr, sems,
):
    steps = up_scr.shape[0]
    rows, width = gy.shape
    half = width // 2
    core = s[0] % 2
    pairs = []
    for n in range(steps):
        strip = pl.ds(n * width, width)
        pairs += [(w_down.at[layer, strip], down_scr.at[n]), (w_up.at[layer, :, strip], up_scr.at[n])]
    pairs.append((w_out.at[layer], out_scr))
    copies = fetch(pairs, sems)
    grad = gy[...].astype(F32)
    unit = unit2[...]
    total = normalize_back(grad, unit, rs2[:, 0:1], gain[layer, 1:2, :])
    sums[...] = jnp.zeros_like(sums)
    sums[1:2, :] = jnp.sum(grad * unit, axis=0, keepdims=True)
    sums[3:4, :] = jnp.sum(grad, axis=0, keepdims=True)
    low = total.astype(BF)
    d_down[...] = low
    sums[5:6, :] = jnp.sum(low.astype(F32), axis=0, keepdims=True)
    for n in range(steps):
        strip = slice(n * width, (n + 1) * width)
        copies[2 * n].wait()
        low = (dot_nt(d_down[...], down_scr[n]) * slope[:, strip].astype(F32)).astype(BF)
        ref, at = (d_up, n) if n < steps // 2 else (d_up_more, n - steps // 2)
        ref[:, at * width : (at + 1) * width] = low
        sums[6 + n : 7 + n, :] = jnp.sum(low.astype(F32), axis=0, keepdims=True)
        copies[2 * n + 1].wait()
        total = total + dot_nt(low, up_scr[n])
    unit = unit1[...]
    first = normalize_back(total, unit, rs1[:, 0:1], gain[layer, 0:1, :])
    sums[0:1, :] = jnp.sum(total * unit, axis=0, keepdims=True)
    sums[2:3, :] = jnp.sum(total, axis=0, keepdims=True)
    d_first[...] = first
    low = first.astype(BF)
    d_branch[:, :width] = low
    sums[4:5, :] = jnp.sum(low.astype(F32), axis=0, keepdims=True)
    copies[-1].wait()
    row = lax.broadcasted_iota(jnp.int32, (128, 128), 0)
    column = lax.broadcasted_iota(jnp.int32, (128, 128), 1)
    heads = half // 64
    stats = jnp.zeros((rows, 128), F32)
    tall = lax.broadcasted_iota(jnp.int32, (half, 128), 0)
    wide = lax.broadcasted_iota(jnp.int32, (half, 128), 1)
    for at, part in ((core, att[:rows]), (1 - core, oatt[rows:])):
        move = (row < 2 * heads) & (column == at * 64 + row)
        stats = stats + dot_nn(part[:, half:], jnp.where(move, 1.0, 0.0).astype(BF))
        grad = dot_nt(low, out_scr[pl.ds(pl.multiple_of(at * half, 128), half), :])
        product = grad.astype(BF).astype(F32) * part[:, :half].astype(F32)
        place = wide - at * 64 - 2 * heads
        pick = (place == tall // 64) | (place == tall // 64 + heads)
        stats = stats + lax.dot_general(
            product, jnp.where(pick, 1.0, 0.0), (((1,), (0,)), ((), ())),
            precision=lax.Precision.HIGHEST, preferred_element_type=F32,
        )
    top = stats.astype(BF)
    lane = lax.broadcasted_iota(jnp.int32, (rows, 128), 1) % 64
    under = (lane >= 3 * heads) & (lane < 4 * heads)
    d_branch[:, width:] = jnp.where(under, stats - top.astype(F32), stats).astype(BF)


def ffn_back_call(
    layer, scal, gy, unit2, rs2, slope, unit1, rs1, gain, att, oatt, w_up, w_down, w_out, after=()
):
    rows, width = gy.shape
    wide = w_up.shape[2]
    steps = wide // width
    out_shape = (
        sds((rows, width)), sds((rows, wide // 2)), sds((rows, wide // 2)),
        sds((rows, width + 128)), sds((rows, width), F32),
        sds((16, width), F32),
    )
    arrays = (gy, unit2, rs2, slope, unit1, rs1, gain, att, oatt)
    return call(
        functools.partial(ffn_back_kernel, layer),
        "ffn_back",
        out_shape,
        [whole(a.shape) for a in arrays] + [far()] * 3,
        tuple(whole(o.shape) for o in out_shape),
        (1,),
        [
            pltpu.VMEM((steps, width, width), BF),
            pltpu.VMEM((steps, width, width), BF),
            pltpu.VMEM((width, width), BF),
            pltpu.SemaphoreType.DMA((2 * steps + 1,)),
        ],
        1,
        arrays + (w_up, w_down, w_out),
        scal,
        after,
    )


def input_back_kernel(layer, s, d_first, dq, dkv, odq, odkv, w, gx, w_scr, sems):
    rows, width = d_first.shape
    half = width // 2
    core = s[0] % 2
    steps = w_scr.shape[0]
    tall = width // steps
    copies = fetch([(w.at[layer, pl.ds(n * tall, tall)], w_scr.at[n]) for n in range(steps)], sems)
    for n in range(steps):
        copies[n].wait()
        strip = slice(n * tall, (n + 1) * tall)
        result = d_first[:, strip]
        for at, q_part, kv_part in (
            (core * half, dq[:rows], dkv),
            ((1 - core) * half, odq[rows:], odkv),
        ):
            for i, part in enumerate((q_part, kv_part[:, :half], kv_part[:, half:])):
                columns = pl.ds(pl.multiple_of(i * width + at, 128), half)
                result = result + dot_nt(part, w_scr[n, :, columns])
        gx[:, strip] = result


def input_back_call(layer, scal, d_first, dq, dkv, odq, odkv, w_qkv, after=()):
    rows, width = d_first.shape
    arrays = (d_first, dq, dkv, odq, odkv)
    return call(
        functools.partial(input_back_kernel, layer),
        "input_back",
        sds((rows, width), F32),
        [whole(a.shape) for a in arrays] + [far()],
        whole((rows, width)),
        (1,),
        [pltpu.VMEM((3, width // 3, 3 * width), BF), pltpu.SemaphoreType.DMA((3,))],
        1,
        arrays + (w_qkv,),
        scal,
        after,
    )


def gather_rows(s, turned, picked, order):
    chip, core = s[0] // 2, s[0] % 2
    share = picked.shape[0] // 4
    for at in range(4):
        place = at if order is None else chip ^ order[at]
        begin = pl.multiple_of(place * (2 * share) + core * share, 32)
        picked[at * share : (at + 1) * share, :] = turned[pl.ds(begin, share), :]


def up_grad_kernel(s, x_m, x_o, *refs):
    keep, send, turned, picked = refs[-4:]
    rows, width = x_m.shape
    turned[:, :rows] = x_m[...].T
    turned[:, rows:] = x_o[...].T
    gather_rows(s, turned, picked, (0, 2, 1, 3))
    share = picked.shape[0] // 4
    steps = keep.shape[1] // share
    for n in range(steps):
        g_m, g_o = refs[:2] if n < steps // 2 else refs[2:4]
        at = n % (steps // 2)
        strip = slice(at * width, (at + 1) * width)
        grad = dot_nn(picked[:, :rows], g_m[:, strip]) + dot_nn(picked[:, rows:], g_o[:, strip])
        for at in range(2):
            place = slice(n * share, (n + 1) * share)
            keep[at, place, :] = grad[at * share : (at + 1) * share].astype(BF)
            send[at, place, :] = grad[(2 + at) * share : (3 + at) * share].astype(BF)


def up_grad_call(scal, *args, after=()):
    rows, width = args[0].shape
    out = sds((2, args[2].shape[1] // 4, width))
    return call(
        up_grad_kernel,
        "up_grad",
        (out, out),
        [whole(a.shape) for a in args],
        (whole(out.shape),) * 2,
        (1,),
        [pltpu.VMEM((width, 2 * rows), BF), pltpu.VMEM((width // 2, 2 * rows), BF)],
        1,
        args,
        scal,
        after,
    )


def down_grad_kernel(s, a_m, a_o, g_m, g_o, keep, send):
    n = pl.program_id(0)
    grad = dot_nn(a_m[...].T, g_m[...]) + dot_nn(a_o[...].T, g_o[...])
    grad = grad.astype(BF)

    @pl.when(n < 2)
    def _():
        keep[...] = grad

    @pl.when(n >= 2)
    def _():
        send[...] = grad


def down_grad_call(scal, a_m, a_o, g_m, g_o, after=()):
    rows, wide = a_m.shape
    width = g_m.shape[1]
    share = wide // 8
    strip = whole((rows, width))
    out = sds((2, share, width))
    picked = pl.BlockSpec((rows, share), lambda n, s: (0, 2 * ((s[0] // 2) ^ n) + s[0] % 2))
    return call(
        down_grad_kernel,
        "down_grad",
        (out, out),
        [picked, picked, strip, strip],
        (
            pl.BlockSpec((None, share, width), lambda n, s: (jnp.minimum(n, 1), 0, 0)),
            pl.BlockSpec((None, share, width), lambda n, s: (jnp.maximum(n - 2, 0), 0, 0)),
        ),
        (4,),
        [],
        1,
        (a_m, a_o, g_m, g_o),
        scal,
        after,
    )


def out_grad_kernel(joined, s, x_m, x_o, dq, dkv_m, dkv_r, odq, odkv_m, odkv_r, att, oatt, b_m, b_o,
    sums_m, sums_o, *refs,
):
    turned, picked = refs[-2:]
    keep_a, send_a, keep_b, send_b = refs[-6:-2]
    if joined:
        first_a, second_a, first_b, second_b = refs[:4]
        rows_in = first_a.shape[1]
        rows_out = keep_a.shape[1]
        send_b[:rows_in, :] = (first_a[1].astype(F32) + second_a[1].astype(F32)).astype(BF)
        send_a[:rows_in, :] = (first_b[1].astype(F32) + second_b[1].astype(F32)).astype(BF)
        sent_a, sent_b = (
            [ref.at[pl.ds(rows_in + at * rows_out, rows_out)] for at in range(2)]
            for ref in (send_a, send_b)
        )
    else:
        sent_a, sent_b = ([ref.at[at] for at in range(2)] for ref in (send_a, send_b))
    places_a = [keep_a.at[0], keep_a.at[1], sent_a[0], sent_a[1]]
    places_b = [keep_b.at[0], sent_b[0], keep_b.at[1], sent_b[1]]
    skip = 0
    rows, width = x_m.shape
    half = width // 2
    core = s[0] % 2
    share = width // 8
    mine = pl.ds(pl.multiple_of(core * half, 128), half)
    other = pl.ds(pl.multiple_of((1 - core) * half, 128), half)
    turned[:, :rows] = x_m[...].T
    turned[:, rows:] = x_o[...].T
    order = (0, 2, 1, 3)
    gather_rows(s, turned, picked, order)
    left_m, left_o = picked[:, :rows], picked[:, rows:]

    def put(places, begin, grad, columns):
        for at in range(4):
            part = grad[at * share : (at + 1) * share].astype(BF)
            places[at][begin : begin + share, columns] = part

    for at, places, begin in ((0, places_a, 0), (1, places_a, share), (2, places_b, skip)):
        if at == 0:
            pairs = ((dq[:rows], dq[rows:]), (odq[rows:], odq[:rows]))
        else:
            cut = slice((at - 1) * half, at * half)
            pairs = ((dkv_m[:, cut], dkv_r[:, cut]), (odkv_r[:, cut], odkv_m[:, cut]))
        for columns, (mine_rows, other_rows) in zip((mine, other), pairs):
            grad = dot_nn(left_m, mine_rows) + dot_nn(left_o, other_rows)
            put(places, begin, grad, columns)
    turned[mine, :] = att[:, :half].T
    turned[other, :rows] = oatt[rows:, :half].T
    turned[other, rows:] = oatt[:rows, :half].T
    gather_rows(s, turned, picked, order)
    grad = dot_nn(picked[:, :rows], b_m[:, :width])
    grad = grad + dot_nn(picked[:, rows:], b_o[:, :width])
    put(places_b, skip + share, grad, slice(0, width))
    small = (sums_m[...] + sums_o[...]).astype(BF)
    begin = skip + 2 * share
    ends = places_a + places_b
    for ref in ends:
        ref[begin:, :] = small
    value = [ref[:, half:] for ref in (dkv_m, dkv_r, odkv_m, odkv_r)]
    for row, parts in ((10, (dq[...], odq[...])), (11, value)):
        count = len(parts) // 2
        for columns, group in ((mine, parts[:count]), (other, parts[count:])):
            line = sum(jnp.sum(p.astype(F32), axis=0, keepdims=True) for p in group).astype(BF)
            for ref in ends:
                ref[begin + row : begin + row + 1, columns] = line


def out_grad_call(scal, *args, joined=(), after=()):
    rows, width = args[0].shape
    share = 2 * (width // 8) + 16
    keep = sds((2, share, width))
    send = sds((joined[0].shape[1] + 2 * share, width)) if joined else keep
    args += tuple(joined)
    return call(
        functools.partial(out_grad_kernel, bool(joined)),
        "out_grad",
        (keep, send, keep, send),
        [whole(a.shape) for a in args],
        (whole(keep.shape), whole(send.shape)) * 2,
        (1,),
        [pltpu.VMEM((width, 2 * rows), BF), pltpu.VMEM((width // 2, 2 * rows), BF)],
        1,
        args,
        scal,
        after,
    )


def over_core(array):
    return lax.ppermute(array, "seq", [(i, i ^ 1) for i in range(8)])


def over_x(array):
    return lax.ppermute(array, "seq", [(i, i ^ 2) for i in range(8)])


def over_y(array):
    return lax.ppermute(array, "seq", [(i, i ^ 4) for i in range(8)])


def over_bucket(array, pairs):
    return lax.ppermute(array, "bucket", pairs)


def view(ref, cut):
    if cut is None:
        return ref[...]
    return ref[cut] if isinstance(cut, int) else ref[cut[0] : cut[0] + cut[1], :]


def parted(parts):
    arrays = tuple(p[0] if isinstance(p, tuple) else p for p in parts)
    cuts = tuple(p[1] if isinstance(p, tuple) else None for p in parts)
    return arrays, cuts


def sum_kernel(cuts, s, *refs):
    total = sum(view(ref, cut).astype(F32) for ref, cut in zip(refs, cuts))
    refs[-1][...] = total.astype(BF)


def sum_call(scal, parts, shape, after=()):
    arrays, cuts = parted(parts)
    return call(
        functools.partial(sum_kernel, cuts), "sum", sds(shape), [whole(a.shape) for a in arrays],
        whole(shape), (1,), [], 1, arrays, scal, after,
    )


def sort_kernel(cuts, s, *refs):
    mine, other = refs[-2:]
    halves = [list(zip(refs[at : at + 3], cuts[at : at + 3])) for at in (0, 3)]
    outer = (s[0] == 0) | (s[0] == 3)

    def write(first, second):
        for out, half in ((mine, halves[first]), (other, halves[second])):
            out[...] = sum(view(ref, cut).astype(F32) for ref, cut in half).astype(BF)

    @pl.when(outer)
    def _():
        write(0, 1)

    @pl.when(jnp.logical_not(outer))
    def _():
        write(1, 0)


def bucket_start(zscal, keep_a, keep_b, got_a, got_b, pass_a, pass_b, after):
    parts = [first_of(keep_a), first_of(got_a), pass_a, first_of(keep_b), first_of(got_b), pass_b]
    arrays, cuts = parted(parts)
    shape = keep_a.shape[1:]
    mine, other = call(
        functools.partial(sort_kernel, cuts), "sort", (sds(shape),) * 2,
        [whole(a.shape) for a in arrays], (whole(shape),) * 2, (1,), [], 1, arrays, zscal, after,
    )
    return mine, over_bucket(other, NEAR)


def first_of(stack):
    return stack[0] if isinstance(stack, tuple) else (stack, 0)


def second_of(stack):
    return stack[1] if isinstance(stack, tuple) else (stack, 1)


def bucket_middle(scal, mine, got, after):
    mine = sum_call(scal, (mine, got), mine.shape, after)
    return mine, over_bucket(mine, FAR)


def bucket_last(scal, mine, got, after):
    mine = sum_call(scal, (mine, got), mine.shape, after)
    return mine, over_bucket(mine, NEAR)


def bucket_end(mine, other):
    place = lax.axis_index("bucket")
    outer = (place == 0) | (place == 3)
    return jnp.where(outer, mine, other), jnp.where(outer, other, mine)


def phase_one(keep_a, send_a, keep_b, send_b):
    return keep_a, keep_b, over_x(send_a), over_y(send_b)


def phase_two(scal, keep_a, keep_b, got_a, got_b, after):
    shape = keep_a.shape[1:]
    pass_a = sum_call(scal, (second_of(keep_a), second_of(got_a)), shape, after)
    pass_b = sum_call(scal, (second_of(keep_b), second_of(got_b)), shape, (pass_a,))
    return keep_a, keep_b, got_a, got_b, over_y(pass_a), over_x(pass_b), (pass_b,)


def fast_local(
    frames, w_qkv, b_qv, w_out, b_out, ln_gain, ln_shift, w_up, b_up, w_down, b_down,
    cotangent, clip_lengths, valid_lengths,
):
    rows, width = frames.shape[1:]
    place = lax.axis_index("seq")
    scal = place.astype(jnp.int32)[None]
    zscal = lax.axis_index("bucket").astype(jnp.int32)[None]
    blocks = place ^ jnp.arange(8, dtype=jnp.int32)
    position = (blocks[:, None] * rows + jnp.arange(rows, dtype=jnp.int32)[None]).reshape(-1)
    ends = jnp.cumsum(clip_lengths[0])
    starts = ends - clip_lengths[0]
    inside = (position[:, None] >= starts) & (position[:, None] < ends)
    segment = jnp.sum(jnp.where(inside, jnp.arange(ends.shape[0], dtype=jnp.int32), 0), axis=1)
    live = jnp.any(inside & (position[:, None] < starts + valid_lengths[0]), axis=1)
    tags = jnp.where(live, segment, -1).reshape(8, rows, 1)
    tags = jnp.broadcast_to(tags, (8, rows, 128))
    seg_rows = segment[None]
    seg_row = seg_rows[:, : 2 * rows]

    x = frames[0]
    saved = []
    before = ()
    for layer in range(LAYERS):
        attend = functools.partial(attend_call, layer, scal)
        x_r, x_x, x_y = over_core(x), over_x(x), over_y(x)
        kv, q, qt, w_all, acc, top = attend((), seg_row, w_qkv, b_qv, (x, x_r), tags, (0, 1))
        x_x, x_y = gate((x_x, x_y), (top,))
        x_d = over_y(x_x)
        x_xr, x_yr = over_core(x_x), over_core(x_y)
        kv_x, kv_y, q_x, q_y, acc, top = attend(
            (qt, w_all, acc, top), seg_row, w_qkv, b_qv, (x_x, x_xr, x_y, x_yr), tags,
            (2, 3, 4, 5), after=before,
        )
        (x_d,) = gate((x_d,), (top,))
        x_dr = over_core(x_d)
        kv_d, q_d, att = attend(
            (qt, w_all, acc, top), seg_row, w_qkv, b_qv, (x_d, x_dr), tags, (6, 7), last=True
        )
        oatt = over_core(att)
        unit1, rs1, normed, act, slope, unit2, rs2, y = ffn_call(
            layer, scal, x, att, oatt, w_out, b_out, ln_gain, ln_shift, w_up, b_up, w_down, b_down
        )
        before = (over_core(normed), over_core(act))
        saved.append(
            (x, x_r, q, q_x, q_y, q_d, kv, kv_x, kv_y, kv_d, att, oatt)
            + (unit1, rs1, normed, act, slope, unit2, rs2) + before
        )
        x = y
    activations = x[None]

    grad = cotangent[0]
    done = ()
    for layer in reversed(range(LAYERS)):
        top_layer = layer == LAYERS - 1
        x, x_r, q, q_x, q_y, q_d, kv, kv_x, kv_y, kv_d, att, oatt = saved[layer][:12]
        unit1, rs1, normed, act, slope, unit2, rs2, o_normed, o_act = saved[layer][12:]
        normed, act, o_normed, o_act = (stored(a) for a in (normed, act, o_normed, o_act))
        slope, unit1, unit2 = (stored(a) for a in (slope, unit1, unit2))
        d_down, d_up, d_up_more, ext, d_first, sums = ffn_back_call(
            layer, scal, grad, unit2, rs2, slope, unit1, rs1, ln_gain, att, oatt, w_up, w_down,
            w_out, done
        )
        ext_r, ext_x, ext_y = over_core(ext), over_x(ext), over_y(ext)
        o_up, o_more, o_down = over_core(d_up), over_core(d_up_more), over_core(d_down)
        done = before if top_layer else ()
        if not top_layer:
            done = ()
        w_mine, qt, dot, stats, dq, dkv, kv_near, tag_near = back_own_call(
            layer, scal, ext, ext_r, q, seg_rows, kv, tags, w_out, after=done
        )
        done = (dkv,)
        if not top_layer:
            early = bucket_start(zscal, *late[:-1], (dkv,))
            middle = phase_two(scal, *middle, early[:1])
            done = middle[-1]
        dq = back_dq_call(
            scal, qt, dot, stats, dq, seg_rows, (kv_x,), tags, (2, 3), False, after=done
        )
        ext_x, ext_y = gate((ext_x, ext_y), (dq,))
        ext_d = over_y(ext_x)
        ext_xr, ext_yr = over_core(ext_x), over_core(ext_y)
        keep_a, send_a = up_grad_call(
            scal, normed, o_normed, d_up, o_up, d_up_more, o_more, after=(ext_xr, ext_yr)
        )
        done = (keep_a,)
        if not top_layer:
            middle = bucket_start(zscal, *middle[:-1], done)
            done = middle[:1]
        keep_b, send_b = down_grad_call(scal, act, o_act, d_down, o_down, after=done)
        done = (keep_b,)
        if not top_layer:
            early = bucket_middle(scal, *early, done)
            done = early[:1]
        late = phase_one(keep_a, send_a, keep_b, send_b)
        dq = back_dq_call(
            scal, qt, dot, stats, dq, seg_rows, (kv_y, kv_d), tags, (4, 5, 6, 7), True, after=done
        )
        done = (dq,)
        odq = over_core(dq)
        (dkv,) = back_dkv_call(
            scal, w_mine, kv_near, tag_near, dkv, (ext_x, ext_xr, ext_y, ext_yr), (q_x, q_y),
            seg_rows, (1, 2), False, after=done
        )
        (ext_d,) = gate((ext_d,), (dkv,))
        ext_dr = over_core(ext_d)
        done = (odq,)
        if not top_layer:
            middle = bucket_middle(scal, *middle, (dkv,))
            done = (odq, middle[0])
        (sums,) = gate((sums,), (dkv,))
        o_sums = over_core(sums)
        g_m, g_r = back_dkv_call(
            scal, w_mine, kv_near, tag_near, dkv, (ext_d, ext_dr), (q_d,), seg_rows, (3,), True,
            after=done,
        )
        o_m, o_r = over_core(g_m), over_core(g_r)
        done = (g_m,)
        if not top_layer:
            early = bucket_last(scal, *early, done)
            late = phase_two(scal, *late, early[:1])
            done = late[-1]
        out_args = (
            stored(x), stored(x_r), dq, g_m, g_r, odq, o_m, o_r, stored(att), stored(oatt),
            stored(ext), stored(ext_r), sums, o_sums,
        )
        if top_layer:
            keep_a, keep_b, got_a, got_b = late
            middle_a, sent_x, middle_b, sent_y = out_grad_call(
                scal, *out_args, joined=(keep_a, got_a, keep_b, got_b), after=(o_m,)
            )
            got_x, got_y = over_x(sent_x), over_y(sent_y)
            first, more = keep_a.shape[1], middle_a.shape[1]
            late += ((got_y, (0, first)), (got_x, (0, first)), ())
            middle = (middle_a, middle_b) + tuple(
                ((got, (first, more)), (got, (first + more, more))) for got in (got_x, got_y)
            )
            done = (middle_a,)
        grad = input_back_call(layer, scal, d_first, dq, g_m, odq, o_r, w_qkv, after=(o_m,) + done)
        done = (grad,)
    middle = bucket_last(scal, *middle, done)
    parts = out_grad_call(scal, *out_args, after=middle[:1])
    last = phase_one(*parts)
    late = bucket_start(zscal, *late[:-1], parts[:1])
    last = phase_two(scal, *last, late[:1])
    late = bucket_middle(scal, *late, last[-1])
    last = bucket_start(zscal, *last[:-1], late[:1])
    last = bucket_middle(scal, *last, last[:1])
    late = bucket_last(scal, *late, last[:1])
    last = bucket_last(scal, *last, late[:1])
    ffn_1, att_1, ffn_0, att_0 = (bucket_end(*pair) for pair in (early, middle, late, last))
    ffn_parts = (ffn_0, ffn_1)
    att_parts = (att_0, att_1)

    share = width // 8

    def both(make):
        return jnp.stack([make(layer).astype(F32) for layer in range(LAYERS)])

    small = both(lambda l: att_parts[l][0][2 * share :])

    def own(array, axis):
        size = array.shape[axis] // 8
        return lax.dynamic_slice_in_dim(array, place * size, size, axis)

    def beside(array):
        parts = array.shape[0] // share
        return array.reshape(parts, share, width).transpose(1, 0, 2).reshape(share, -1)

    return (
        activations,
        grad[None],
        both(
            lambda l: jnp.concatenate(
                [beside(att_parts[l][0][: 2 * share]), att_parts[l][1][:share]], axis=1
            )
        ),
        own(small[:, 10:12].reshape(LAYERS, -1), 1),
        both(lambda l: att_parts[l][1][share : 2 * share]),
        own(small[:, 4], 1),
        own(small[:, 0:2], 2),
        own(small[:, 2:4], 2),
        both(lambda l: beside(ffn_parts[l][0])),
        own(small[:, 6:10].reshape(LAYERS, -1), 1),
        both(lambda l: ffn_parts[l][1]),
        own(small[:, 5], 1),
    )


def clip_tags(lengths, valid, begin, count):
    position = begin + jnp.arange(count, dtype=jnp.int32)
    ends = jnp.cumsum(lengths)
    starts = ends - lengths
    inside = (position[:, None] >= starts[None, :]) & (position[:, None] < ends[None, :])
    labels = jnp.arange(lengths.shape[0], dtype=jnp.int32)
    segment = jnp.sum(jnp.where(inside, labels[None, :], 0), axis=1)
    live = jnp.any(inside & (position[:, None] < (starts + valid)[None, :]), axis=1)
    return (segment, jnp.where(live, segment, -1))


def layer_norm(hidden, gain, shift):
    center = hidden - jnp.mean(hidden, axis=-1, keepdims=True)
    spread = jnp.mean(center * center, axis=-1, keepdims=True)
    return center * lax.rsqrt(spread + 1e-05) * gain + shift


def exact_gelu(hidden):
    return jax.nn.gelu(hidden, approximate=False)


def split_heads(matrix):
    return matrix.reshape(matrix.shape[0], HEADS, -1)


def pair_terms(
    query_heads,
    grad_heads,
    log_total,
    correction,
    query_seg,
    key_heads,
    value_heads,
    key_tag,
    scale,
):
    scores = (
        jnp.einsum("qhd,khd->hqk", query_heads, key_heads, preferred_element_type=jnp.float32)
        * scale
    )
    allowed = (query_seg[:, None] == key_tag[None, :])[None]
    scores = jnp.where(allowed, scores, -1e30)
    probs = jnp.where(allowed, jnp.exp(scores - log_total[..., None]), 0.0)
    grad_probs = jnp.einsum(
        "qhd,khd->hqk", grad_heads, value_heads, preferred_element_type=jnp.float32
    )
    grad_scores = (probs * (grad_probs - correction[..., None])).astype(jnp.bfloat16)
    return (probs.astype(jnp.bfloat16), grad_scores)


def forward_layer(hidden, weights, query_seg, lengths, valid):
    w_qkv, b_qv, w_out, b_out, gain, shift, w_up, b_up, w_down, b_down = weights
    rows, width = hidden.shape
    scale = (width // HEADS) ** (-0.5)
    inputs = hidden.astype(jnp.bfloat16)
    projected = jnp.dot(inputs, w_qkv, preferred_element_type=jnp.float32)
    queries = (projected[:, :width] + b_qv[:width]).astype(jnp.bfloat16)
    keys = projected[:, width : 2 * width].astype(jnp.bfloat16)
    values = (projected[:, 2 * width :] + b_qv[width:]).astype(jnp.bfloat16)
    query_heads = split_heads(queries)
    initial = (
        jnp.full((HEADS, rows), -1e30, jnp.float32),
        jnp.zeros((HEADS, rows), jnp.float32),
        jnp.zeros((HEADS, rows, width // HEADS), jnp.float32),
    )
    key_piece = lax.all_gather(keys, "seq", axis=0, tiled=True)
    value_piece = lax.all_gather(values, "seq", axis=0, tiled=True)
    count = key_piece.shape[0] // rows
    key_blocks = key_piece.reshape(count, rows, HEADS, -1)
    value_blocks = value_piece.reshape(count, rows, HEADS, -1)

    def fold_inner(state, item):
        key_heads, value_heads, block_at = item
        _, block_tag = clip_tags(lengths, valid, block_at * rows, rows)
        running, denominator, weighted = state
        scores = (
            jnp.einsum("qhd,khd->hqk", query_heads, key_heads, preferred_element_type=jnp.float32)
            * scale
        )
        allowed = (query_seg[:, None] == block_tag[None, :])[None]
        scores = jnp.where(allowed, scores, -1e30)
        raised = jnp.maximum(running, jnp.max(scores, axis=-1))
        block_probs = jnp.where(allowed, jnp.exp(scores - raised[..., None]), 0.0)
        factor = jnp.exp(running - raised)
        denominator = denominator * factor + jnp.sum(block_probs, axis=-1)
        weighted = weighted * factor[..., None] + jnp.einsum(
            "hqk,khd->hqd",
            block_probs.astype(jnp.bfloat16),
            value_heads,
            preferred_element_type=jnp.float32,
        )
        return ((raised, denominator, weighted), None)

    state, _ = lax.scan(
        fold_inner, initial, (key_blocks, value_blocks, jnp.arange(count, dtype=jnp.int32))
    )
    running, denominator, weighted = state
    attended = (weighted / denominator[..., None]).transpose(1, 0, 2).reshape(rows, width)
    log_total = running + jnp.log(denominator)
    attended_low = attended.astype(jnp.bfloat16)
    branch = jnp.dot(attended_low, w_out, preferred_element_type=jnp.float32) + b_out
    first_sum = inputs.astype(jnp.float32) + branch
    normed = layer_norm(first_sum, gain[0], shift[0]).astype(jnp.bfloat16)
    up_pre = jnp.dot(normed, w_up, preferred_element_type=jnp.float32) + b_up
    activated = exact_gelu(up_pre).astype(jnp.bfloat16)
    second_sum = (
        normed.astype(jnp.float32)
        + jnp.dot(activated, w_down, preferred_element_type=jnp.float32)
        + b_down
    )
    output = layer_norm(second_sum, gain[1], shift[1])
    kept = (
        inputs,
        queries,
        keys,
        values,
        attended,
        attended_low,
        log_total,
        None,
        first_sum,
        normed,
        up_pre,
        activated,
        second_sum,
    )
    return (output, kept)


def attention_grads(kept, grad_att, query_seg, lengths, valid):
    (
        inputs,
        queries,
        keys,
        values,
        attended,
        attended_low,
        log_total,
        gathered,
        first_sum,
        normed,
        up_pre,
        activated,
        second_sum,
    ) = kept
    rows, width = queries.shape
    scale = (width // HEADS) ** (-0.5)
    query_heads = split_heads(queries)
    grad_heads = split_heads(grad_att)
    correction = jnp.sum(grad_heads.astype(jnp.float32) * split_heads(attended), axis=-1).T
    key_all, value_all = (
        lax.all_gather(keys, "seq", axis=0, tiled=True),
        lax.all_gather(values, "seq", axis=0, tiled=True),
    )
    count = key_all.shape[0] // rows
    key_blocks = key_all.reshape(count, rows, HEADS, -1)
    value_blocks = value_all.reshape(count, rows, HEADS, -1)
    block_ids = jnp.arange(count, dtype=jnp.int32)
    zero_heads = jnp.zeros((rows, HEADS, width // HEADS), jnp.float32)

    def attention_inner(acc, item):
        key_heads, value_heads, block_at = item
        _, block_tag = clip_tags(lengths, valid, block_at * rows, rows)
        probs, grad_scores = pair_terms(
            query_heads,
            grad_heads,
            log_total,
            correction,
            query_seg,
            key_heads,
            value_heads,
            block_tag,
            scale,
        )
        acc = (
            acc
            + jnp.einsum("hqk,khd->qhd", grad_scores, key_heads, preferred_element_type=jnp.float32)
            * scale
        )
        key_term = (
            jnp.einsum("hqk,qhd->khd", grad_scores, query_heads, preferred_element_type=jnp.float32)
            * scale
        )
        value_term = jnp.einsum(
            "hqk,qhd->khd", probs, grad_heads, preferred_element_type=jnp.float32
        )
        return (
            acc,
            jnp.concatenate(
                [key_term.reshape(rows, width), value_term.reshape(rows, width)], axis=1
            ),
        )

    grad_query, terms = lax.scan(attention_inner, zero_heads, (key_blocks, value_blocks, block_ids))
    summed = lax.psum_scatter(
        terms.reshape(count * rows, 2 * width).astype(jnp.bfloat16),
        "seq",
        scatter_dimension=0,
        tiled=True,
    ).astype(jnp.float32)
    grad_key = summed[:, :width]
    grad_value = summed[:, width:]
    return (grad_query.reshape(rows, width), grad_key, grad_value)


def backward_layer(grad_out, kept, weights, query_seg, lengths, valid):
    w_qkv, b_qv, w_out, b_out, gain, shift, w_up, b_up, w_down, b_down = weights
    (
        inputs,
        queries,
        keys,
        values,
        attended,
        attended_low,
        log_total,
        gathered,
        first_sum,
        normed,
        up_pre,
        activated,
        second_sum,
    ) = kept
    _, pull_second = jax.vjp(layer_norm, second_sum, gain[1], shift[1])
    grad_second, gain_second, shift_second = pull_second(grad_out)
    grad_down = grad_second.astype(jnp.bfloat16)
    sum_down = jnp.sum(grad_down, axis=0, dtype=jnp.float32)
    weight_down = jnp.einsum("rf,rd->fd", activated, grad_down, preferred_element_type=jnp.float32)
    grad_activated = jnp.einsum("rd,fd->rf", grad_down, w_down, preferred_element_type=jnp.float32)
    _, pull_gelu = jax.vjp(exact_gelu, up_pre)
    grad_up = pull_gelu(grad_activated)[0].astype(jnp.bfloat16)
    sum_up = jnp.sum(grad_up, axis=0, dtype=jnp.float32)
    weight_up = jnp.einsum("rd,rf->df", normed, grad_up, preferred_element_type=jnp.float32)
    grad_normed = grad_second + jnp.einsum(
        "rf,df->rd", grad_up, w_up, preferred_element_type=jnp.float32
    )
    _, pull_first = jax.vjp(layer_norm, first_sum, gain[0], shift[0])
    grad_first, gain_first, shift_first = pull_first(grad_normed)
    grad_branch = grad_first.astype(jnp.bfloat16)
    sum_out = jnp.sum(grad_branch, axis=0, dtype=jnp.float32)
    weight_out = jnp.einsum(
        "re,rd->ed", attended_low, grad_branch, preferred_element_type=jnp.float32
    )
    grad_att = jnp.einsum(
        "rd,ed->re", grad_branch, w_out, preferred_element_type=jnp.float32
    ).astype(jnp.bfloat16)
    grad_query, grad_key, grad_value = attention_grads(kept, grad_att, query_seg, lengths, valid)
    grad_proj = jnp.concatenate(
        [
            grad_query.astype(jnp.bfloat16),
            grad_key.astype(jnp.bfloat16),
            grad_value.astype(jnp.bfloat16),
        ],
        axis=1,
    )
    width = inputs.shape[1]
    sum_qv = jnp.concatenate(
        [
            jnp.sum(grad_proj[:, :width], axis=0, dtype=jnp.float32),
            jnp.sum(grad_proj[:, 2 * width :], axis=0, dtype=jnp.float32),
        ]
    )
    weight_qkv = jnp.einsum("rd,re->de", inputs, grad_proj, preferred_element_type=jnp.float32)
    grad_input = grad_first + jnp.einsum(
        "re,de->rd", grad_proj, w_qkv, preferred_element_type=jnp.float32
    )
    gains = jnp.stack([gain_first, gain_second])
    shifts = jnp.stack([shift_first, shift_second])
    return (
        grad_input,
        (
            weight_qkv,
            sum_qv,
            weight_out,
            sum_out,
            gains,
            shifts,
            weight_up,
            sum_up,
            weight_down,
            sum_down,
        ),
    )


def local(
    frames,
    w_qkv,
    b_qv,
    w_out,
    b_out,
    ln_gain,
    ln_shift,
    w_up,
    b_up,
    w_down,
    b_down,
    cotangent,
    clip_lengths,
    valid_lengths,
):
    rows = frames.shape[1]
    lengths = clip_lengths[0]
    valid = valid_lengths[0]
    offset = lax.axis_index("seq") * rows
    query_seg, key_tag = clip_tags(lengths, valid, offset, rows)
    layer_weights = [
        tuple(
            (
                array[layer_at]
                for array in (
                    w_qkv,
                    b_qv,
                    w_out,
                    b_out,
                    ln_gain,
                    ln_shift,
                    w_up,
                    b_up,
                    w_down,
                    b_down,
                )
            )
        )
        for layer_at in range(LAYERS)
    ]
    hidden = frames[0].astype(jnp.float32)
    saved = []
    for layer_at in range(LAYERS):
        hidden, kept = forward_layer(hidden, layer_weights[layer_at], query_seg, lengths, valid)
        saved.append(kept)
    activations = hidden.astype(jnp.bfloat16)[None]
    grad_hidden = cotangent[0].astype(jnp.float32)
    per_layer = [None] * LAYERS
    for layer_at in reversed(range(LAYERS)):
        grad_hidden, per_layer[layer_at] = backward_layer(
            grad_hidden, saved[layer_at], layer_weights[layer_at], query_seg, lengths, valid
        )
    stacked = [
        jnp.stack([per_layer[layer_at][member] for layer_at in range(LAYERS)])
        for member in range(10)
    ]
    g_wqkv, g_bqv, g_wout, g_bout, g_gain, g_shift, g_wup, g_bup, g_wdown, g_bdown = stacked
    shares = (
        lax.psum_scatter(
            g_wqkv.astype(jnp.bfloat16), "seq", scatter_dimension=1, tiled=True
        ).astype(jnp.float32),
        lax.psum_scatter(g_bqv.astype(jnp.bfloat16), "seq", scatter_dimension=1, tiled=True).astype(
            jnp.float32
        ),
        lax.psum_scatter(
            g_wout.astype(jnp.bfloat16), "seq", scatter_dimension=1, tiled=True
        ).astype(jnp.float32),
        lax.psum_scatter(
            g_bout.astype(jnp.bfloat16), "seq", scatter_dimension=1, tiled=True
        ).astype(jnp.float32),
        lax.psum_scatter(
            g_gain.astype(jnp.bfloat16), "seq", scatter_dimension=2, tiled=True
        ).astype(jnp.float32),
        lax.psum_scatter(
            g_shift.astype(jnp.bfloat16), "seq", scatter_dimension=2, tiled=True
        ).astype(jnp.float32),
        lax.psum_scatter(g_wup.astype(jnp.bfloat16), "seq", scatter_dimension=1, tiled=True).astype(
            jnp.float32
        ),
        lax.psum_scatter(g_bup.astype(jnp.bfloat16), "seq", scatter_dimension=1, tiled=True).astype(
            jnp.float32
        ),
        lax.psum_scatter(
            g_wdown.astype(jnp.bfloat16), "seq", scatter_dimension=1, tiled=True
        ).astype(jnp.float32),
        lax.psum_scatter(
            g_bdown.astype(jnp.bfloat16), "seq", scatter_dimension=1, tiled=True
        ).astype(jnp.float32),
    )
    s_wqkv, s_bqv, s_wout, s_bout, s_gain, s_shift, s_wup, s_bup, s_wdown, s_bdown = shares
    totals = (
        lax.psum(s_wqkv.astype(jnp.bfloat16), "bucket").astype(jnp.float32),
        lax.psum(s_bqv.astype(jnp.bfloat16), "bucket").astype(jnp.float32),
        lax.psum(s_wout.astype(jnp.bfloat16), "bucket").astype(jnp.float32),
        lax.psum(s_bout.astype(jnp.bfloat16), "bucket").astype(jnp.float32),
        lax.psum(s_gain.astype(jnp.bfloat16), "bucket").astype(jnp.float32),
        lax.psum(s_shift.astype(jnp.bfloat16), "bucket").astype(jnp.float32),
        lax.psum(s_wup.astype(jnp.bfloat16), "bucket").astype(jnp.float32),
        lax.psum(s_bup.astype(jnp.bfloat16), "bucket").astype(jnp.float32),
        lax.psum(s_wdown.astype(jnp.bfloat16), "bucket").astype(jnp.float32),
        lax.psum(s_bdown.astype(jnp.bfloat16), "bucket").astype(jnp.float32),
    )
    return (
        activations,
        grad_hidden[None],
        totals[0],
        totals[1],
        totals[2],
        totals[3],
        totals[4],
        totals[5],
        totals[6],
        totals[7],
        totals[8],
        totals[9],
    )


def solution(mesh):
    placed = (
        P("bucket", "seq", None),
        P(),
        P(),
        P(),
        P(),
        P(),
        P(),
        P(),
        P(),
        P(),
        P(),
        P("bucket", "seq", None),
        P("bucket", None),
        P("bucket", None),
    )
    chips_2x2 = mesh.shape["seq"] == 8 and mesh.shape["bucket"] == 4
    return jax.shard_map(
        fast_local if chips_2x2 else local,
        mesh=mesh,
        in_specs=placed,
        out_specs=(
            P("bucket", "seq", None),
            P("bucket", "seq", None),
            P(None, "seq", None),
            P(None, "seq"),
            P(None, "seq", None),
            P(None, "seq"),
            P(None, None, "seq"),
            P(None, None, "seq"),
            P(None, "seq", None),
            P(None, "seq"),
            P(None, "seq", None),
            P(None, "seq"),
        ),
        check_vma=False,
    )
```

```python
import functools
import math

import jax
import jax.numpy as jnp
from jax import lax
from jax.experimental import pallas as pl
from jax.experimental.pallas import tpu as pltpu
from jax.sharding import PartitionSpec as P

HEADS = 12
LAYERS = 2
NEAR = [(0, 1), (1, 0), (2, 3), (3, 2)]
FAR = [(0, 3), (3, 0), (1, 2), (2, 1)]
BF = jnp.bfloat16
F32 = jnp.float32
LOW = -1e30
SLACK = 6 * 1024 * 1024


def dot_nn(a, b):
    return lax.dot_general(a, b, (((1,), (0,)), ((), ())), preferred_element_type=F32)


def dot_nt(a, b):
    return lax.dot_general(a, b, (((1,), (1,)), ((), ())), preferred_element_type=F32)


def block_bytes(spec, array):
    if spec.block_shape is None:
        return 0
    lanes = [n for n in spec.block_shape if n is not None]
    lanes[-1] += -lanes[-1] % 128
    return math.prod(lanes) * array.dtype.itemsize


def call(body, name, out_shape, in_specs, out_specs, grid, scratch, flops, args, scalars, after=()):
    args = tuple(
        stored(a) if p.memory_space == pltpu.HBM else a for p, a in zip(in_specs, args)
    )
    count = len(args)

    def run(scal, *refs):
        body(scal, *refs[:count], *refs[count + len(after) :])

    need = sum(block_bytes(p, a) for p, a in zip(in_specs, args))
    need += sum(block_bytes(p, a) for p, a in zip(jax.tree.leaves(out_specs), jax.tree.leaves(out_shape)))
    need = need + sum(
        math.prod(m.shape) * jnp.dtype(m.dtype).itemsize for m in scratch if m.memory_space == pltpu.VMEM
    )
    return pl.pallas_call(
        run,
        name=name,
        out_shape=out_shape,
        grid_spec=pltpu.PrefetchScalarGridSpec(
            num_scalar_prefetch=1,
            grid=grid,
            in_specs=list(in_specs) + [pl.BlockSpec(memory_space=pl.ANY)] * len(after),
            out_specs=out_specs,
            scratch_shapes=scratch,
        ),
        compiler_params=pltpu.CompilerParams(vmem_limit_bytes=need + SLACK),
        cost_estimate=pl.CostEstimate(
            flops=int(flops), bytes_accessed=1 + int(flops / 400), transcendentals=0
        ),
    )(scalars, *args, *after)


def whole(shape):
    return pl.BlockSpec(shape, lambda i, s: (0,) * len(shape))


def kept(shape, dtype=BF):
    return pltpu.HBM(shape, dtype)


def near(shape, dtype=BF):
    return pltpu.VMEM(shape, dtype)


def held(array):
    return pltpu.with_memory_space_constraint(array, pltpu.VMEM)


def stored(array):
    return pltpu.with_memory_space_constraint(array, pltpu.HBM)


def gate(arrays, after, space=pltpu.VMEM):
    anywhere = pl.BlockSpec(memory_space=pl.ANY)
    count = len(arrays)

    def body(*refs):
        pass

    return pl.pallas_call(
        body,
        name="gate",
        out_shape=tuple(sds(a.shape, a.dtype) for a in arrays),
        in_specs=[anywhere] * (count + len(after)),
        out_specs=(anywhere,) * count,
        input_output_aliases={i: i for i in range(count)},
        compiler_params=pltpu.CompilerParams(vmem_limit_bytes=1024 * 1024),
        cost_estimate=pl.CostEstimate(flops=1, bytes_accessed=1, transcendentals=0),
    )(*(pltpu.with_memory_space_constraint(a, space) for a in arrays), *after)


def far():
    return pl.BlockSpec(memory_space=pltpu.HBM)


def fetch(pairs, sems):
    copies = [pltpu.make_async_copy(src, dst, sems.at[i]) for i, (src, dst) in enumerate(pairs)]
    for copy in copies:
        copy.start()
    return copies


def sds(shape, dtype=BF):
    return jax.ShapeDtypeStruct(shape, dtype)


def mask_of(tag, seg):
    ok = jnp.concatenate([tag] * (seg.shape[1] // 128), axis=1) == seg
    return jnp.where(ok, 0.0, LOW)


def attend_kernel(layer, chips, first, last, *refs):
    refs = list(refs)
    core = refs.pop(0)[0] % 2
    if not first:
        qt, w_all, acc_in, m_in = (refs.pop(0) for _ in range(4))
    seg_ref, bias_ref, bias_k, w_ref = (refs.pop(0) for _ in range(4))
    xs = [refs.pop(0) for _ in range(2 * chips)]
    tags = [refs.pop(0) for _ in range(2 * chips)]
    kv_outs = [refs.pop(0) for _ in range(chips)]
    q_outs = [refs.pop(0) for _ in range(chips)]
    if first:
        qt, w_all = (refs.pop(0) for _ in range(2))
    if last:
        att_ref = refs.pop(0)
    else:
        acc_out, m_out = refs.pop(0), refs.pop(0)
    s_scr, vt_scr, kvs, qs, out_sems = (refs.pop(0) for _ in range(5))
    rows, width = xs[0].shape
    half = width // 2
    heads = half // 64
    queries = seg_ref.shape[1]
    high = vt_scr.shape[1]
    pair = 2 * rows
    leaving = []

    def leave(src, dst):
        copy = pltpu.make_async_copy(src, dst, out_sems.at[len(leaving)])
        copy.start()
        leaving.append(copy)

    if first:
        sems = refs.pop(0)
        begin = [pl.multiple_of(width * i + core * half, 128) for i in range(3)]
        copies = fetch(
            [(w_ref.at[layer, :, pl.ds(begin[i], half)], w_all.at[i]) for i in range(3)], sems
        )
    bias_q = bias_ref[layer : layer + 1, :]
    bias_v = bias_k[layer : layer + 1, :]
    for c in range(chips):
        x = jnp.concatenate([xs[2 * c][...], xs[2 * c + 1][...]], axis=0)
        if first:
            copies.pop(0).wait()
        q = (dot_nn(x, w_all[0]) + bias_q).astype(BF) * BF(0.125)
        qs[c] = q
        leave(qs.at[c], q_outs[c])
        if first:
            qt[...] = q.T
            copies.pop(0).wait()
            copies.pop(0).wait()
        kvs[c, :, :half] = dot_nn(x, w_all[1]).astype(BF)
        values = (dot_nn(x, w_all[2]) + bias_v).astype(BF)
        kvs[c, :, half:] = values
        leave(kvs.at[c], kv_outs[c])
        turned = values.T
        for h in range(heads):
            vt_scr[h, :64, c * pair : (c + 1) * pair] = turned[h * 64 : (h + 1) * 64]
    vt_scr[:, 64:, :] = jnp.ones((heads, high - 64, chips * pair), BF)
    seg = seg_ref[...]
    outs, lses = [], []
    if not last:
        m_out[...] = jnp.zeros_like(m_out)
    for h in range(heads):
        qh = qt[h * 64 : (h + 1) * 64, :]
        m8 = None
        for b in range(2 * chips):
            key = slice((b % 2) * rows, (b % 2 + 1) * rows)
            scores = dot_nn(kvs[b // 2, key, h * 64 : (h + 1) * 64], qh)
            ok = jnp.concatenate([tags[b][...]] * (queries // 128), axis=1) == seg
            scores = jnp.where(ok, scores, LOW)
            s_scr[h % 2, b * rows : (b + 1) * rows, :] = scores
            top = jnp.max(scores.reshape(rows // 8, 8, queries), axis=0)
            m8 = top if m8 is None else jnp.maximum(m8, top)
        m = jnp.max(m8, axis=0, keepdims=True)
        if not first:
            m_old = m_in[h : h + 1, :]
            m = jnp.maximum(m, m_old)
        acc = jnp.zeros((high, queries), F32)
        for b in range(2 * chips):
            probs = jnp.exp(s_scr[h % 2, b * rows : (b + 1) * rows, :] - m).astype(BF)
            acc = acc + dot_nn(vt_scr[h, :, b * rows : (b + 1) * rows], probs)
        if not first:
            acc = acc + acc_in[h] * jnp.exp(m_old - m)
        if last:
            total = acc[64:65]
            outs.append((acc[:64] / total).astype(BF))
            lses.append(m + jnp.log(total))
        else:
            acc_out[h] = acc
            m_out[h : h + 1, :] = m
    if last:
        lse = jnp.concatenate(lses, axis=0)
        top = lse.astype(BF).astype(F32)
        rest = jnp.zeros((128 - 2 * heads, queries), F32)
        tail = jnp.concatenate([top, lse - top, rest], axis=0)
        att_ref[:, :half] = jnp.concatenate(outs, axis=0).T
        att_ref[:, half:] = tail.T.astype(BF)
    for copy in leaving:
        copy.wait()


def tag_specs(tag_ids, rows):
    return [pl.BlockSpec((None, rows, 128), lambda i, s, r=r: (r, 0, 0)) for r in tag_ids]


def attend_call(layer, scal, state, seg_row, w_qkv, b_qv, xs, tags, tag_ids, last=False, after=()):
    first = not state
    rows, width = xs[0].shape
    half = width // 2
    heads = half // 64
    queries = 2 * rows
    chips = len(xs) // 2
    high = 80
    out_shape = tuple(kept((2 * rows, width)) for _ in range(chips))
    out_shape += tuple(kept((2 * rows, half)) for _ in range(chips))
    if first:
        out_shape += (near((half, queries)), near((3, width, half)))
    if last:
        out_shape += (sds((queries, half + 128)),)
    else:
        out_shape += (near((heads, high, queries), F32), near((8, queries), F32))
    out_specs = [whole(o.shape) for o in out_shape]
    for i in range(2 * chips):
        out_specs[i] = far()

    def bias(part):
        return pl.BlockSpec((LAYERS, half), lambda i, s: (0, 2 * part + s[0] % 2))

    state = tuple(held(a) for a in state)
    specs = [whole(a.shape) for a in state]
    specs += [whole(seg_row.shape), bias(0), bias(1), far()]
    specs += [whole(x.shape) for x in xs] + tag_specs(tag_ids, rows)
    args = state + (seg_row, b_qv, b_qv, w_qkv) + tuple(xs) + (tags,) * len(xs)
    scratch = [
        pltpu.VMEM((2, chips * 2 * rows, queries), F32),
        pltpu.VMEM((heads, high, chips * 2 * rows), BF),
        pltpu.VMEM((chips, 2 * rows, width), BF),
        pltpu.VMEM((chips, 2 * rows, half), BF),
        pltpu.SemaphoreType.DMA((2 * chips,)),
    ]
    if first:
        scratch.append(pltpu.SemaphoreType.DMA((3,)))
    return call(
        functools.partial(attend_kernel, layer, chips, first, last),
        "attend",
        out_shape,
        specs,
        tuple(out_specs),
        (1,),
        scratch,
        chips * 12 * 4 * queries * half * rows,
        args,
        scal,
        after,
    )


def back_queries(core, ext_m, ext_r, w_out, turned_scr):
    rows, wide = ext_m.shape
    width = wide - 128
    ext = jnp.concatenate([ext_m[...], ext_r[...]], axis=0)
    grad = dot_nt(ext[:, :width], w_out).astype(BF)
    turned_scr[...] = ext[:, width:].T.astype(F32)
    part = turned_scr[pl.ds(pl.multiple_of(core * 64, 64), 64), :]
    heads = width // 128
    lse = part[:heads] + part[heads : 2 * heads]
    corr = part[2 * heads : 3 * heads] + part[3 * heads : 4 * heads]
    return grad, grad.T, lse, corr


def pair_terms_kernel(keys, values, qt, dot, lse, corr, mask):
    scores = dot_nn(keys, qt)
    grad = dot_nn(values, dot)
    probs = jnp.exp(scores - lse + mask)
    return probs.astype(BF), (probs * (grad - corr)).astype(BF)


def back_own_kernel(
    layer, s, ext_m, ext_r, q, seg_ref, kv, tag_m, tag_r, w_ref,
    w_out, qt, dot, stats, dq, dkv, kv_out, tag_out, turned_scr, sems,
):
    core = s[0] % 2
    rows = ext_m.shape[0]
    half = q.shape[1]
    heads = half // 64
    queries = 2 * rows
    (copy,) = fetch(
        [(w_ref.at[layer, pl.ds(pl.multiple_of(core * half, 128), half)], w_out)], sems
    )
    kv_out[...] = kv[...]
    tag_out[0] = tag_m[...]
    tag_out[1] = tag_r[...]
    qt[...] = q[...].T
    copy.wait()
    do, turned, lse, corr = back_queries(core, ext_m, ext_r, w_out[...], turned_scr)
    dot[...] = turned
    stats[...] = jnp.zeros_like(stats)
    stats[:heads, :] = lse
    stats[8 : 8 + heads, :] = corr
    seg = seg_ref[...]
    for b in range(2):
        key = slice(b * rows, (b + 1) * rows)
        kt = kv[key, :half].T
        ok = mask_of(tag_out[b], seg)
        for h in range(heads):
            sl = slice(h * 64, (h + 1) * 64)
            vl = slice(half + h * 64, half + (h + 1) * 64)
            probs, grad = pair_terms_kernel(
                kv[key, sl], kv[key, vl], qt[sl, :], dot[sl, :], lse[h : h + 1],
                corr[h : h + 1], ok,
            )
            term = dot_nn(kt[sl], grad)
            if b == 0:
                dq[sl, :] = term
            else:
                dq[sl, :] += term
            dkv[key, sl] = dot_nn(grad, q[:, sl])
            dkv[key, vl] = dot_nn(probs, do[:, sl])


def back_own_call(layer, scal, ext_m, ext_r, q, seg_rows, kv, tags, w_out, after=()):
    rows = ext_m.shape[0]
    queries, half = q.shape
    width = 2 * half
    out_shape = (
        near((half, width)), near((half, queries)), near((half, queries)),
        near((16, queries), F32), near((half, queries), F32), near((queries, width), F32),
        near((queries, width)), near((2, rows, 128), jnp.int32),
    )
    return call(
        functools.partial(back_own_kernel, layer),
        "back_own",
        out_shape,
        [whole(ext_m.shape), whole(ext_r.shape), whole(q.shape), seg_spec(queries, 0), whole(kv.shape)]
        + tag_specs((0, 1), rows) + [far()],
        tuple(whole(o.shape) for o in out_shape),
        (1,),
        [pltpu.VMEM((128, queries), F32), pltpu.SemaphoreType.DMA((1,))],
        1,
        (ext_m, ext_r, q, seg_rows, kv, tags, tags, w_out),
        scal,
        after,
    )


def seg_spec(queries, at):
    return pl.BlockSpec((1, queries), lambda i, s: (0, at))


def back_dq_kernel(chips, last, s, *refs):
    refs = list(refs)
    qt, dot, stats, dq_in, seg_ref = (refs.pop(0) for _ in range(5))
    kvs = [refs.pop(0) for _ in range(chips)]
    tags = [refs.pop(0) for _ in range(2 * chips)]
    dq_out, dq_scr, kv_scr, sems = refs
    copies = fetch([(kvs[c], kv_scr.at[c]) for c in range(chips)], sems)
    rows = tags[0].shape[0]
    half, queries = qt.shape
    heads = half // 64
    seg = seg_ref[...]
    dq_scr[...] = dq_in[...]
    for c in range(chips):
        copies[c].wait()
        for b in range(2):
            key = slice(b * rows, (b + 1) * rows)
            kt = kv_scr[c, key, :half].T
            ok = mask_of(tags[2 * c + b][...], seg)
            for h in range(heads):
                sl = slice(h * 64, (h + 1) * 64)
                vl = slice(half + h * 64, half + (h + 1) * 64)
                _, grad = pair_terms_kernel(
                    kv_scr[c, key, sl], kv_scr[c, key, vl], qt[sl, :], dot[sl, :],
                    stats[h : h + 1, :], stats[8 + h : 9 + h, :], ok,
                )
                dq_scr[sl, :] += dot_nn(kt[sl], grad)
    if last:
        dq_out[...] = (dq_scr[...] * 0.125).astype(BF).T
    else:
        dq_out[...] = dq_scr[...]


def back_dq_call(scal, qt, dot, stats, dq, seg_rows, kvs, tags, tag_ids, last, after=()):
    half, queries = qt.shape
    rows = queries // 2
    chips = len(kvs)
    state = tuple(held(a) for a in (qt, dot, stats, dq))
    out = sds((queries, half)) if last else near((half, queries), F32)
    return call(
        functools.partial(back_dq_kernel, chips, last),
        "back_dq",
        out,
        [whole(a.shape) for a in state] + [seg_spec(queries, 0)] + [far()] * chips
        + tag_specs(tag_ids, rows),
        whole(out.shape),
        (1,),
        [
            pltpu.VMEM((half, queries), F32),
            pltpu.VMEM((chips, queries, 2 * half), BF),
            pltpu.SemaphoreType.DMA((chips,)),
        ],
        1,
        state + (seg_rows,) + tuple(kvs) + (tags,) * (2 * chips),
        scal,
        after,
    )


def back_dkv_kernel(chips, last, s, *refs):
    refs = list(refs)
    w_out, kv, tag, dkv_in = (refs.pop(0) for _ in range(4))
    exts = [refs.pop(0) for _ in range(2 * chips)]
    qs = [refs.pop(0) for _ in range(chips)]
    segs = [refs.pop(0) for _ in range(chips)]
    if last:
        out_m, out_r = refs.pop(0), refs.pop(0)
    else:
        dkv_out = refs.pop(0)
    dkv, q_scr, turned_scr, sems = refs
    copies = fetch([(qs[c], q_scr.at[c]) for c in range(chips)], sems)
    core = s[0] % 2
    rows = exts[0].shape[0]
    half, width = w_out.shape
    heads = half // 64
    queries = 2 * rows
    dkv[...] = dkv_in[...]
    for c in range(chips):
        do, dot, lse, corr = back_queries(
            core, exts[2 * c], exts[2 * c + 1], w_out[...], turned_scr
        )
        copies[c].wait()
        q = q_scr[c]
        qt = q.T
        seg = segs[c][...]
        for b in range(2):
            key = slice(b * rows, (b + 1) * rows)
            ok = mask_of(tag[b], seg)
            for h in range(heads):
                sl = slice(h * 64, (h + 1) * 64)
                vl = slice(half + h * 64, half + (h + 1) * 64)
                probs, grad = pair_terms_kernel(
                    kv[key, sl], kv[key, vl], qt[sl], dot[sl], lse[h : h + 1], corr[h : h + 1], ok
                )
                dkv[key, sl] += dot_nn(grad, q[:, sl])
                dkv[key, vl] += dot_nn(probs, do[:, sl])
    if last:
        out_m[...] = dkv[:rows, :].astype(BF)
        out_r[...] = dkv[rows:, :].astype(BF)
    else:
        dkv_out[...] = dkv[...]


def back_dkv_call(scal, w_out, kv, tag, dkv, exts, qs, seg_rows, seg_ids, last, after=()):
    queries, width = kv.shape
    rows, half = queries // 2, width // 2
    chips = len(qs)
    state = tuple(held(a) for a in (w_out, kv, tag, dkv))
    flat = sds((rows, width))
    out_shape = (flat, flat) if last else (near((queries, width), F32),)
    return call(
        functools.partial(back_dkv_kernel, chips, last),
        "back_dkv",
        out_shape,
        [whole(a.shape) for a in state] + [whole(e.shape) for e in exts] + [far()] * chips
        + [seg_spec(queries, at) for at in seg_ids],
        tuple(whole(o.shape) for o in out_shape),
        (1,),
        [
            pltpu.VMEM((queries, width), F32),
            pltpu.VMEM((chips, queries, half), BF),
            pltpu.VMEM((128, queries), F32),
            pltpu.SemaphoreType.DMA((chips,)),
        ],
        1,
        state + tuple(exts) + tuple(qs) + (seg_rows,) * chips,
        scal,
        after,
    )


def normalize(hidden):
    center = hidden - jnp.mean(hidden, axis=-1, keepdims=True)
    spread = lax.rsqrt(jnp.mean(center * center, axis=-1, keepdims=True) + 1e-05)
    return center * spread, spread


def normalize_back(grad, unit, spread, gain):
    scaled = grad * gain
    mean = jnp.mean(scaled, axis=-1, keepdims=True)
    along = jnp.mean(scaled * unit, axis=-1, keepdims=True)
    return spread * (scaled - mean - unit * along)


def gauss(up):
    size = jnp.abs(up)
    bell = jnp.exp(-0.5 * up * up)
    t = 1.0 / (1.0 + 0.23164189 * size)
    poly = 0.5307027145 * t - 0.7265760135
    poly = poly * t + 0.7107068705
    poly = poly * t - 0.142248368
    poly = poly * t + 0.127414796
    tail = poly * t * bell
    return jnp.where(up < 0, tail, 1.0 - tail), bell


def ffn_kernel(
    layer, s, x, att, oatt, b_out, gain, shift, b_up, b_down, w_out, w_up, w_down,
    unit1, rs1, normed, act, slope, unit2, rs2, y, kept_scr, unit_scr, kept_sems, out_scr,
    up_scr, down_scr, sems,
):
    rows, width = x.shape
    half = width // 2
    core = s[0] % 2
    steps = up_scr.shape[0]
    pairs = [(w_out.at[layer], out_scr)]
    for n in range(steps):
        strip = pl.ds(n * width, width)
        pairs += [(w_up.at[layer, :, strip], up_scr.at[n]), (w_down.at[layer, strip], down_scr.at[n])]
    copies = fetch(pairs, sems)
    copies[0].wait()
    mine = pl.multiple_of(core * half, 128)
    other = pl.multiple_of((1 - core) * half, 128)
    branch = dot_nn(att[:rows, :half], out_scr[pl.ds(mine, half), :])
    branch = branch + dot_nn(oatt[rows:, :half], out_scr[pl.ds(other, half), :])
    first = x[...].astype(F32) + branch + b_out[layer : layer + 1, :]
    unit, spread = normalize(first)
    unit_scr[0] = unit
    leaving = [pltpu.make_async_copy(unit_scr.at[0], unit1, kept_sems.at[2 * steps])]
    leaving[0].start()
    rs1[...] = jnp.broadcast_to(spread, rs1.shape)
    low = (unit * gain[layer, 0:1, :] + shift[layer, 0:1, :]).astype(BF)
    normed[...] = low
    total = low.astype(F32) + b_down[layer : layer + 1, :]
    copies[1].wait()
    following = dot_nn(low, up_scr[0])
    for n in range(steps):
        strip = slice(n * width, (n + 1) * width)
        up = following + b_up[layer : layer + 1, strip]
        copies[2 + 2 * n].wait()
        if n + 1 < steps:
            copies[3 + 2 * n].wait()
            following = dot_nn(normed[...], up_scr[n + 1])
        phi, bell = gauss(up)
        low = (up * phi).astype(BF)
        kept_scr[0, :, strip] = low
        kept_scr[1, :, strip] = (phi + up * (0.3989422804014327 * bell)).astype(BF)
        for i, ref in enumerate((act, slope)):
            copy = pltpu.make_async_copy(
                kept_scr.at[i, :, strip], ref.at[:, strip], kept_sems.at[2 * n + i]
            )
            copy.start()
            leaving.append(copy)
        total = total + dot_nn(low, down_scr[n])
    unit, spread = normalize(total)
    unit_scr[1] = unit
    leaving.append(pltpu.make_async_copy(unit_scr.at[1], unit2, kept_sems.at[2 * steps + 1]))
    leaving[-1].start()
    rs2[...] = jnp.broadcast_to(spread, rs2.shape)
    y[...] = (unit * gain[layer, 1:2, :] + shift[layer, 1:2, :]).astype(BF)
    for copy in leaving:
        copy.wait()


def ffn_call(
    layer, scal, x, att, oatt, w_out, b_out, gain, shift, w_up, b_up, w_down, b_down, after=()
):
    rows, width = x.shape
    wide = w_up.shape[2]
    steps = wide // width
    vec = sds((rows, 128), F32)
    out_shape = (
        kept((rows, width), F32), vec, sds((rows, width)), kept((rows, wide)), kept((rows, wide)),
        kept((rows, width), F32), vec, sds((rows, width)),
    )
    out_specs = [whole(o.shape) for o in out_shape]
    for i in (0, 3, 4, 5):
        out_specs[i] = far()
    arrays = (x, att, oatt, b_out, gain, shift, b_up, b_down)
    return call(
        functools.partial(ffn_kernel, layer),
        "ffn",
        out_shape,
        [whole(a.shape) for a in arrays] + [far()] * 3,
        tuple(out_specs),
        (1,),
        [
            pltpu.VMEM((2, rows, wide), BF),
            pltpu.VMEM((2, rows, width), F32),
            pltpu.SemaphoreType.DMA((2 * steps + 2,)),
            pltpu.VMEM((width, width), BF),
            pltpu.VMEM((steps, width, width), BF),
            pltpu.VMEM((steps, width, width), BF),
            pltpu.SemaphoreType.DMA((1 + 2 * steps,)),
        ],
        4 * rows * width * wide + 2 * rows * width * width,
        arrays + (w_out, w_up, w_down),
        scal,
        after,
    )


def ffn_back_kernel(
    layer, s, gy, unit2, rs2, slope, unit1, rs1, gain, att, oatt, w_up, w_down, w_out,
    d_down, d_up, d_up_more, d_branch, d_first, sums, up_scr, down_scr, out_scr, sems,
):
    steps = up_scr.shape[0]
    rows, width = gy.shape
    half = width // 2
    core = s[0] % 2
    pairs = []
    for n in range(steps):
        strip = pl.ds(n * width, width)
        pairs += [(w_down.at[layer, strip], down_scr.at[n]), (w_up.at[layer, :, strip], up_scr.at[n])]
    pairs.append((w_out.at[layer], out_scr))
    copies = fetch(pairs, sems)
    grad = gy[...].astype(F32)
    unit = unit2[...]
    total = normalize_back(grad, unit, rs2[:, 0:1], gain[layer, 1:2, :])
    sums[...] = jnp.zeros_like(sums)
    sums[1:2, :] = jnp.sum(grad * unit, axis=0, keepdims=True)
    sums[3:4, :] = jnp.sum(grad, axis=0, keepdims=True)
    low = total.astype(BF)
    d_down[...] = low
    sums[5:6, :] = jnp.sum(low.astype(F32), axis=0, keepdims=True)
    copies[0].wait()
    following = dot_nt(low, down_scr[0])
    for n in range(steps):
        strip = slice(n * width, (n + 1) * width)
        low = (following * slope[:, strip].astype(F32)).astype(BF)
        copies[2 * n + 1].wait()
        if n + 1 < steps:
            copies[2 * n + 2].wait()
            following = dot_nt(d_down[...], down_scr[n + 1])
        ref, at = (d_up, n) if n < steps // 2 else (d_up_more, n - steps // 2)
        ref[:, at * width : (at + 1) * width] = low
        sums[6 + n : 7 + n, :] = jnp.sum(low.astype(F32), axis=0, keepdims=True)
        total = total + dot_nt(low, up_scr[n])
    unit = unit1[...]
    first = normalize_back(total, unit, rs1[:, 0:1], gain[layer, 0:1, :])
    sums[0:1, :] = jnp.sum(total * unit, axis=0, keepdims=True)
    sums[2:3, :] = jnp.sum(total, axis=0, keepdims=True)
    d_first[...] = first
    low = first.astype(BF)
    d_branch[:, :width] = low
    sums[4:5, :] = jnp.sum(low.astype(F32), axis=0, keepdims=True)
    copies[-1].wait()
    row = lax.broadcasted_iota(jnp.int32, (128, 128), 0)
    column = lax.broadcasted_iota(jnp.int32, (128, 128), 1)
    heads = half // 64
    stats = jnp.zeros((rows, 128), F32)
    tall = lax.broadcasted_iota(jnp.int32, (half, 128), 0)
    wide = lax.broadcasted_iota(jnp.int32, (half, 128), 1)
    for at, part in ((core, att[:rows]), (1 - core, oatt[rows:])):
        move = (row < 2 * heads) & (column == at * 64 + row)
        stats = stats + dot_nn(part[:, half:], jnp.where(move, 1.0, 0.0).astype(BF))
        grad = dot_nt(low, out_scr[pl.ds(pl.multiple_of(at * half, 128), half), :])
        product = grad.astype(BF).astype(F32) * part[:, :half].astype(F32)
        place = wide - at * 64 - 2 * heads
        pick = (place == tall // 64) | (place == tall // 64 + heads)
        stats = stats + lax.dot_general(
            product, jnp.where(pick, 1.0, 0.0), (((1,), (0,)), ((), ())),
            precision=lax.Precision.HIGHEST, preferred_element_type=F32,
        )
    top = stats.astype(BF)
    lane = lax.broadcasted_iota(jnp.int32, (rows, 128), 1) % 64
    under = (lane >= 3 * heads) & (lane < 4 * heads)
    d_branch[:, width:] = jnp.where(under, stats - top.astype(F32), stats).astype(BF)


def ffn_back_call(
    layer, scal, gy, unit2, rs2, slope, unit1, rs1, gain, att, oatt, w_up, w_down, w_out, after=()
):
    rows, width = gy.shape
    wide = w_up.shape[2]
    steps = wide // width
    out_shape = (
        sds((rows, width)), sds((rows, wide // 2)), sds((rows, wide // 2)),
        sds((rows, width + 128)), sds((rows, width), F32),
        sds((16, width), F32),
    )
    arrays = (gy, unit2, rs2, slope, unit1, rs1, gain, att, oatt)
    return call(
        functools.partial(ffn_back_kernel, layer),
        "ffn_back",
        out_shape,
        [whole(a.shape) for a in arrays] + [far()] * 3,
        tuple(whole(o.shape) for o in out_shape),
        (1,),
        [
            pltpu.VMEM((steps, width, width), BF),
            pltpu.VMEM((steps, width, width), BF),
            pltpu.VMEM((width, width), BF),
            pltpu.SemaphoreType.DMA((2 * steps + 1,)),
        ],
        1,
        arrays + (w_up, w_down, w_out),
        scal,
        after,
    )


def input_back_kernel(layer, s, d_first, dq, dkv, odq, odkv, w, gx, w_scr, sems):
    rows, width = d_first.shape
    half = width // 2
    core = s[0] % 2
    steps = w_scr.shape[0]
    tall = width // steps
    copies = fetch([(w.at[layer, pl.ds(n * tall, tall)], w_scr.at[n]) for n in range(steps)], sems)
    for n in range(steps):
        copies[n].wait()
        strip = slice(n * tall, (n + 1) * tall)
        result = d_first[:, strip]
        for at, q_part, kv_part in (
            (core * half, dq[:rows], dkv),
            ((1 - core) * half, odq[rows:], odkv),
        ):
            for i, part in enumerate((q_part, kv_part[:, :half], kv_part[:, half:])):
                columns = pl.ds(pl.multiple_of(i * width + at, 128), half)
                result = result + dot_nt(part, w_scr[n, :, columns])
        gx[:, strip] = result


def input_back_call(layer, scal, d_first, dq, dkv, odq, odkv, w_qkv, after=()):
    rows, width = d_first.shape
    arrays = (d_first, dq, dkv, odq, odkv)
    return call(
        functools.partial(input_back_kernel, layer),
        "input_back",
        sds((rows, width), F32),
        [whole(a.shape) for a in arrays] + [far()],
        whole((rows, width)),
        (1,),
        [pltpu.VMEM((3, width // 3, 3 * width), BF), pltpu.SemaphoreType.DMA((3,))],
        1,
        arrays + (w_qkv,),
        scal,
        after,
    )


def gather_rows(s, turned, picked, order):
    chip, core = s[0] // 2, s[0] % 2
    share = picked.shape[0] // 4
    for at in range(4):
        place = at if order is None else chip ^ order[at]
        begin = pl.multiple_of(place * (2 * share) + core * share, 32)
        picked[at * share : (at + 1) * share, :] = turned[pl.ds(begin, share), :]


def up_grad_kernel(s, x_m, x_o, *refs):
    keep, send, turned, picked = refs[-4:]
    rows, width = x_m.shape
    turned[:, :rows] = x_m[...].T
    turned[:, rows:] = x_o[...].T
    gather_rows(s, turned, picked, (0, 2, 1, 3))
    share = picked.shape[0] // 4
    steps = keep.shape[1] // share
    for n in range(steps):
        g_m, g_o = refs[:2] if n < steps // 2 else refs[2:4]
        at = n % (steps // 2)
        strip = slice(at * width, (at + 1) * width)
        grad = dot_nn(picked[:, :rows], g_m[:, strip]) + dot_nn(picked[:, rows:], g_o[:, strip])
        for at in range(2):
            place = slice(n * share, (n + 1) * share)
            keep[at, place, :] = grad[at * share : (at + 1) * share].astype(BF)
            send[at, place, :] = grad[(2 + at) * share : (3 + at) * share].astype(BF)


def up_grad_call(scal, *args, after=()):
    rows, width = args[0].shape
    out = sds((2, args[2].shape[1] // 4, width))
    return call(
        up_grad_kernel,
        "up_grad",
        (out, out),
        [whole(a.shape) for a in args],
        (whole(out.shape),) * 2,
        (1,),
        [pltpu.VMEM((width, 2 * rows), BF), pltpu.VMEM((width // 2, 2 * rows), BF)],
        1,
        args,
        scal,
        after,
    )


def down_grad_kernel(s, a_m, a_o, g_m, g_o, keep, send):
    n = pl.program_id(0)
    grad = dot_nn(a_m[...].T, g_m[...]) + dot_nn(a_o[...].T, g_o[...])
    grad = grad.astype(BF)

    @pl.when(n < 2)
    def _():
        keep[...] = grad

    @pl.when(n >= 2)
    def _():
        send[...] = grad


def down_grad_call(scal, a_m, a_o, g_m, g_o, after=()):
    rows, wide = a_m.shape
    width = g_m.shape[1]
    share = wide // 8
    strip = whole((rows, width))
    out = sds((2, share, width))
    picked = pl.BlockSpec((rows, share), lambda n, s: (0, 2 * ((s[0] // 2) ^ n) + s[0] % 2))
    return call(
        down_grad_kernel,
        "down_grad",
        (out, out),
        [picked, picked, strip, strip],
        (
            pl.BlockSpec((None, share, width), lambda n, s: (jnp.minimum(n, 1), 0, 0)),
            pl.BlockSpec((None, share, width), lambda n, s: (jnp.maximum(n - 2, 0), 0, 0)),
        ),
        (4,),
        [],
        1,
        (a_m, a_o, g_m, g_o),
        scal,
        after,
    )


def out_grad_kernel(joined, s, x_m, x_o, dq, dkv_m, dkv_r, odq, odkv_m, odkv_r, att, oatt, b_m, b_o,
    sums_m, sums_o, *refs,
):
    turned, picked = refs[-2:]
    keep_a, send_a, keep_b, send_b = refs[-6:-2]
    if joined:
        first_a, second_a, first_b, second_b = refs[:4]
        rows_in = first_a.shape[1]
        rows_out = keep_a.shape[1]
        send_b[:rows_in, :] = (first_a[1].astype(F32) + second_a[1].astype(F32)).astype(BF)
        send_a[:rows_in, :] = (first_b[1].astype(F32) + second_b[1].astype(F32)).astype(BF)
        sent_a, sent_b = (
            [ref.at[pl.ds(rows_in + at * rows_out, rows_out)] for at in range(2)]
            for ref in (send_a, send_b)
        )
    else:
        sent_a, sent_b = ([ref.at[at] for at in range(2)] for ref in (send_a, send_b))
    places_a = [keep_a.at[0], keep_a.at[1], sent_a[0], sent_a[1]]
    places_b = [keep_b.at[0], sent_b[0], keep_b.at[1], sent_b[1]]
    skip = 0
    rows, width = x_m.shape
    half = width // 2
    core = s[0] % 2
    share = width // 8
    mine = pl.ds(pl.multiple_of(core * half, 128), half)
    other = pl.ds(pl.multiple_of((1 - core) * half, 128), half)
    turned[:, :rows] = x_m[...].T
    turned[:, rows:] = x_o[...].T
    order = (0, 2, 1, 3)
    gather_rows(s, turned, picked, order)
    left_m, left_o = picked[:, :rows], picked[:, rows:]

    def put(places, begin, grad, columns):
        for at in range(4):
            part = grad[at * share : (at + 1) * share].astype(BF)
            places[at][begin : begin + share, columns] = part

    for at, places, begin in ((0, places_a, 0), (1, places_a, share), (2, places_b, skip)):
        if at == 0:
            pairs = ((dq[:rows], dq[rows:]), (odq[rows:], odq[:rows]))
        else:
            cut = slice((at - 1) * half, at * half)
            pairs = ((dkv_m[:, cut], dkv_r[:, cut]), (odkv_r[:, cut], odkv_m[:, cut]))
        for columns, (mine_rows, other_rows) in zip((mine, other), pairs):
            grad = dot_nn(left_m, mine_rows) + dot_nn(left_o, other_rows)
            put(places, begin, grad, columns)
    turned[mine, :] = att[:, :half].T
    turned[other, :rows] = oatt[rows:, :half].T
    turned[other, rows:] = oatt[:rows, :half].T
    gather_rows(s, turned, picked, order)
    grad = dot_nn(picked[:, :rows], b_m[:, :width])
    grad = grad + dot_nn(picked[:, rows:], b_o[:, :width])
    put(places_b, skip + share, grad, slice(0, width))
    small = (sums_m[...] + sums_o[...]).astype(BF)
    begin = skip + 2 * share
    ends = places_a + places_b
    for ref in ends:
        ref[begin:, :] = small
    value = [ref[:, half:] for ref in (dkv_m, dkv_r, odkv_m, odkv_r)]
    for row, parts in ((10, (dq[...], odq[...])), (11, value)):
        count = len(parts) // 2
        for columns, group in ((mine, parts[:count]), (other, parts[count:])):
            line = sum(jnp.sum(p.astype(F32), axis=0, keepdims=True) for p in group).astype(BF)
            for ref in ends:
                ref[begin + row : begin + row + 1, columns] = line


def out_grad_call(scal, *args, joined=(), after=()):
    rows, width = args[0].shape
    share = 2 * (width // 8) + 16
    keep = sds((2, share, width))
    send = sds((joined[0].shape[1] + 2 * share, width)) if joined else keep
    args += tuple(joined)
    return call(
        functools.partial(out_grad_kernel, bool(joined)),
        "out_grad",
        (keep, send, keep, send),
        [whole(a.shape) for a in args],
        (whole(keep.shape), whole(send.shape)) * 2,
        (1,),
        [pltpu.VMEM((width, 2 * rows), BF), pltpu.VMEM((width // 2, 2 * rows), BF)],
        1,
        args,
        scal,
        after,
    )


def over_core(array):
    return lax.ppermute(array, "seq", [(i, i ^ 1) for i in range(8)])


def over_x(array):
    return lax.ppermute(array, "seq", [(i, i ^ 2) for i in range(8)])


def over_y(array):
    return lax.ppermute(array, "seq", [(i, i ^ 4) for i in range(8)])


def over_bucket(array, pairs):
    return lax.ppermute(array, "bucket", pairs)


def view(ref, cut):
    if cut is None:
        return ref[...]
    return ref[cut] if isinstance(cut, int) else ref[cut[0] : cut[0] + cut[1], :]


def parted(parts):
    arrays = tuple(p[0] if isinstance(p, tuple) else p for p in parts)
    cuts = tuple(p[1] if isinstance(p, tuple) else None for p in parts)
    return arrays, cuts


def sum_kernel(cuts, s, *refs):
    total = sum(view(ref, cut).astype(F32) for ref, cut in zip(refs, cuts))
    refs[-1][...] = total.astype(BF)


def sum_call(scal, parts, shape, after=()):
    arrays, cuts = parted(parts)
    return call(
        functools.partial(sum_kernel, cuts), "sum", sds(shape), [whole(a.shape) for a in arrays],
        whole(shape), (1,), [], 1, arrays, scal, after,
    )


def sort_kernel(cuts, s, *refs):
    mine, other = refs[-2:]
    halves = [list(zip(refs[at : at + 3], cuts[at : at + 3])) for at in (0, 3)]
    outer = (s[0] == 0) | (s[0] == 3)

    def write(first, second):
        for out, half in ((mine, halves[first]), (other, halves[second])):
            out[...] = sum(view(ref, cut).astype(F32) for ref, cut in half).astype(BF)

    @pl.when(outer)
    def _():
        write(0, 1)

    @pl.when(jnp.logical_not(outer))
    def _():
        write(1, 0)


def bucket_start(zscal, keep_a, keep_b, got_a, got_b, pass_a, pass_b, after):
    parts = [first_of(keep_a), first_of(got_a), pass_a, first_of(keep_b), first_of(got_b), pass_b]
    arrays, cuts = parted(parts)
    shape = keep_a.shape[1:]
    mine, other = call(
        functools.partial(sort_kernel, cuts), "sort", (sds(shape),) * 2,
        [whole(a.shape) for a in arrays], (whole(shape),) * 2, (1,), [], 1, arrays, zscal, after,
    )
    return mine, over_bucket(other, NEAR)


def first_of(stack):
    return stack[0] if isinstance(stack, tuple) else (stack, 0)


def second_of(stack):
    return stack[1] if isinstance(stack, tuple) else (stack, 1)


def bucket_middle(scal, mine, got, after):
    mine = sum_call(scal, (mine, got), mine.shape, after)
    return mine, over_bucket(mine, FAR)


def bucket_last(scal, mine, got, after):
    mine = sum_call(scal, (mine, got), mine.shape, after)
    return mine, over_bucket(mine, NEAR)


def bucket_end(mine, other):
    place = lax.axis_index("bucket")
    outer = (place == 0) | (place == 3)
    return jnp.where(outer, mine, other), jnp.where(outer, other, mine)


def phase_one(keep_a, send_a, keep_b, send_b):
    return keep_a, keep_b, over_x(send_a), over_y(send_b)


def phase_two(scal, keep_a, keep_b, got_a, got_b, after):
    shape = keep_a.shape[1:]
    pass_a = sum_call(scal, (second_of(keep_a), second_of(got_a)), shape, after)
    pass_b = sum_call(scal, (second_of(keep_b), second_of(got_b)), shape, (pass_a,))
    return keep_a, keep_b, got_a, got_b, over_y(pass_a), over_x(pass_b), (pass_b,)


def fast_local(
    frames, w_qkv, b_qv, w_out, b_out, ln_gain, ln_shift, w_up, b_up, w_down, b_down,
    cotangent, clip_lengths, valid_lengths,
):
    rows, width = frames.shape[1:]
    place = lax.axis_index("seq")
    scal = place.astype(jnp.int32)[None]
    zscal = lax.axis_index("bucket").astype(jnp.int32)[None]
    blocks = place ^ jnp.arange(8, dtype=jnp.int32)
    position = (blocks[:, None] * rows + jnp.arange(rows, dtype=jnp.int32)[None]).reshape(-1)
    ends = jnp.cumsum(clip_lengths[0])
    starts = ends - clip_lengths[0]
    inside = (position[:, None] >= starts) & (position[:, None] < ends)
    segment = jnp.sum(jnp.where(inside, jnp.arange(ends.shape[0], dtype=jnp.int32), 0), axis=1)
    live = jnp.any(inside & (position[:, None] < starts + valid_lengths[0]), axis=1)
    tags = jnp.where(live, segment, -1).reshape(8, rows, 1)
    tags = jnp.broadcast_to(tags, (8, rows, 128))
    seg_rows = segment[None]
    seg_row = seg_rows[:, : 2 * rows]

    x = frames[0]
    saved = []
    before = ()
    for layer in range(LAYERS):
        attend = functools.partial(attend_call, layer, scal)
        x_r, x_x, x_y = over_core(x), over_x(x), over_y(x)
        kv, q, qt, w_all, acc, top = attend((), seg_row, w_qkv, b_qv, (x, x_r), tags, (0, 1))
        x_x, x_y = gate((x_x, x_y), (top,))
        x_d = over_y(x_x)
        x_xr, x_yr = over_core(x_x), over_core(x_y)
        kv_x, kv_y, q_x, q_y, acc, top = attend(
            (qt, w_all, acc, top), seg_row, w_qkv, b_qv, (x_x, x_xr, x_y, x_yr), tags,
            (2, 3, 4, 5), after=before,
        )
        (x_d,) = gate((x_d,), (top,))
        x_dr = over_core(x_d)
        kv_d, q_d, att = attend(
            (qt, w_all, acc, top), seg_row, w_qkv, b_qv, (x_d, x_dr), tags, (6, 7), last=True
        )
        oatt = over_core(att)
        unit1, rs1, normed, act, slope, unit2, rs2, y = ffn_call(
            layer, scal, x, att, oatt, w_out, b_out, ln_gain, ln_shift, w_up, b_up, w_down, b_down
        )
        before = (over_core(normed), over_core(act))
        saved.append(
            (x, x_r, q, q_x, q_y, q_d, kv, kv_x, kv_y, kv_d, att, oatt)
            + (unit1, rs1, normed, act, slope, unit2, rs2) + before
        )
        x = y
    activations = x[None]

    grad = cotangent[0]
    done = ()
    for layer in reversed(range(LAYERS)):
        top_layer = layer == LAYERS - 1
        x, x_r, q, q_x, q_y, q_d, kv, kv_x, kv_y, kv_d, att, oatt = saved[layer][:12]
        unit1, rs1, normed, act, slope, unit2, rs2, o_normed, o_act = saved[layer][12:]
        normed, act, o_normed, o_act = (stored(a) for a in (normed, act, o_normed, o_act))
        slope, unit1, unit2 = (stored(a) for a in (slope, unit1, unit2))
        d_down, d_up, d_up_more, ext, d_first, sums = ffn_back_call(
            layer, scal, grad, unit2, rs2, slope, unit1, rs1, ln_gain, att, oatt, w_up, w_down,
            w_out, done
        )
        ext_r, ext_x, ext_y = over_core(ext), over_x(ext), over_y(ext)
        o_up, o_more, o_down = over_core(d_up), over_core(d_up_more), over_core(d_down)
        done = before if top_layer else ()
        if not top_layer:
            done = ()
        w_mine, qt, dot, stats, dq, dkv, kv_near, tag_near = back_own_call(
            layer, scal, ext, ext_r, q, seg_rows, kv, tags, w_out, after=done
        )
        done = (dkv,)
        if not top_layer:
            early = bucket_start(zscal, *late[:-1], (dkv,))
            middle = phase_two(scal, *middle, early[:1])
            done = middle[-1]
        dq = back_dq_call(
            scal, qt, dot, stats, dq, seg_rows, (kv_x,), tags, (2, 3), False, after=done
        )
        ext_x, ext_y = gate((ext_x, ext_y), (dq,))
        ext_d = over_y(ext_x)
        ext_xr, ext_yr = over_core(ext_x), over_core(ext_y)
        keep_a, send_a = up_grad_call(
            scal, normed, o_normed, d_up, o_up, d_up_more, o_more, after=(ext_xr, ext_yr)
        )
        done = (keep_a,)
        if not top_layer:
            middle = bucket_start(zscal, *middle[:-1], done)
            done = middle[:1]
        keep_b, send_b = down_grad_call(scal, act, o_act, d_down, o_down, after=done)
        done = (keep_b,)
        if not top_layer:
            early = bucket_middle(scal, *early, done)
            done = early[:1]
        late = phase_one(keep_a, send_a, keep_b, send_b)
        dq = back_dq_call(
            scal, qt, dot, stats, dq, seg_rows, (kv_y, kv_d), tags, (4, 5, 6, 7), True, after=done
        )
        done = (dq,)
        odq = over_core(dq)
        (dkv,) = back_dkv_call(
            scal, w_mine, kv_near, tag_near, dkv, (ext_x, ext_xr, ext_y, ext_yr), (q_x, q_y),
            seg_rows, (1, 2), False, after=done
        )
        (ext_d,) = gate((ext_d,), (dkv,))
        ext_dr = over_core(ext_d)
        done = ()
        if not top_layer:
            middle = bucket_middle(scal, *middle, (dkv,))
            done = middle[:1]
        (sums,) = gate((sums,), (dkv,))
        o_sums = over_core(sums)
        g_m, g_r = back_dkv_call(
            scal, w_mine, kv_near, tag_near, dkv, (ext_d, ext_dr), (q_d,), seg_rows, (3,), True,
            after=done,
        )
        o_m, o_r = over_core(g_m), over_core(g_r)
        done = (g_m,)
        if not top_layer:
            early = bucket_last(scal, *early, done)
            done = early[:1]
        out_args = (
            stored(x), stored(x_r), dq, g_m, g_r, odq, o_m, o_r, stored(att), stored(oatt),
            stored(ext), stored(ext_r), sums, o_sums,
        )
        if top_layer:
            keep_a, keep_b, got_a, got_b = late
            middle_a, sent_x, middle_b, sent_y = out_grad_call(
                scal, *out_args, joined=(keep_a, got_a, keep_b, got_b), after=(o_m,)
            )
            got_x, got_y = over_x(sent_x), over_y(sent_y)
            first, more = keep_a.shape[1], middle_a.shape[1]
            late += ((got_y, (0, first)), (got_x, (0, first)), ())
            middle = (middle_a, middle_b) + tuple(
                ((got, (first, more)), (got, (first + more, more))) for got in (got_x, got_y)
            )
            done = (middle_a,)
        grad = input_back_call(layer, scal, d_first, dq, g_m, odq, o_r, w_qkv, after=(o_m,) + done)
        done = (grad,)
    late = phase_two(scal, *late, done)
    middle = bucket_last(scal, *middle, late[-1])
    parts = out_grad_call(scal, *out_args, after=middle[:1] + early[1:])
    last = phase_one(*parts)
    late = bucket_start(zscal, *late[:-1], parts[:1])
    last = phase_two(scal, *last, late[:1] + middle[1:])
    late = bucket_middle(scal, *late, last[-1])
    last = bucket_start(zscal, *last[:-1], late[:1])
    last = bucket_middle(scal, *last, last[:1])
    late = bucket_last(scal, *late, last[:1])
    last = bucket_last(scal, *last, late[:1])
    ffn_1, att_1, ffn_0, att_0 = (bucket_end(*pair) for pair in (early, middle, late, last))
    ffn_parts = (ffn_0, ffn_1)
    att_parts = (att_0, att_1)

    share = width // 8

    def both(make):
        return jnp.stack([make(layer).astype(F32) for layer in range(LAYERS)])

    small = both(lambda l: att_parts[l][0][2 * share :])

    def own(array, axis):
        size = array.shape[axis] // 8
        return lax.dynamic_slice_in_dim(array, place * size, size, axis)

    def beside(array):
        parts = array.shape[0] // share
        return array.reshape(parts, share, width).transpose(1, 0, 2).reshape(share, -1)

    return (
        activations,
        grad[None],
        both(
            lambda l: jnp.concatenate(
                [beside(att_parts[l][0][: 2 * share]), att_parts[l][1][:share]], axis=1
            )
        ),
        own(small[:, 10:12].reshape(LAYERS, -1), 1),
        both(lambda l: att_parts[l][1][share : 2 * share]),
        own(small[:, 4], 1),
        own(small[:, 0:2], 2),
        own(small[:, 2:4], 2),
        both(lambda l: beside(ffn_parts[l][0])),
        own(small[:, 6:10].reshape(LAYERS, -1), 1),
        both(lambda l: ffn_parts[l][1]),
        own(small[:, 5], 1),
    )


def clip_tags(lengths, valid, begin, count):
    position = begin + jnp.arange(count, dtype=jnp.int32)
    ends = jnp.cumsum(lengths)
    starts = ends - lengths
    inside = (position[:, None] >= starts[None, :]) & (position[:, None] < ends[None, :])
    labels = jnp.arange(lengths.shape[0], dtype=jnp.int32)
    segment = jnp.sum(jnp.where(inside, labels[None, :], 0), axis=1)
    live = jnp.any(inside & (position[:, None] < (starts + valid)[None, :]), axis=1)
    return (segment, jnp.where(live, segment, -1))


def layer_norm(hidden, gain, shift):
    center = hidden - jnp.mean(hidden, axis=-1, keepdims=True)
    spread = jnp.mean(center * center, axis=-1, keepdims=True)
    return center * lax.rsqrt(spread + 1e-05) * gain + shift


def exact_gelu(hidden):
    return jax.nn.gelu(hidden, approximate=False)


def split_heads(matrix):
    return matrix.reshape(matrix.shape[0], HEADS, -1)


def pair_terms(
    query_heads,
    grad_heads,
    log_total,
    correction,
    query_seg,
    key_heads,
    value_heads,
    key_tag,
    scale,
):
    scores = (
        jnp.einsum("qhd,khd->hqk", query_heads, key_heads, preferred_element_type=jnp.float32)
        * scale
    )
    allowed = (query_seg[:, None] == key_tag[None, :])[None]
    scores = jnp.where(allowed, scores, -1e30)
    probs = jnp.where(allowed, jnp.exp(scores - log_total[..., None]), 0.0)
    grad_probs = jnp.einsum(
        "qhd,khd->hqk", grad_heads, value_heads, preferred_element_type=jnp.float32
    )
    grad_scores = (probs * (grad_probs - correction[..., None])).astype(jnp.bfloat16)
    return (probs.astype(jnp.bfloat16), grad_scores)


def forward_layer(hidden, weights, query_seg, lengths, valid):
    w_qkv, b_qv, w_out, b_out, gain, shift, w_up, b_up, w_down, b_down = weights
    rows, width = hidden.shape
    scale = (width // HEADS) ** (-0.5)
    inputs = hidden.astype(jnp.bfloat16)
    projected = jnp.dot(inputs, w_qkv, preferred_element_type=jnp.float32)
    queries = (projected[:, :width] + b_qv[:width]).astype(jnp.bfloat16)
    keys = projected[:, width : 2 * width].astype(jnp.bfloat16)
    values = (projected[:, 2 * width :] + b_qv[width:]).astype(jnp.bfloat16)
    query_heads = split_heads(queries)
    initial = (
        jnp.full((HEADS, rows), -1e30, jnp.float32),
        jnp.zeros((HEADS, rows), jnp.float32),
        jnp.zeros((HEADS, rows, width // HEADS), jnp.float32),
    )
    key_piece = lax.all_gather(keys, "seq", axis=0, tiled=True)
    value_piece = lax.all_gather(values, "seq", axis=0, tiled=True)
    count = key_piece.shape[0] // rows
    key_blocks = key_piece.reshape(count, rows, HEADS, -1)
    value_blocks = value_piece.reshape(count, rows, HEADS, -1)

    def fold_inner(state, item):
        key_heads, value_heads, block_at = item
        _, block_tag = clip_tags(lengths, valid, block_at * rows, rows)
        running, denominator, weighted = state
        scores = (
            jnp.einsum("qhd,khd->hqk", query_heads, key_heads, preferred_element_type=jnp.float32)
            * scale
        )
        allowed = (query_seg[:, None] == block_tag[None, :])[None]
        scores = jnp.where(allowed, scores, -1e30)
        raised = jnp.maximum(running, jnp.max(scores, axis=-1))
        block_probs = jnp.where(allowed, jnp.exp(scores - raised[..., None]), 0.0)
        factor = jnp.exp(running - raised)
        denominator = denominator * factor + jnp.sum(block_probs, axis=-1)
        weighted = weighted * factor[..., None] + jnp.einsum(
            "hqk,khd->hqd",
            block_probs.astype(jnp.bfloat16),
            value_heads,
            preferred_element_type=jnp.float32,
        )
        return ((raised, denominator, weighted), None)

    state, _ = lax.scan(
        fold_inner, initial, (key_blocks, value_blocks, jnp.arange(count, dtype=jnp.int32))
    )
    running, denominator, weighted = state
    attended = (weighted / denominator[..., None]).transpose(1, 0, 2).reshape(rows, width)
    log_total = running + jnp.log(denominator)
    attended_low = attended.astype(jnp.bfloat16)
    branch = jnp.dot(attended_low, w_out, preferred_element_type=jnp.float32) + b_out
    first_sum = inputs.astype(jnp.float32) + branch
    normed = layer_norm(first_sum, gain[0], shift[0]).astype(jnp.bfloat16)
    up_pre = jnp.dot(normed, w_up, preferred_element_type=jnp.float32) + b_up
    activated = exact_gelu(up_pre).astype(jnp.bfloat16)
    second_sum = (
        normed.astype(jnp.float32)
        + jnp.dot(activated, w_down, preferred_element_type=jnp.float32)
        + b_down
    )
    output = layer_norm(second_sum, gain[1], shift[1])
    kept = (
        inputs,
        queries,
        keys,
        values,
        attended,
        attended_low,
        log_total,
        None,
        first_sum,
        normed,
        up_pre,
        activated,
        second_sum,
    )
    return (output, kept)


def attention_grads(kept, grad_att, query_seg, lengths, valid):
    (
        inputs,
        queries,
        keys,
        values,
        attended,
        attended_low,
        log_total,
        gathered,
        first_sum,
        normed,
        up_pre,
        activated,
        second_sum,
    ) = kept
    rows, width = queries.shape
    scale = (width // HEADS) ** (-0.5)
    query_heads = split_heads(queries)
    grad_heads = split_heads(grad_att)
    correction = jnp.sum(grad_heads.astype(jnp.float32) * split_heads(attended), axis=-1).T
    key_all, value_all = (
        lax.all_gather(keys, "seq", axis=0, tiled=True),
        lax.all_gather(values, "seq", axis=0, tiled=True),
    )
    count = key_all.shape[0] // rows
    key_blocks = key_all.reshape(count, rows, HEADS, -1)
    value_blocks = value_all.reshape(count, rows, HEADS, -1)
    block_ids = jnp.arange(count, dtype=jnp.int32)
    zero_heads = jnp.zeros((rows, HEADS, width // HEADS), jnp.float32)

    def attention_inner(acc, item):
        key_heads, value_heads, block_at = item
        _, block_tag = clip_tags(lengths, valid, block_at * rows, rows)
        probs, grad_scores = pair_terms(
            query_heads,
            grad_heads,
            log_total,
            correction,
            query_seg,
            key_heads,
            value_heads,
            block_tag,
            scale,
        )
        acc = (
            acc
            + jnp.einsum("hqk,khd->qhd", grad_scores, key_heads, preferred_element_type=jnp.float32)
            * scale
        )
        key_term = (
            jnp.einsum("hqk,qhd->khd", grad_scores, query_heads, preferred_element_type=jnp.float32)
            * scale
        )
        value_term = jnp.einsum(
            "hqk,qhd->khd", probs, grad_heads, preferred_element_type=jnp.float32
        )
        return (
            acc,
            jnp.concatenate(
                [key_term.reshape(rows, width), value_term.reshape(rows, width)], axis=1
            ),
        )

    grad_query, terms = lax.scan(attention_inner, zero_heads, (key_blocks, value_blocks, block_ids))
    summed = lax.psum_scatter(
        terms.reshape(count * rows, 2 * width).astype(jnp.bfloat16),
        "seq",
        scatter_dimension=0,
        tiled=True,
    ).astype(jnp.float32)
    grad_key = summed[:, :width]
    grad_value = summed[:, width:]
    return (grad_query.reshape(rows, width), grad_key, grad_value)


def backward_layer(grad_out, kept, weights, query_seg, lengths, valid):
    w_qkv, b_qv, w_out, b_out, gain, shift, w_up, b_up, w_down, b_down = weights
    (
        inputs,
        queries,
        keys,
        values,
        attended,
        attended_low,
        log_total,
        gathered,
        first_sum,
        normed,
        up_pre,
        activated,
        second_sum,
    ) = kept
    _, pull_second = jax.vjp(layer_norm, second_sum, gain[1], shift[1])
    grad_second, gain_second, shift_second = pull_second(grad_out)
    grad_down = grad_second.astype(jnp.bfloat16)
    sum_down = jnp.sum(grad_down, axis=0, dtype=jnp.float32)
    weight_down = jnp.einsum("rf,rd->fd", activated, grad_down, preferred_element_type=jnp.float32)
    grad_activated = jnp.einsum("rd,fd->rf", grad_down, w_down, preferred_element_type=jnp.float32)
    _, pull_gelu = jax.vjp(exact_gelu, up_pre)
    grad_up = pull_gelu(grad_activated)[0].astype(jnp.bfloat16)
    sum_up = jnp.sum(grad_up, axis=0, dtype=jnp.float32)
    weight_up = jnp.einsum("rd,rf->df", normed, grad_up, preferred_element_type=jnp.float32)
    grad_normed = grad_second + jnp.einsum(
        "rf,df->rd", grad_up, w_up, preferred_element_type=jnp.float32
    )
    _, pull_first = jax.vjp(layer_norm, first_sum, gain[0], shift[0])
    grad_first, gain_first, shift_first = pull_first(grad_normed)
    grad_branch = grad_first.astype(jnp.bfloat16)
    sum_out = jnp.sum(grad_branch, axis=0, dtype=jnp.float32)
    weight_out = jnp.einsum(
        "re,rd->ed", attended_low, grad_branch, preferred_element_type=jnp.float32
    )
    grad_att = jnp.einsum(
        "rd,ed->re", grad_branch, w_out, preferred_element_type=jnp.float32
    ).astype(jnp.bfloat16)
    grad_query, grad_key, grad_value = attention_grads(kept, grad_att, query_seg, lengths, valid)
    grad_proj = jnp.concatenate(
        [
            grad_query.astype(jnp.bfloat16),
            grad_key.astype(jnp.bfloat16),
            grad_value.astype(jnp.bfloat16),
        ],
        axis=1,
    )
    width = inputs.shape[1]
    sum_qv = jnp.concatenate(
        [
            jnp.sum(grad_proj[:, :width], axis=0, dtype=jnp.float32),
            jnp.sum(grad_proj[:, 2 * width :], axis=0, dtype=jnp.float32),
        ]
    )
    weight_qkv = jnp.einsum("rd,re->de", inputs, grad_proj, preferred_element_type=jnp.float32)
    grad_input = grad_first + jnp.einsum(
        "re,de->rd", grad_proj, w_qkv, preferred_element_type=jnp.float32
    )
    gains = jnp.stack([gain_first, gain_second])
    shifts = jnp.stack([shift_first, shift_second])
    return (
        grad_input,
        (
            weight_qkv,
            sum_qv,
            weight_out,
            sum_out,
            gains,
            shifts,
            weight_up,
            sum_up,
            weight_down,
            sum_down,
        ),
    )


def local(
    frames,
    w_qkv,
    b_qv,
    w_out,
    b_out,
    ln_gain,
    ln_shift,
    w_up,
    b_up,
    w_down,
    b_down,
    cotangent,
    clip_lengths,
    valid_lengths,
):
    rows = frames.shape[1]
    lengths = clip_lengths[0]
    valid = valid_lengths[0]
    offset = lax.axis_index("seq") * rows
    query_seg, key_tag = clip_tags(lengths, valid, offset, rows)
    layer_weights = [
        tuple(
            (
                array[layer_at]
                for array in (
                    w_qkv,
                    b_qv,
                    w_out,
                    b_out,
                    ln_gain,
                    ln_shift,
                    w_up,
                    b_up,
                    w_down,
                    b_down,
                )
            )
        )
        for layer_at in range(LAYERS)
    ]
    hidden = frames[0].astype(jnp.float32)
    saved = []
    for layer_at in range(LAYERS):
        hidden, kept = forward_layer(hidden, layer_weights[layer_at], query_seg, lengths, valid)
        saved.append(kept)
    activations = hidden.astype(jnp.bfloat16)[None]
    grad_hidden = cotangent[0].astype(jnp.float32)
    per_layer = [None] * LAYERS
    for layer_at in reversed(range(LAYERS)):
        grad_hidden, per_layer[layer_at] = backward_layer(
            grad_hidden, saved[layer_at], layer_weights[layer_at], query_seg, lengths, valid
        )
    stacked = [
        jnp.stack([per_layer[layer_at][member] for layer_at in range(LAYERS)])
        for member in range(10)
    ]
    g_wqkv, g_bqv, g_wout, g_bout, g_gain, g_shift, g_wup, g_bup, g_wdown, g_bdown = stacked
    shares = (
        lax.psum_scatter(
            g_wqkv.astype(jnp.bfloat16), "seq", scatter_dimension=1, tiled=True
        ).astype(jnp.float32),
        lax.psum_scatter(g_bqv.astype(jnp.bfloat16), "seq", scatter_dimension=1, tiled=True).astype(
            jnp.float32
        ),
        lax.psum_scatter(
            g_wout.astype(jnp.bfloat16), "seq", scatter_dimension=1, tiled=True
        ).astype(jnp.float32),
        lax.psum_scatter(
            g_bout.astype(jnp.bfloat16), "seq", scatter_dimension=1, tiled=True
        ).astype(jnp.float32),
        lax.psum_scatter(
            g_gain.astype(jnp.bfloat16), "seq", scatter_dimension=2, tiled=True
        ).astype(jnp.float32),
        lax.psum_scatter(
            g_shift.astype(jnp.bfloat16), "seq", scatter_dimension=2, tiled=True
        ).astype(jnp.float32),
        lax.psum_scatter(g_wup.astype(jnp.bfloat16), "seq", scatter_dimension=1, tiled=True).astype(
            jnp.float32
        ),
        lax.psum_scatter(g_bup.astype(jnp.bfloat16), "seq", scatter_dimension=1, tiled=True).astype(
            jnp.float32
        ),
        lax.psum_scatter(
            g_wdown.astype(jnp.bfloat16), "seq", scatter_dimension=1, tiled=True
        ).astype(jnp.float32),
        lax.psum_scatter(
            g_bdown.astype(jnp.bfloat16), "seq", scatter_dimension=1, tiled=True
        ).astype(jnp.float32),
    )
    s_wqkv, s_bqv, s_wout, s_bout, s_gain, s_shift, s_wup, s_bup, s_wdown, s_bdown = shares
    totals = (
        lax.psum(s_wqkv.astype(jnp.bfloat16), "bucket").astype(jnp.float32),
        lax.psum(s_bqv.astype(jnp.bfloat16), "bucket").astype(jnp.float32),
        lax.psum(s_wout.astype(jnp.bfloat16), "bucket").astype(jnp.float32),
        lax.psum(s_bout.astype(jnp.bfloat16), "bucket").astype(jnp.float32),
        lax.psum(s_gain.astype(jnp.bfloat16), "bucket").astype(jnp.float32),
        lax.psum(s_shift.astype(jnp.bfloat16), "bucket").astype(jnp.float32),
        lax.psum(s_wup.astype(jnp.bfloat16), "bucket").astype(jnp.float32),
        lax.psum(s_bup.astype(jnp.bfloat16), "bucket").astype(jnp.float32),
        lax.psum(s_wdown.astype(jnp.bfloat16), "bucket").astype(jnp.float32),
        lax.psum(s_bdown.astype(jnp.bfloat16), "bucket").astype(jnp.float32),
    )
    return (
        activations,
        grad_hidden[None],
        totals[0],
        totals[1],
        totals[2],
        totals[3],
        totals[4],
        totals[5],
        totals[6],
        totals[7],
        totals[8],
        totals[9],
    )


def solution(mesh):
    placed = (
        P("bucket", "seq", None),
        P(),
        P(),
        P(),
        P(),
        P(),
        P(),
        P(),
        P(),
        P(),
        P(),
        P("bucket", "seq", None),
        P("bucket", None),
        P("bucket", None),
    )
    chips_2x2 = mesh.shape["seq"] == 8 and mesh.shape["bucket"] == 4
    return jax.shard_map(
        fast_local if chips_2x2 else local,
        mesh=mesh,
        in_specs=placed,
        out_specs=(
            P("bucket", "seq", None),
            P("bucket", "seq", None),
            P(None, "seq", None),
            P(None, "seq"),
            P(None, "seq", None),
            P(None, "seq"),
            P(None, None, "seq"),
            P(None, None, "seq"),
            P(None, "seq", None),
            P(None, "seq"),
            P(None, "seq", None),
            P(None, "seq"),
        ),
        check_vma=False,
    )
```

```python
import functools
import math

import jax
import jax.numpy as jnp
from jax import lax
from jax.experimental import pallas as pl
from jax.experimental.pallas import tpu as pltpu
from jax.sharding import PartitionSpec as P

HEADS = 12
LAYERS = 2
NEAR = [(0, 1), (1, 0), (2, 3), (3, 2)]
FAR = [(0, 3), (3, 0), (1, 2), (2, 1)]
BF = jnp.bfloat16
F32 = jnp.float32
LOW = -1e30
SLACK = 6 * 1024 * 1024


def dot_nn(a, b):
    return lax.dot_general(a, b, (((1,), (0,)), ((), ())), preferred_element_type=F32)


def dot_nt(a, b):
    return lax.dot_general(a, b, (((1,), (1,)), ((), ())), preferred_element_type=F32)


def block_bytes(spec, array):
    if spec.block_shape is None:
        return 0
    lanes = [n for n in spec.block_shape if n is not None]
    lanes[-1] += -lanes[-1] % 128
    return math.prod(lanes) * array.dtype.itemsize


def call(body, name, out_shape, in_specs, out_specs, grid, scratch, flops, args, scalars, after=()):
    args = tuple(
        stored(a) if p.memory_space == pltpu.HBM else a for p, a in zip(in_specs, args)
    )
    count = len(args)

    def run(scal, *refs):
        body(scal, *refs[:count], *refs[count + len(after) :])

    need = sum(block_bytes(p, a) for p, a in zip(in_specs, args))
    need += sum(block_bytes(p, a) for p, a in zip(jax.tree.leaves(out_specs), jax.tree.leaves(out_shape)))
    need = need + sum(
        math.prod(m.shape) * jnp.dtype(m.dtype).itemsize for m in scratch if m.memory_space == pltpu.VMEM
    )
    return pl.pallas_call(
        run,
        name=name,
        out_shape=out_shape,
        grid_spec=pltpu.PrefetchScalarGridSpec(
            num_scalar_prefetch=1,
            grid=grid,
            in_specs=list(in_specs) + [pl.BlockSpec(memory_space=pl.ANY)] * len(after),
            out_specs=out_specs,
            scratch_shapes=scratch,
        ),
        compiler_params=pltpu.CompilerParams(vmem_limit_bytes=need + SLACK),
        cost_estimate=pl.CostEstimate(
            flops=int(flops), bytes_accessed=1 + int(flops / 400), transcendentals=0
        ),
    )(scalars, *args, *after)


def whole(shape):
    return pl.BlockSpec(shape, lambda i, s: (0,) * len(shape))


def kept(shape, dtype=BF):
    return pltpu.HBM(shape, dtype)


def near(shape, dtype=BF):
    return pltpu.VMEM(shape, dtype)


def held(array):
    return pltpu.with_memory_space_constraint(array, pltpu.VMEM)


def stored(array):
    return pltpu.with_memory_space_constraint(array, pltpu.HBM)


def gate(arrays, after, space=pltpu.VMEM):
    anywhere = pl.BlockSpec(memory_space=pl.ANY)
    count = len(arrays)

    def body(*refs):
        pass

    return pl.pallas_call(
        body,
        name="gate",
        out_shape=tuple(sds(a.shape, a.dtype) for a in arrays),
        in_specs=[anywhere] * (count + len(after)),
        out_specs=(anywhere,) * count,
        input_output_aliases={i: i for i in range(count)},
        compiler_params=pltpu.CompilerParams(vmem_limit_bytes=1024 * 1024),
        cost_estimate=pl.CostEstimate(flops=1, bytes_accessed=1, transcendentals=0),
    )(*(pltpu.with_memory_space_constraint(a, space) for a in arrays), *after)


def far():
    return pl.BlockSpec(memory_space=pltpu.HBM)


def fetch(pairs, sems):
    copies = [pltpu.make_async_copy(src, dst, sems.at[i]) for i, (src, dst) in enumerate(pairs)]
    for copy in copies:
        copy.start()
    return copies


def sds(shape, dtype=BF):
    return jax.ShapeDtypeStruct(shape, dtype)


def mask_of(tag, seg):
    ok = jnp.concatenate([tag] * (seg.shape[1] // 128), axis=1) == seg
    return jnp.where(ok, 0.0, LOW)


def attend_kernel(layer, chips, first, last, *refs):
    refs = list(refs)
    core = refs.pop(0)[0] % 2
    if not first:
        qt, w_all, acc_in, m_in = (refs.pop(0) for _ in range(4))
    seg_ref, bias_ref, bias_k, w_ref = (refs.pop(0) for _ in range(4))
    xs = [refs.pop(0) for _ in range(2 * chips)]
    tags = [refs.pop(0) for _ in range(2 * chips)]
    kv_outs = [refs.pop(0) for _ in range(chips)]
    q_outs = [refs.pop(0) for _ in range(chips)]
    if first:
        qt, w_all = (refs.pop(0) for _ in range(2))
    if last:
        att_ref = refs.pop(0)
    else:
        acc_out, m_out = refs.pop(0), refs.pop(0)
    s_scr, vt_scr, kvs, qs, out_sems = (refs.pop(0) for _ in range(5))
    rows, width = xs[0].shape
    half = width // 2
    heads = half // 64
    queries = seg_ref.shape[1]
    high = vt_scr.shape[1]
    pair = 2 * rows
    leaving = []

    def leave(src, dst):
        copy = pltpu.make_async_copy(src, dst, out_sems.at[len(leaving)])
        copy.start()
        leaving.append(copy)

    if first:
        sems = refs.pop(0)
        begin = [pl.multiple_of(width * i + core * half, 128) for i in range(3)]
        copies = fetch(
            [(w_ref.at[layer, :, pl.ds(begin[i], half)], w_all.at[i]) for i in range(3)], sems
        )
    bias_q = bias_ref[layer : layer + 1, :]
    bias_v = bias_k[layer : layer + 1, :]
    for c in range(chips):
        x = jnp.concatenate([xs[2 * c][...], xs[2 * c + 1][...]], axis=0)
        if first:
            copies.pop(0).wait()
        q = (dot_nn(x, w_all[0]) + bias_q).astype(BF) * BF(0.125)
        qs[c] = q
        leave(qs.at[c], q_outs[c])
        if first:
            qt[...] = q.T
            copies.pop(0).wait()
            copies.pop(0).wait()
        kvs[c, :, :half] = dot_nn(x, w_all[1]).astype(BF)
        values = (dot_nn(x, w_all[2]) + bias_v).astype(BF)
        kvs[c, :, half:] = values
        leave(kvs.at[c], kv_outs[c])
        turned = values.T
        for h in range(heads):
            vt_scr[h, :64, c * pair : (c + 1) * pair] = turned[h * 64 : (h + 1) * 64]
    vt_scr[:, 64:, :] = jnp.ones((heads, high - 64, chips * pair), BF)
    seg = seg_ref[...]
    outs, lses = [], []
    if not last:
        m_out[...] = jnp.zeros_like(m_out)
    for h in range(heads):
        qh = qt[h * 64 : (h + 1) * 64, :]
        m8 = None
        for b in range(2 * chips):
            key = slice((b % 2) * rows, (b % 2 + 1) * rows)
            scores = dot_nn(kvs[b // 2, key, h * 64 : (h + 1) * 64], qh)
            ok = jnp.concatenate([tags[b][...]] * (queries // 128), axis=1) == seg
            scores = jnp.where(ok, scores, LOW)
            s_scr[h % 2, b * rows : (b + 1) * rows, :] = scores
            top = jnp.max(scores.reshape(rows // 8, 8, queries), axis=0)
            m8 = top if m8 is None else jnp.maximum(m8, top)
        m = jnp.max(m8, axis=0, keepdims=True)
        if not first:
            m_old = m_in[h : h + 1, :]
            m = jnp.maximum(m, m_old)
        acc = jnp.zeros((high, queries), F32)
        for b in range(2 * chips):
            probs = jnp.exp(s_scr[h % 2, b * rows : (b + 1) * rows, :] - m).astype(BF)
            acc = acc + dot_nn(vt_scr[h, :, b * rows : (b + 1) * rows], probs)
        if not first:
            acc = acc + acc_in[h] * jnp.exp(m_old - m)
        if last:
            total = acc[64:65]
            outs.append((acc[:64] / total).astype(BF))
            lses.append(m + jnp.log(total))
        else:
            acc_out[h] = acc
            m_out[h : h + 1, :] = m
    if last:
        lse = jnp.concatenate(lses, axis=0)
        top = lse.astype(BF).astype(F32)
        rest = jnp.zeros((128 - 2 * heads, queries), F32)
        tail = jnp.concatenate([top, lse - top, rest], axis=0)
        att_ref[:, :half] = jnp.concatenate(outs, axis=0).T
        att_ref[:, half:] = tail.T.astype(BF)
    for copy in leaving:
        copy.wait()


def tag_specs(tag_ids, rows):
    return [pl.BlockSpec((None, rows, 128), lambda i, s, r=r: (r, 0, 0)) for r in tag_ids]


def attend_call(layer, scal, state, seg_row, w_qkv, b_qv, xs, tags, tag_ids, last=False, after=()):
    first = not state
    rows, width = xs[0].shape
    half = width // 2
    heads = half // 64
    queries = 2 * rows
    chips = len(xs) // 2
    high = 80
    out_shape = tuple(kept((2 * rows, width)) for _ in range(chips))
    out_shape += tuple(kept((2 * rows, half)) for _ in range(chips))
    if first:
        out_shape += (near((half, queries)), near((3, width, half)))
    if last:
        out_shape += (sds((queries, half + 128)),)
    else:
        out_shape += (near((heads, high, queries), F32), near((8, queries), F32))
    out_specs = [whole(o.shape) for o in out_shape]
    for i in range(2 * chips):
        out_specs[i] = far()

    def bias(part):
        return pl.BlockSpec((LAYERS, half), lambda i, s: (0, 2 * part + s[0] % 2))

    state = tuple(held(a) for a in state)
    specs = [whole(a.shape) for a in state]
    specs += [whole(seg_row.shape), bias(0), bias(1), far()]
    specs += [whole(x.shape) for x in xs] + tag_specs(tag_ids, rows)
    args = state + (seg_row, b_qv, b_qv, w_qkv) + tuple(xs) + (tags,) * len(xs)
    scratch = [
        pltpu.VMEM((2, chips * 2 * rows, queries), F32),
        pltpu.VMEM((heads, high, chips * 2 * rows), BF),
        pltpu.VMEM((chips, 2 * rows, width), BF),
        pltpu.VMEM((chips, 2 * rows, half), BF),
        pltpu.SemaphoreType.DMA((2 * chips,)),
    ]
    if first:
        scratch.append(pltpu.SemaphoreType.DMA((3,)))
    return call(
        functools.partial(attend_kernel, layer, chips, first, last),
        "attend",
        out_shape,
        specs,
        tuple(out_specs),
        (1,),
        scratch,
        chips * 12 * 4 * queries * half * rows,
        args,
        scal,
        after,
    )


def back_queries(core, ext_m, ext_r, w_out, turned_scr):
    rows, wide = ext_m.shape
    width = wide - 128
    ext = jnp.concatenate([ext_m[...], ext_r[...]], axis=0)
    grad = dot_nt(ext[:, :width], w_out).astype(BF)
    turned_scr[...] = ext[:, width:].T.astype(F32)
    part = turned_scr[pl.ds(pl.multiple_of(core * 64, 64), 64), :]
    heads = width // 128
    lse = part[:heads] + part[heads : 2 * heads]
    corr = part[2 * heads : 3 * heads] + part[3 * heads : 4 * heads]
    return grad, grad.T, lse, corr


def pair_terms_kernel(keys, values, qt, dot, lse, corr, mask):
    scores = dot_nn(keys, qt)
    grad = dot_nn(values, dot)
    probs = jnp.exp(scores - lse + mask)
    return probs.astype(BF), (probs * (grad - corr)).astype(BF)


def back_own_kernel(
    layer, s, ext_m, ext_r, q, seg_ref, kv, tag_m, tag_r, w_ref,
    w_out, qt, dot, stats, dq, dkv, kv_out, tag_out, turned_scr, sems,
):
    core = s[0] % 2
    rows = ext_m.shape[0]
    half = q.shape[1]
    heads = half // 64
    queries = 2 * rows
    (copy,) = fetch(
        [(w_ref.at[layer, pl.ds(pl.multiple_of(core * half, 128), half)], w_out)], sems
    )
    kv_out[...] = kv[...]
    tag_out[0] = tag_m[...]
    tag_out[1] = tag_r[...]
    qt[...] = q[...].T
    copy.wait()
    do, turned, lse, corr = back_queries(core, ext_m, ext_r, w_out[...], turned_scr)
    dot[...] = turned
    stats[...] = jnp.zeros_like(stats)
    stats[:heads, :] = lse
    stats[8 : 8 + heads, :] = corr
    seg = seg_ref[...]
    for b in range(2):
        key = slice(b * rows, (b + 1) * rows)
        kt = kv[key, :half].T
        ok = mask_of(tag_out[b], seg)
        for h in range(heads):
            sl = slice(h * 64, (h + 1) * 64)
            vl = slice(half + h * 64, half + (h + 1) * 64)
            probs, grad = pair_terms_kernel(
                kv[key, sl], kv[key, vl], qt[sl, :], dot[sl, :], lse[h : h + 1],
                corr[h : h + 1], ok,
            )
            term = dot_nn(kt[sl], grad)
            if b == 0:
                dq[sl, :] = term
            else:
                dq[sl, :] += term
            dkv[key, sl] = dot_nn(grad, q[:, sl])
            dkv[key, vl] = dot_nn(probs, do[:, sl])


def back_own_call(layer, scal, ext_m, ext_r, q, seg_rows, kv, tags, w_out, after=()):
    rows = ext_m.shape[0]
    queries, half = q.shape
    width = 2 * half
    out_shape = (
        near((half, width)), near((half, queries)), near((half, queries)),
        near((16, queries), F32), near((half, queries), F32), near((queries, width), F32),
        near((queries, width)), near((2, rows, 128), jnp.int32),
    )
    return call(
        functools.partial(back_own_kernel, layer),
        "back_own",
        out_shape,
        [whole(ext_m.shape), whole(ext_r.shape), whole(q.shape), seg_spec(queries, 0), whole(kv.shape)]
        + tag_specs((0, 1), rows) + [far()],
        tuple(whole(o.shape) for o in out_shape),
        (1,),
        [pltpu.VMEM((128, queries), F32), pltpu.SemaphoreType.DMA((1,))],
        1,
        (ext_m, ext_r, q, seg_rows, kv, tags, tags, w_out),
        scal,
        after,
    )


def seg_spec(queries, at):
    return pl.BlockSpec((1, queries), lambda i, s: (0, at))


def back_dq_kernel(chips, last, s, *refs):
    refs = list(refs)
    qt, dot, stats, dq_in, seg_ref = (refs.pop(0) for _ in range(5))
    kvs = [refs.pop(0) for _ in range(chips)]
    tags = [refs.pop(0) for _ in range(2 * chips)]
    dq_out, dq_scr, kv_scr, sems = refs
    copies = fetch([(kvs[c], kv_scr.at[c]) for c in range(chips)], sems)
    rows = tags[0].shape[0]
    half, queries = qt.shape
    heads = half // 64
    seg = seg_ref[...]
    dq_scr[...] = dq_in[...]
    for c in range(chips):
        copies[c].wait()
        for b in range(2):
            key = slice(b * rows, (b + 1) * rows)
            kt = kv_scr[c, key, :half].T
            ok = mask_of(tags[2 * c + b][...], seg)
            for h in range(heads):
                sl = slice(h * 64, (h + 1) * 64)
                vl = slice(half + h * 64, half + (h + 1) * 64)
                _, grad = pair_terms_kernel(
                    kv_scr[c, key, sl], kv_scr[c, key, vl], qt[sl, :], dot[sl, :],
                    stats[h : h + 1, :], stats[8 + h : 9 + h, :], ok,
                )
                dq_scr[sl, :] += dot_nn(kt[sl], grad)
    if last:
        dq_out[...] = (dq_scr[...] * 0.125).astype(BF).T
    else:
        dq_out[...] = dq_scr[...]


def back_dq_call(scal, qt, dot, stats, dq, seg_rows, kvs, tags, tag_ids, last, after=()):
    half, queries = qt.shape
    rows = queries // 2
    chips = len(kvs)
    state = tuple(held(a) for a in (qt, dot, stats, dq))
    out = sds((queries, half)) if last else near((half, queries), F32)
    return call(
        functools.partial(back_dq_kernel, chips, last),
        "back_dq",
        out,
        [whole(a.shape) for a in state] + [seg_spec(queries, 0)] + [far()] * chips
        + tag_specs(tag_ids, rows),
        whole(out.shape),
        (1,),
        [
            pltpu.VMEM((half, queries), F32),
            pltpu.VMEM((chips, queries, 2 * half), BF),
            pltpu.SemaphoreType.DMA((chips,)),
        ],
        1,
        state + (seg_rows,) + tuple(kvs) + (tags,) * (2 * chips),
        scal,
        after,
    )


def back_dkv_kernel(chips, last, s, *refs):
    refs = list(refs)
    w_out, kv, tag, dkv_in = (refs.pop(0) for _ in range(4))
    exts = [refs.pop(0) for _ in range(2 * chips)]
    qs = [refs.pop(0) for _ in range(chips)]
    segs = [refs.pop(0) for _ in range(chips)]
    if last:
        out_m, out_r = refs.pop(0), refs.pop(0)
    else:
        dkv_out = refs.pop(0)
    dkv, q_scr, turned_scr, sems = refs
    copies = fetch([(qs[c], q_scr.at[c]) for c in range(chips)], sems)
    core = s[0] % 2
    rows = exts[0].shape[0]
    half, width = w_out.shape
    heads = half // 64
    queries = 2 * rows
    dkv[...] = dkv_in[...]
    for c in range(chips):
        do, dot, lse, corr = back_queries(
            core, exts[2 * c], exts[2 * c + 1], w_out[...], turned_scr
        )
        copies[c].wait()
        q = q_scr[c]
        qt = q.T
        seg = segs[c][...]
        for b in range(2):
            key = slice(b * rows, (b + 1) * rows)
            ok = mask_of(tag[b], seg)
            for h in range(heads):
                sl = slice(h * 64, (h + 1) * 64)
                vl = slice(half + h * 64, half + (h + 1) * 64)
                probs, grad = pair_terms_kernel(
                    kv[key, sl], kv[key, vl], qt[sl], dot[sl], lse[h : h + 1], corr[h : h + 1], ok
                )
                dkv[key, sl] += dot_nn(grad, q[:, sl])
                dkv[key, vl] += dot_nn(probs, do[:, sl])
    if last:
        out_m[...] = dkv[:rows, :].astype(BF)
        out_r[...] = dkv[rows:, :].astype(BF)
    else:
        dkv_out[...] = dkv[...]


def back_dkv_call(scal, w_out, kv, tag, dkv, exts, qs, seg_rows, seg_ids, last, after=()):
    queries, width = kv.shape
    rows, half = queries // 2, width // 2
    chips = len(qs)
    state = tuple(held(a) for a in (w_out, kv, tag, dkv))
    flat = sds((rows, width))
    out_shape = (flat, flat) if last else (near((queries, width), F32),)
    return call(
        functools.partial(back_dkv_kernel, chips, last),
        "back_dkv",
        out_shape,
        [whole(a.shape) for a in state] + [whole(e.shape) for e in exts] + [far()] * chips
        + [seg_spec(queries, at) for at in seg_ids],
        tuple(whole(o.shape) for o in out_shape),
        (1,),
        [
            pltpu.VMEM((queries, width), F32),
            pltpu.VMEM((chips, queries, half), BF),
            pltpu.VMEM((128, queries), F32),
            pltpu.SemaphoreType.DMA((chips,)),
        ],
        1,
        state + tuple(exts) + tuple(qs) + (seg_rows,) * chips,
        scal,
        after,
    )


def normalize(hidden):
    center = hidden - jnp.mean(hidden, axis=-1, keepdims=True)
    spread = lax.rsqrt(jnp.mean(center * center, axis=-1, keepdims=True) + 1e-05)
    return center * spread, spread


def normalize_back(grad, unit, spread, gain):
    scaled = grad * gain
    mean = jnp.mean(scaled, axis=-1, keepdims=True)
    along = jnp.mean(scaled * unit, axis=-1, keepdims=True)
    return spread * (scaled - mean - unit * along)


def gauss(up):
    size = jnp.abs(up)
    bell = jnp.exp(-0.5 * up * up)
    t = 1.0 / (1.0 + 0.23164189 * size)
    poly = 0.5307027145 * t - 0.7265760135
    poly = poly * t + 0.7107068705
    poly = poly * t - 0.142248368
    poly = poly * t + 0.127414796
    tail = poly * t * bell
    return jnp.where(up < 0, tail, 1.0 - tail), bell


def ffn_kernel(
    layer, s, x, att, oatt, b_out, gain, shift, b_up, b_down, w_out, w_up, w_down,
    unit1, rs1, normed, act, slope, unit2, rs2, y, kept_scr, unit_scr, kept_sems, out_scr,
    up_scr, down_scr, sems,
):
    rows, width = x.shape
    half = width // 2
    core = s[0] % 2
    steps = up_scr.shape[0]
    pairs = [(w_out.at[layer], out_scr)]
    for n in range(steps):
        strip = pl.ds(n * width, width)
        pairs += [(w_up.at[layer, :, strip], up_scr.at[n]), (w_down.at[layer, strip], down_scr.at[n])]
    copies = fetch(pairs, sems)
    copies[0].wait()
    mine = pl.multiple_of(core * half, 128)
    other = pl.multiple_of((1 - core) * half, 128)
    branch = dot_nn(att[:rows, :half], out_scr[pl.ds(mine, half), :])
    branch = branch + dot_nn(oatt[rows:, :half], out_scr[pl.ds(other, half), :])
    first = x[...].astype(F32) + branch + b_out[layer : layer + 1, :]
    unit, spread = normalize(first)
    unit_scr[0] = unit
    leaving = [pltpu.make_async_copy(unit_scr.at[0], unit1, kept_sems.at[2 * steps])]
    leaving[0].start()
    rs1[...] = jnp.broadcast_to(spread, rs1.shape)
    low = (unit * gain[layer, 0:1, :] + shift[layer, 0:1, :]).astype(BF)
    normed[...] = low
    total = low.astype(F32) + b_down[layer : layer + 1, :]
    copies[1].wait()
    following = dot_nn(low, up_scr[0])
    for n in range(steps):
        strip = slice(n * width, (n + 1) * width)
        up = following + b_up[layer : layer + 1, strip]
        copies[2 + 2 * n].wait()
        if n + 1 < steps:
            copies[3 + 2 * n].wait()
            following = dot_nn(normed[...], up_scr[n + 1])
        phi, bell = gauss(up)
        low = (up * phi).astype(BF)
        kept_scr[0, :, strip] = low
        kept_scr[1, :, strip] = (phi + up * (0.3989422804014327 * bell)).astype(BF)
        for i, ref in enumerate((act, slope)):
            copy = pltpu.make_async_copy(
                kept_scr.at[i, :, strip], ref.at[:, strip], kept_sems.at[2 * n + i]
            )
            copy.start()
            leaving.append(copy)
        total = total + dot_nn(low, down_scr[n])
    unit, spread = normalize(total)
    unit_scr[1] = unit
    leaving.append(pltpu.make_async_copy(unit_scr.at[1], unit2, kept_sems.at[2 * steps + 1]))
    leaving[-1].start()
    rs2[...] = jnp.broadcast_to(spread, rs2.shape)
    y[...] = (unit * gain[layer, 1:2, :] + shift[layer, 1:2, :]).astype(BF)
    for copy in leaving:
        copy.wait()


def ffn_call(
    layer, scal, x, att, oatt, w_out, b_out, gain, shift, w_up, b_up, w_down, b_down, after=()
):
    rows, width = x.shape
    wide = w_up.shape[2]
    steps = wide // width
    vec = sds((rows, 128), F32)
    out_shape = (
        kept((rows, width), F32), vec, sds((rows, width)), kept((rows, wide)), kept((rows, wide)),
        kept((rows, width), F32), vec, sds((rows, width)),
    )
    out_specs = [whole(o.shape) for o in out_shape]
    for i in (0, 3, 4, 5):
        out_specs[i] = far()
    arrays = (x, att, oatt, b_out, gain, shift, b_up, b_down)
    return call(
        functools.partial(ffn_kernel, layer),
        "ffn",
        out_shape,
        [whole(a.shape) for a in arrays] + [far()] * 3,
        tuple(out_specs),
        (1,),
        [
            pltpu.VMEM((2, rows, wide), BF),
            pltpu.VMEM((2, rows, width), F32),
            pltpu.SemaphoreType.DMA((2 * steps + 2,)),
            pltpu.VMEM((width, width), BF),
            pltpu.VMEM((steps, width, width), BF),
            pltpu.VMEM((steps, width, width), BF),
            pltpu.SemaphoreType.DMA((1 + 2 * steps,)),
        ],
        4 * rows * width * wide + 2 * rows * width * width,
        arrays + (w_out, w_up, w_down),
        scal,
        after,
    )


def ffn_back_kernel(
    layer, s, gy, unit2, rs2, slope, unit1, rs1, gain, att, oatt, w_up, w_down, w_out,
    d_down, d_up, d_up_more, d_branch, d_first, sums, up_scr, down_scr, out_scr, sems,
):
    steps = up_scr.shape[0]
    rows, width = gy.shape
    half = width // 2
    core = s[0] % 2
    pairs = []
    for n in range(steps):
        strip = pl.ds(n * width, width)
        pairs += [(w_down.at[layer, strip], down_scr.at[n]), (w_up.at[layer, :, strip], up_scr.at[n])]
    pairs.append((w_out.at[layer], out_scr))
    copies = fetch(pairs, sems)
    grad = gy[...].astype(F32)
    unit = unit2[...]
    total = normalize_back(grad, unit, rs2[:, 0:1], gain[layer, 1:2, :])
    sums[...] = jnp.zeros_like(sums)
    sums[1:2, :] = jnp.sum(grad * unit, axis=0, keepdims=True)
    sums[3:4, :] = jnp.sum(grad, axis=0, keepdims=True)
    low = total.astype(BF)
    d_down[...] = low
    sums[5:6, :] = jnp.sum(low.astype(F32), axis=0, keepdims=True)
    copies[0].wait()
    following = dot_nt(low, down_scr[0])
    for n in range(steps):
        strip = slice(n * width, (n + 1) * width)
        low = (following * slope[:, strip].astype(F32)).astype(BF)
        copies[2 * n + 1].wait()
        if n + 1 < steps:
            copies[2 * n + 2].wait()
            following = dot_nt(d_down[...], down_scr[n + 1])
        ref, at = (d_up, n) if n < steps // 2 else (d_up_more, n - steps // 2)
        ref[:, at * width : (at + 1) * width] = low
        sums[6 + n : 7 + n, :] = jnp.sum(low.astype(F32), axis=0, keepdims=True)
        total = total + dot_nt(low, up_scr[n])
    unit = unit1[...]
    first = normalize_back(total, unit, rs1[:, 0:1], gain[layer, 0:1, :])
    sums[0:1, :] = jnp.sum(total * unit, axis=0, keepdims=True)
    sums[2:3, :] = jnp.sum(total, axis=0, keepdims=True)
    d_first[...] = first
    low = first.astype(BF)
    d_branch[:, :width] = low
    sums[4:5, :] = jnp.sum(low.astype(F32), axis=0, keepdims=True)
    copies[-1].wait()
    row = lax.broadcasted_iota(jnp.int32, (128, 128), 0)
    column = lax.broadcasted_iota(jnp.int32, (128, 128), 1)
    heads = half // 64
    stats = jnp.zeros((rows, 128), F32)
    tall = lax.broadcasted_iota(jnp.int32, (half, 128), 0)
    wide = lax.broadcasted_iota(jnp.int32, (half, 128), 1)
    for at, part in ((core, att[:rows]), (1 - core, oatt[rows:])):
        move = (row < 2 * heads) & (column == at * 64 + row)
        stats = stats + dot_nn(part[:, half:], jnp.where(move, 1.0, 0.0).astype(BF))
        grad = dot_nt(low, out_scr[pl.ds(pl.multiple_of(at * half, 128), half), :])
        product = grad.astype(BF).astype(F32) * part[:, :half].astype(F32)
        place = wide - at * 64 - 2 * heads
        pick = (place == tall // 64) | (place == tall // 64 + heads)
        stats = stats + lax.dot_general(
            product, jnp.where(pick, 1.0, 0.0), (((1,), (0,)), ((), ())),
            precision=lax.Precision.HIGHEST, preferred_element_type=F32,
        )
    top = stats.astype(BF)
    lane = lax.broadcasted_iota(jnp.int32, (rows, 128), 1) % 64
    under = (lane >= 3 * heads) & (lane < 4 * heads)
    d_branch[:, width:] = jnp.where(under, stats - top.astype(F32), stats).astype(BF)


def ffn_back_call(
    layer, scal, gy, unit2, rs2, slope, unit1, rs1, gain, att, oatt, w_up, w_down, w_out, after=()
):
    rows, width = gy.shape
    wide = w_up.shape[2]
    steps = wide // width
    out_shape = (
        sds((rows, width)), sds((rows, wide // 2)), sds((rows, wide // 2)),
        sds((rows, width + 128)), sds((rows, width), F32),
        sds((16, width), F32),
    )
    arrays = (gy, unit2, rs2, slope, unit1, rs1, gain, att, oatt)
    return call(
        functools.partial(ffn_back_kernel, layer),
        "ffn_back",
        out_shape,
        [whole(a.shape) for a in arrays] + [far()] * 3,
        tuple(whole(o.shape) for o in out_shape),
        (1,),
        [
            pltpu.VMEM((steps, width, width), BF),
            pltpu.VMEM((steps, width, width), BF),
            pltpu.VMEM((width, width), BF),
            pltpu.SemaphoreType.DMA((2 * steps + 1,)),
        ],
        1,
        arrays + (w_up, w_down, w_out),
        scal,
        after,
    )


def input_back_kernel(layer, s, d_first, dq, dkv, odq, odkv, w, gx, w_scr, sems):
    rows, width = d_first.shape
    half = width // 2
    core = s[0] % 2
    steps = w_scr.shape[0]
    tall = width // steps
    copies = fetch([(w.at[layer, pl.ds(n * tall, tall)], w_scr.at[n]) for n in range(steps)], sems)
    for n in range(steps):
        copies[n].wait()
        strip = slice(n * tall, (n + 1) * tall)
        result = d_first[:, strip]
        for at, q_part, kv_part in (
            (core * half, dq[:rows], dkv),
            ((1 - core) * half, odq[rows:], odkv),
        ):
            for i, part in enumerate((q_part, kv_part[:, :half], kv_part[:, half:])):
                columns = pl.ds(pl.multiple_of(i * width + at, 128), half)
                result = result + dot_nt(part, w_scr[n, :, columns])
        gx[:, strip] = result


def input_back_call(layer, scal, d_first, dq, dkv, odq, odkv, w_qkv, after=()):
    rows, width = d_first.shape
    arrays = (d_first, dq, dkv, odq, odkv)
    return call(
        functools.partial(input_back_kernel, layer),
        "input_back",
        sds((rows, width), F32),
        [whole(a.shape) for a in arrays] + [far()],
        whole((rows, width)),
        (1,),
        [pltpu.VMEM((3, width // 3, 3 * width), BF), pltpu.SemaphoreType.DMA((3,))],
        1,
        arrays + (w_qkv,),
        scal,
        after,
    )


def gather_rows(s, turned, picked, order):
    chip, core = s[0] // 2, s[0] % 2
    share = picked.shape[0] // 4
    for at in range(4):
        place = at if order is None else chip ^ order[at]
        begin = pl.multiple_of(place * (2 * share) + core * share, 32)
        picked[at * share : (at + 1) * share, :] = turned[pl.ds(begin, share), :]


def up_grad_kernel(s, x_m, x_o, *refs):
    keep, send, turned, picked = refs[-4:]
    rows, width = x_m.shape
    turned[:, :rows] = x_m[...].T
    turned[:, rows:] = x_o[...].T
    gather_rows(s, turned, picked, (0, 2, 1, 3))
    share = picked.shape[0] // 4
    steps = keep.shape[1] // share
    for n in range(steps):
        g_m, g_o = refs[:2] if n < steps // 2 else refs[2:4]
        at = n % (steps // 2)
        strip = slice(at * width, (at + 1) * width)
        grad = dot_nn(picked[:, :rows], g_m[:, strip]) + dot_nn(picked[:, rows:], g_o[:, strip])
        for at in range(2):
            place = slice(n * share, (n + 1) * share)
            keep[at, place, :] = grad[at * share : (at + 1) * share].astype(BF)
            send[at, place, :] = grad[(2 + at) * share : (3 + at) * share].astype(BF)


def up_grad_call(scal, *args, after=()):
    rows, width = args[0].shape
    out = sds((2, args[2].shape[1] // 4, width))
    return call(
        up_grad_kernel,
        "up_grad",
        (out, out),
        [whole(a.shape) for a in args],
        (whole(out.shape),) * 2,
        (1,),
        [pltpu.VMEM((width, 2 * rows), BF), pltpu.VMEM((width // 2, 2 * rows), BF)],
        1,
        args,
        scal,
        after,
    )


def down_grad_kernel(s, a_m, a_o, g_m, g_o, keep, send):
    n = pl.program_id(0)
    grad = dot_nn(a_m[...].T, g_m[...]) + dot_nn(a_o[...].T, g_o[...])
    grad = grad.astype(BF)

    @pl.when(n < 2)
    def _():
        keep[...] = grad

    @pl.when(n >= 2)
    def _():
        send[...] = grad


def down_grad_call(scal, a_m, a_o, g_m, g_o, after=()):
    rows, wide = a_m.shape
    width = g_m.shape[1]
    share = wide // 8
    strip = whole((rows, width))
    out = sds((2, share, width))
    picked = pl.BlockSpec((rows, share), lambda n, s: (0, 2 * ((s[0] // 2) ^ n) + s[0] % 2))
    return call(
        down_grad_kernel,
        "down_grad",
        (out, out),
        [picked, picked, strip, strip],
        (
            pl.BlockSpec((None, share, width), lambda n, s: (jnp.minimum(n, 1), 0, 0)),
            pl.BlockSpec((None, share, width), lambda n, s: (jnp.maximum(n - 2, 0), 0, 0)),
        ),
        (4,),
        [],
        1,
        (a_m, a_o, g_m, g_o),
        scal,
        after,
    )


def out_grad_kernel(joined, s, x_m, x_o, dq, dkv_m, dkv_r, odq, odkv_m, odkv_r, att, oatt, b_m, b_o,
    sums_m, sums_o, *refs,
):
    turned, picked = refs[-2:]
    keep_a, send_a, keep_b, send_b = refs[-6:-2]
    if joined:
        first_a, second_a, first_b, second_b = refs[:4]
        rows_in = first_a.shape[1]
        rows_out = keep_a.shape[1]
        send_b[:rows_in, :] = (first_a[1].astype(F32) + second_a[1].astype(F32)).astype(BF)
        send_a[:rows_in, :] = (first_b[1].astype(F32) + second_b[1].astype(F32)).astype(BF)
        sent_a, sent_b = (
            [ref.at[pl.ds(rows_in + at * rows_out, rows_out)] for at in range(2)]
            for ref in (send_a, send_b)
        )
    else:
        sent_a, sent_b = ([ref.at[at] for at in range(2)] for ref in (send_a, send_b))
    places_a = [keep_a.at[0], keep_a.at[1], sent_a[0], sent_a[1]]
    places_b = [keep_b.at[0], sent_b[0], keep_b.at[1], sent_b[1]]
    skip = 0
    rows, width = x_m.shape
    half = width // 2
    core = s[0] % 2
    share = width // 8
    mine = pl.ds(pl.multiple_of(core * half, 128), half)
    other = pl.ds(pl.multiple_of((1 - core) * half, 128), half)
    turned[:, :rows] = x_m[...].T
    turned[:, rows:] = x_o[...].T
    order = (0, 2, 1, 3)
    gather_rows(s, turned, picked, order)
    left_m, left_o = picked[:, :rows], picked[:, rows:]

    def put(places, begin, grad, columns):
        for at in range(4):
            part = grad[at * share : (at + 1) * share].astype(BF)
            places[at][begin : begin + share, columns] = part

    for at, places, begin in ((0, places_a, 0), (1, places_a, share), (2, places_b, skip)):
        if at == 0:
            pairs = ((dq[:rows], dq[rows:]), (odq[rows:], odq[:rows]))
        else:
            cut = slice((at - 1) * half, at * half)
            pairs = ((dkv_m[:, cut], dkv_r[:, cut]), (odkv_r[:, cut], odkv_m[:, cut]))
        for columns, (mine_rows, other_rows) in zip((mine, other), pairs):
            grad = dot_nn(left_m, mine_rows) + dot_nn(left_o, other_rows)
            put(places, begin, grad, columns)
    turned[mine, :] = att[:, :half].T
    turned[other, :rows] = oatt[rows:, :half].T
    turned[other, rows:] = oatt[:rows, :half].T
    gather_rows(s, turned, picked, order)
    grad = dot_nn(picked[:, :rows], b_m[:, :width])
    grad = grad + dot_nn(picked[:, rows:], b_o[:, :width])
    put(places_b, skip + share, grad, slice(0, width))
    small = (sums_m[...] + sums_o[...]).astype(BF)
    begin = skip + 2 * share
    ends = places_a + places_b
    for ref in ends:
        ref[begin:, :] = small
    value = [ref[:, half:] for ref in (dkv_m, dkv_r, odkv_m, odkv_r)]
    for row, parts in ((10, (dq[...], odq[...])), (11, value)):
        count = len(parts) // 2
        for columns, group in ((mine, parts[:count]), (other, parts[count:])):
            line = sum(jnp.sum(p.astype(F32), axis=0, keepdims=True) for p in group).astype(BF)
            for ref in ends:
                ref[begin + row : begin + row + 1, columns] = line


def out_grad_call(scal, *args, joined=(), after=()):
    rows, width = args[0].shape
    share = 2 * (width // 8) + 16
    keep = sds((2, share, width))
    send = sds((joined[0].shape[1] + 2 * share, width)) if joined else keep
    args += tuple(joined)
    return call(
        functools.partial(out_grad_kernel, bool(joined)),
        "out_grad",
        (keep, send, keep, send),
        [whole(a.shape) for a in args],
        (whole(keep.shape), whole(send.shape)) * 2,
        (1,),
        [pltpu.VMEM((width, 2 * rows), BF), pltpu.VMEM((width // 2, 2 * rows), BF)],
        1,
        args,
        scal,
        after,
    )


def over_core(array):
    return lax.ppermute(array, "seq", [(i, i ^ 1) for i in range(8)])


def over_x(array):
    return lax.ppermute(array, "seq", [(i, i ^ 2) for i in range(8)])


def over_y(array):
    return lax.ppermute(array, "seq", [(i, i ^ 4) for i in range(8)])


def over_bucket(array, pairs):
    return lax.ppermute(array, "bucket", pairs)


def view(ref, cut):
    if cut is None:
        return ref[...]
    return ref[cut] if isinstance(cut, int) else ref[cut[0] : cut[0] + cut[1], :]


def parted(parts):
    arrays = tuple(p[0] if isinstance(p, tuple) else p for p in parts)
    cuts = tuple(p[1] if isinstance(p, tuple) else None for p in parts)
    return arrays, cuts


def sum_kernel(cuts, s, *refs):
    total = sum(view(ref, cut).astype(F32) for ref, cut in zip(refs, cuts))
    refs[-1][...] = total.astype(BF)


def sum_call(scal, parts, shape, after=()):
    arrays, cuts = parted(parts)
    return call(
        functools.partial(sum_kernel, cuts), "sum", sds(shape), [whole(a.shape) for a in arrays],
        whole(shape), (1,), [], 1, arrays, scal, after,
    )


def sort_kernel(cuts, s, *refs):
    mine, other = refs[-2:]
    halves = [list(zip(refs[at : at + 3], cuts[at : at + 3])) for at in (0, 3)]
    outer = (s[0] == 0) | (s[0] == 3)

    def write(first, second):
        for out, half in ((mine, halves[first]), (other, halves[second])):
            out[...] = sum(view(ref, cut).astype(F32) for ref, cut in half).astype(BF)

    @pl.when(outer)
    def _():
        write(0, 1)

    @pl.when(jnp.logical_not(outer))
    def _():
        write(1, 0)


def bucket_start(zscal, keep_a, keep_b, got_a, got_b, pass_a, pass_b, after, pinned=False):
    parts = [first_of(keep_a), first_of(got_a), pass_a, first_of(keep_b), first_of(got_b), pass_b]
    arrays, cuts = parted(parts)
    shape = keep_a.shape[1:]
    specs = [whole(a.shape) for a in arrays]
    if pinned:
        top = pl.BlockSpec((None,) + shape, lambda i, s: (0, 0, 0))
        specs = [top if cut == 0 else spec for spec, cut in zip(specs, cuts)]
        arrays = tuple(stored(a) if cut == 0 else a for a, cut in zip(arrays, cuts))
        cuts = tuple(None if cut == 0 else cut for cut in cuts)
    mine, other = call(
        functools.partial(sort_kernel, cuts), "sort", (sds(shape),) * 2,
        specs, (whole(shape),) * 2, (1,), [], 1, arrays, zscal, after,
    )
    return mine, over_bucket(other, NEAR)


def first_of(stack):
    return stack[0] if isinstance(stack, tuple) else (stack, 0)


def second_of(stack):
    return stack[1] if isinstance(stack, tuple) else (stack, 1)


def bucket_middle(scal, mine, got, after):
    mine = sum_call(scal, (mine, got), mine.shape, after)
    return mine, over_bucket(mine, FAR)


def bucket_last(scal, mine, got, after):
    mine = sum_call(scal, (mine, got), mine.shape, after)
    return mine, over_bucket(mine, NEAR)


def bucket_end(mine, other):
    place = lax.axis_index("bucket")
    outer = (place == 0) | (place == 3)
    return jnp.where(outer, mine, other), jnp.where(outer, other, mine)


def phase_one(keep_a, send_a, keep_b, send_b):
    return keep_a, keep_b, over_x(send_a), over_y(send_b)


def phase_two(scal, keep_a, keep_b, got_a, got_b, after):
    shape = keep_a.shape[1:]
    pass_a = sum_call(scal, (second_of(keep_a), second_of(got_a)), shape, after)
    pass_b = sum_call(scal, (second_of(keep_b), second_of(got_b)), shape, (pass_a,))
    return keep_a, keep_b, got_a, got_b, over_y(pass_a), over_x(pass_b), (pass_b,)


def fast_local(
    frames, w_qkv, b_qv, w_out, b_out, ln_gain, ln_shift, w_up, b_up, w_down, b_down,
    cotangent, clip_lengths, valid_lengths,
):
    rows, width = frames.shape[1:]
    place = lax.axis_index("seq")
    scal = place.astype(jnp.int32)[None]
    zscal = lax.axis_index("bucket").astype(jnp.int32)[None]
    blocks = place ^ jnp.arange(8, dtype=jnp.int32)
    position = (blocks[:, None] * rows + jnp.arange(rows, dtype=jnp.int32)[None]).reshape(-1)
    ends = jnp.cumsum(clip_lengths[0])
    starts = ends - clip_lengths[0]
    inside = (position[:, None] >= starts) & (position[:, None] < ends)
    segment = jnp.sum(jnp.where(inside, jnp.arange(ends.shape[0], dtype=jnp.int32), 0), axis=1)
    live = jnp.any(inside & (position[:, None] < starts + valid_lengths[0]), axis=1)
    tags = jnp.where(live, segment, -1).reshape(8, rows, 1)
    tags = jnp.broadcast_to(tags, (8, rows, 128))
    seg_rows = segment[None]
    seg_row = seg_rows[:, : 2 * rows]

    x = frames[0]
    saved = []
    before = ()
    for layer in range(LAYERS):
        attend = functools.partial(attend_call, layer, scal)
        x_r, x_x, x_y = over_core(x), over_x(x), over_y(x)
        kv, q, qt, w_all, acc, top = attend((), seg_row, w_qkv, b_qv, (x, x_r), tags, (0, 1))
        x_x, x_y = gate((x_x, x_y), (top,))
        x_d = over_y(x_x)
        x_xr, x_yr = over_core(x_x), over_core(x_y)
        kv_x, kv_y, q_x, q_y, acc, top = attend(
            (qt, w_all, acc, top), seg_row, w_qkv, b_qv, (x_x, x_xr, x_y, x_yr), tags,
            (2, 3, 4, 5), after=before,
        )
        (x_d,) = gate((x_d,), (top,))
        x_dr = over_core(x_d)
        kv_d, q_d, att = attend(
            (qt, w_all, acc, top), seg_row, w_qkv, b_qv, (x_d, x_dr), tags, (6, 7), last=True
        )
        oatt = over_core(att)
        unit1, rs1, normed, act, slope, unit2, rs2, y = ffn_call(
            layer, scal, x, att, oatt, w_out, b_out, ln_gain, ln_shift, w_up, b_up, w_down, b_down
        )
        before = (over_core(normed), over_core(act))
        saved.append(
            (x, x_r, q, q_x, q_y, q_d, kv, kv_x, kv_y, kv_d, att, oatt)
            + (unit1, rs1, normed, act, slope, unit2, rs2) + before
        )
        x = y
    activations = x[None]

    grad = cotangent[0]
    done = ()
    for layer in reversed(range(LAYERS)):
        top_layer = layer == LAYERS - 1
        x, x_r, q, q_x, q_y, q_d, kv, kv_x, kv_y, kv_d, att, oatt = saved[layer][:12]
        unit1, rs1, normed, act, slope, unit2, rs2, o_normed, o_act = saved[layer][12:]
        normed, act, o_normed, o_act = (stored(a) for a in (normed, act, o_normed, o_act))
        slope, unit1, unit2 = (stored(a) for a in (slope, unit1, unit2))
        d_down, d_up, d_up_more, ext, d_first, sums = ffn_back_call(
            layer, scal, grad, unit2, rs2, slope, unit1, rs1, ln_gain, att, oatt, w_up, w_down,
            w_out, done
        )
        ext_r, ext_x, ext_y = over_core(ext), over_x(ext), over_y(ext)
        o_up, o_down = over_core(d_up), over_core(d_down)
        done = before if top_layer else ()
        if not top_layer:
            done = ()
        w_mine, qt, dot, stats, dq, dkv, kv_near, tag_near = back_own_call(
            layer, scal, ext, ext_r, q, seg_rows, kv, tags, w_out, after=done
        )
        if not top_layer:
            (d_up_more,) = gate((d_up_more,), (dkv,))
        o_more = over_core(d_up_more)
        done = (dkv,)
        if not top_layer:
            early = bucket_start(zscal, *late[:-1], (dkv,), pinned=True)
            middle = phase_two(scal, *middle, early[:1])
            done = middle[-1]
        dq = back_dq_call(
            scal, qt, dot, stats, dq, seg_rows, (kv_x,), tags, (2, 3), False, after=done
        )
        ext_x, ext_y = gate((ext_x, ext_y), (dq,))
        ext_d = over_y(ext_x)
        ext_xr, ext_yr = over_core(ext_x), over_core(ext_y)
        keep_a, send_a = up_grad_call(
            scal, normed, o_normed, d_up, o_up, d_up_more, o_more, after=(ext_xr, ext_yr)
        )
        done = (keep_a,)
        if not top_layer:
            middle = bucket_start(zscal, *middle[:-1], done)
            done = middle[:1]
        keep_b, send_b = down_grad_call(scal, act, o_act, d_down, o_down, after=done)
        done = (keep_b,)
        if not top_layer:
            early = bucket_middle(scal, *early, done)
            done = early[:1]
        late = phase_one(keep_a, send_a, keep_b, send_b)
        dq = back_dq_call(
            scal, qt, dot, stats, dq, seg_rows, (kv_y, kv_d), tags, (4, 5, 6, 7), True, after=done
        )
        done = (dq,)
        odq = over_core(dq)
        (dkv,) = back_dkv_call(
            scal, w_mine, kv_near, tag_near, dkv, (ext_x, ext_xr, ext_y, ext_yr), (q_x, q_y),
            seg_rows, (1, 2), False, after=done
        )
        (ext_d,) = gate((ext_d,), (dkv,))
        ext_dr = over_core(ext_d)
        done = ()
        if not top_layer:
            middle = bucket_middle(scal, *middle, (dkv,))
            done = middle[:1]
        (sums,) = gate((sums,), (dkv,))
        o_sums = over_core(sums)
        g_m, g_r = back_dkv_call(
            scal, w_mine, kv_near, tag_near, dkv, (ext_d, ext_dr), (q_d,), seg_rows, (3,), True,
            after=done,
        )
        o_m, o_r = over_core(g_m), over_core(g_r)
        done = (g_m,)
        if not top_layer:
            early = bucket_last(scal, *early, done)
            done = early[:1]
        out_args = (
            stored(x), stored(x_r), dq, g_m, g_r, odq, o_m, o_r, stored(att), stored(oatt),
            stored(ext), stored(ext_r), sums, o_sums,
        )
        if top_layer:
            keep_a, keep_b, got_a, got_b = late
            middle_a, sent_x, middle_b, sent_y = out_grad_call(
                scal, *out_args, joined=(keep_a, got_a, keep_b, got_b), after=(o_m,)
            )
            got_x, got_y = over_x(sent_x), over_y(sent_y)
            first, more = keep_a.shape[1], middle_a.shape[1]
            late += ((got_y, (0, first)), (got_x, (0, first)), ())
            middle = (middle_a, middle_b) + tuple(
                ((got, (first, more)), (got, (first + more, more))) for got in (got_x, got_y)
            )
            done = (middle_a,)
        grad = input_back_call(layer, scal, d_first, dq, g_m, odq, o_r, w_qkv, after=(o_m,) + done)
        done = (grad,)
    late = phase_two(scal, *late, done)
    middle = bucket_last(scal, *middle, late[-1])
    parts = out_grad_call(scal, *out_args, after=middle[:1] + early[1:])
    last = phase_one(*parts)
    late = bucket_start(zscal, *late[:-1], parts[:1])
    last = phase_two(scal, *last, late[:1] + middle[1:])
    late = bucket_middle(scal, *late, last[-1])
    last = bucket_start(zscal, *last[:-1], late[:1])
    last = bucket_middle(scal, *last, last[:1])
    late = bucket_last(scal, *late, last[:1])
    last = bucket_last(scal, *last, late[:1])
    ffn_1, att_1, ffn_0, att_0 = (bucket_end(*pair) for pair in (early, middle, late, last))
    ffn_parts = (ffn_0, ffn_1)
    att_parts = (att_0, att_1)

    share = width // 8

    def both(make):
        return jnp.stack([make(layer).astype(F32) for layer in range(LAYERS)])

    small = both(lambda l: att_parts[l][0][2 * share :])

    def own(array, axis):
        size = array.shape[axis] // 8
        return lax.dynamic_slice_in_dim(array, place * size, size, axis)

    def beside(array):
        parts = array.shape[0] // share
        return array.reshape(parts, share, width).transpose(1, 0, 2).reshape(share, -1)

    return (
        activations,
        grad[None],
        both(
            lambda l: jnp.concatenate(
                [beside(att_parts[l][0][: 2 * share]), att_parts[l][1][:share]], axis=1
            )
        ),
        own(small[:, 10:12].reshape(LAYERS, -1), 1),
        both(lambda l: att_parts[l][1][share : 2 * share]),
        own(small[:, 4], 1),
        own(small[:, 0:2], 2),
        own(small[:, 2:4], 2),
        both(lambda l: beside(ffn_parts[l][0])),
        own(small[:, 6:10].reshape(LAYERS, -1), 1),
        both(lambda l: ffn_parts[l][1]),
        own(small[:, 5], 1),
    )


def clip_tags(lengths, valid, begin, count):
    position = begin + jnp.arange(count, dtype=jnp.int32)
    ends = jnp.cumsum(lengths)
    starts = ends - lengths
    inside = (position[:, None] >= starts[None, :]) & (position[:, None] < ends[None, :])
    labels = jnp.arange(lengths.shape[0], dtype=jnp.int32)
    segment = jnp.sum(jnp.where(inside, labels[None, :], 0), axis=1)
    live = jnp.any(inside & (position[:, None] < (starts + valid)[None, :]), axis=1)
    return (segment, jnp.where(live, segment, -1))


def layer_norm(hidden, gain, shift):
    center = hidden - jnp.mean(hidden, axis=-1, keepdims=True)
    spread = jnp.mean(center * center, axis=-1, keepdims=True)
    return center * lax.rsqrt(spread + 1e-05) * gain + shift


def exact_gelu(hidden):
    return jax.nn.gelu(hidden, approximate=False)


def split_heads(matrix):
    return matrix.reshape(matrix.shape[0], HEADS, -1)


def pair_terms(
    query_heads,
    grad_heads,
    log_total,
    correction,
    query_seg,
    key_heads,
    value_heads,
    key_tag,
    scale,
):
    scores = (
        jnp.einsum("qhd,khd->hqk", query_heads, key_heads, preferred_element_type=jnp.float32)
        * scale
    )
    allowed = (query_seg[:, None] == key_tag[None, :])[None]
    scores = jnp.where(allowed, scores, -1e30)
    probs = jnp.where(allowed, jnp.exp(scores - log_total[..., None]), 0.0)
    grad_probs = jnp.einsum(
        "qhd,khd->hqk", grad_heads, value_heads, preferred_element_type=jnp.float32
    )
    grad_scores = (probs * (grad_probs - correction[..., None])).astype(jnp.bfloat16)
    return (probs.astype(jnp.bfloat16), grad_scores)


def forward_layer(hidden, weights, query_seg, lengths, valid):
    w_qkv, b_qv, w_out, b_out, gain, shift, w_up, b_up, w_down, b_down = weights
    rows, width = hidden.shape
    scale = (width // HEADS) ** (-0.5)
    inputs = hidden.astype(jnp.bfloat16)
    projected = jnp.dot(inputs, w_qkv, preferred_element_type=jnp.float32)
    queries = (projected[:, :width] + b_qv[:width]).astype(jnp.bfloat16)
    keys = projected[:, width : 2 * width].astype(jnp.bfloat16)
    values = (projected[:, 2 * width :] + b_qv[width:]).astype(jnp.bfloat16)
    query_heads = split_heads(queries)
    initial = (
        jnp.full((HEADS, rows), -1e30, jnp.float32),
        jnp.zeros((HEADS, rows), jnp.float32),
        jnp.zeros((HEADS, rows, width // HEADS), jnp.float32),
    )
    key_piece = lax.all_gather(keys, "seq", axis=0, tiled=True)
    value_piece = lax.all_gather(values, "seq", axis=0, tiled=True)
    count = key_piece.shape[0] // rows
    key_blocks = key_piece.reshape(count, rows, HEADS, -1)
    value_blocks = value_piece.reshape(count, rows, HEADS, -1)

    def fold_inner(state, item):
        key_heads, value_heads, block_at = item
        _, block_tag = clip_tags(lengths, valid, block_at * rows, rows)
        running, denominator, weighted = state
        scores = (
            jnp.einsum("qhd,khd->hqk", query_heads, key_heads, preferred_element_type=jnp.float32)
            * scale
        )
        allowed = (query_seg[:, None] == block_tag[None, :])[None]
        scores = jnp.where(allowed, scores, -1e30)
        raised = jnp.maximum(running, jnp.max(scores, axis=-1))
        block_probs = jnp.where(allowed, jnp.exp(scores - raised[..., None]), 0.0)
        factor = jnp.exp(running - raised)
        denominator = denominator * factor + jnp.sum(block_probs, axis=-1)
        weighted = weighted * factor[..., None] + jnp.einsum(
            "hqk,khd->hqd",
            block_probs.astype(jnp.bfloat16),
            value_heads,
            preferred_element_type=jnp.float32,
        )
        return ((raised, denominator, weighted), None)

    state, _ = lax.scan(
        fold_inner, initial, (key_blocks, value_blocks, jnp.arange(count, dtype=jnp.int32))
    )
    running, denominator, weighted = state
    attended = (weighted / denominator[..., None]).transpose(1, 0, 2).reshape(rows, width)
    log_total = running + jnp.log(denominator)
    attended_low = attended.astype(jnp.bfloat16)
    branch = jnp.dot(attended_low, w_out, preferred_element_type=jnp.float32) + b_out
    first_sum = inputs.astype(jnp.float32) + branch
    normed = layer_norm(first_sum, gain[0], shift[0]).astype(jnp.bfloat16)
    up_pre = jnp.dot(normed, w_up, preferred_element_type=jnp.float32) + b_up
    activated = exact_gelu(up_pre).astype(jnp.bfloat16)
    second_sum = (
        normed.astype(jnp.float32)
        + jnp.dot(activated, w_down, preferred_element_type=jnp.float32)
        + b_down
    )
    output = layer_norm(second_sum, gain[1], shift[1])
    kept = (
        inputs,
        queries,
        keys,
        values,
        attended,
        attended_low,
        log_total,
        None,
        first_sum,
        normed,
        up_pre,
        activated,
        second_sum,
    )
    return (output, kept)


def attention_grads(kept, grad_att, query_seg, lengths, valid):
    (
        inputs,
        queries,
        keys,
        values,
        attended,
        attended_low,
        log_total,
        gathered,
        first_sum,
        normed,
        up_pre,
        activated,
        second_sum,
    ) = kept
    rows, width = queries.shape
    scale = (width // HEADS) ** (-0.5)
    query_heads = split_heads(queries)
    grad_heads = split_heads(grad_att)
    correction = jnp.sum(grad_heads.astype(jnp.float32) * split_heads(attended), axis=-1).T
    key_all, value_all = (
        lax.all_gather(keys, "seq", axis=0, tiled=True),
        lax.all_gather(values, "seq", axis=0, tiled=True),
    )
    count = key_all.shape[0] // rows
    key_blocks = key_all.reshape(count, rows, HEADS, -1)
    value_blocks = value_all.reshape(count, rows, HEADS, -1)
    block_ids = jnp.arange(count, dtype=jnp.int32)
    zero_heads = jnp.zeros((rows, HEADS, width // HEADS), jnp.float32)

    def attention_inner(acc, item):
        key_heads, value_heads, block_at = item
        _, block_tag = clip_tags(lengths, valid, block_at * rows, rows)
        probs, grad_scores = pair_terms(
            query_heads,
            grad_heads,
            log_total,
            correction,
            query_seg,
            key_heads,
            value_heads,
            block_tag,
            scale,
        )
        acc = (
            acc
            + jnp.einsum("hqk,khd->qhd", grad_scores, key_heads, preferred_element_type=jnp.float32)
            * scale
        )
        key_term = (
            jnp.einsum("hqk,qhd->khd", grad_scores, query_heads, preferred_element_type=jnp.float32)
            * scale
        )
        value_term = jnp.einsum(
            "hqk,qhd->khd", probs, grad_heads, preferred_element_type=jnp.float32
        )
        return (
            acc,
            jnp.concatenate(
                [key_term.reshape(rows, width), value_term.reshape(rows, width)], axis=1
            ),
        )

    grad_query, terms = lax.scan(attention_inner, zero_heads, (key_blocks, value_blocks, block_ids))
    summed = lax.psum_scatter(
        terms.reshape(count * rows, 2 * width).astype(jnp.bfloat16),
        "seq",
        scatter_dimension=0,
        tiled=True,
    ).astype(jnp.float32)
    grad_key = summed[:, :width]
    grad_value = summed[:, width:]
    return (grad_query.reshape(rows, width), grad_key, grad_value)


def backward_layer(grad_out, kept, weights, query_seg, lengths, valid):
    w_qkv, b_qv, w_out, b_out, gain, shift, w_up, b_up, w_down, b_down = weights
    (
        inputs,
        queries,
        keys,
        values,
        attended,
        attended_low,
        log_total,
        gathered,
        first_sum,
        normed,
        up_pre,
        activated,
        second_sum,
    ) = kept
    _, pull_second = jax.vjp(layer_norm, second_sum, gain[1], shift[1])
    grad_second, gain_second, shift_second = pull_second(grad_out)
    grad_down = grad_second.astype(jnp.bfloat16)
    sum_down = jnp.sum(grad_down, axis=0, dtype=jnp.float32)
    weight_down = jnp.einsum("rf,rd->fd", activated, grad_down, preferred_element_type=jnp.float32)
    grad_activated = jnp.einsum("rd,fd->rf", grad_down, w_down, preferred_element_type=jnp.float32)
    _, pull_gelu = jax.vjp(exact_gelu, up_pre)
    grad_up = pull_gelu(grad_activated)[0].astype(jnp.bfloat16)
    sum_up = jnp.sum(grad_up, axis=0, dtype=jnp.float32)
    weight_up = jnp.einsum("rd,rf->df", normed, grad_up, preferred_element_type=jnp.float32)
    grad_normed = grad_second + jnp.einsum(
        "rf,df->rd", grad_up, w_up, preferred_element_type=jnp.float32
    )
    _, pull_first = jax.vjp(layer_norm, first_sum, gain[0], shift[0])
    grad_first, gain_first, shift_first = pull_first(grad_normed)
    grad_branch = grad_first.astype(jnp.bfloat16)
    sum_out = jnp.sum(grad_branch, axis=0, dtype=jnp.float32)
    weight_out = jnp.einsum(
        "re,rd->ed", attended_low, grad_branch, preferred_element_type=jnp.float32
    )
    grad_att = jnp.einsum(
        "rd,ed->re", grad_branch, w_out, preferred_element_type=jnp.float32
    ).astype(jnp.bfloat16)
    grad_query, grad_key, grad_value = attention_grads(kept, grad_att, query_seg, lengths, valid)
    grad_proj = jnp.concatenate(
        [
            grad_query.astype(jnp.bfloat16),
            grad_key.astype(jnp.bfloat16),
            grad_value.astype(jnp.bfloat16),
        ],
        axis=1,
    )
    width = inputs.shape[1]
    sum_qv = jnp.concatenate(
        [
            jnp.sum(grad_proj[:, :width], axis=0, dtype=jnp.float32),
            jnp.sum(grad_proj[:, 2 * width :], axis=0, dtype=jnp.float32),
        ]
    )
    weight_qkv = jnp.einsum("rd,re->de", inputs, grad_proj, preferred_element_type=jnp.float32)
    grad_input = grad_first + jnp.einsum(
        "re,de->rd", grad_proj, w_qkv, preferred_element_type=jnp.float32
    )
    gains = jnp.stack([gain_first, gain_second])
    shifts = jnp.stack([shift_first, shift_second])
    return (
        grad_input,
        (
            weight_qkv,
            sum_qv,
            weight_out,
            sum_out,
            gains,
            shifts,
            weight_up,
            sum_up,
            weight_down,
            sum_down,
        ),
    )


def local(
    frames,
    w_qkv,
    b_qv,
    w_out,
    b_out,
    ln_gain,
    ln_shift,
    w_up,
    b_up,
    w_down,
    b_down,
    cotangent,
    clip_lengths,
    valid_lengths,
):
    rows = frames.shape[1]
    lengths = clip_lengths[0]
    valid = valid_lengths[0]
    offset = lax.axis_index("seq") * rows
    query_seg, key_tag = clip_tags(lengths, valid, offset, rows)
    layer_weights = [
        tuple(
            (
                array[layer_at]
                for array in (
                    w_qkv,
                    b_qv,
                    w_out,
                    b_out,
                    ln_gain,
                    ln_shift,
                    w_up,
                    b_up,
                    w_down,
                    b_down,
                )
            )
        )
        for layer_at in range(LAYERS)
    ]
    hidden = frames[0].astype(jnp.float32)
    saved = []
    for layer_at in range(LAYERS):
        hidden, kept = forward_layer(hidden, layer_weights[layer_at], query_seg, lengths, valid)
        saved.append(kept)
    activations = hidden.astype(jnp.bfloat16)[None]
    grad_hidden = cotangent[0].astype(jnp.float32)
    per_layer = [None] * LAYERS
    for layer_at in reversed(range(LAYERS)):
        grad_hidden, per_layer[layer_at] = backward_layer(
            grad_hidden, saved[layer_at], layer_weights[layer_at], query_seg, lengths, valid
        )
    stacked = [
        jnp.stack([per_layer[layer_at][member] for layer_at in range(LAYERS)])
        for member in range(10)
    ]
    g_wqkv, g_bqv, g_wout, g_bout, g_gain, g_shift, g_wup, g_bup, g_wdown, g_bdown = stacked
    shares = (
        lax.psum_scatter(
            g_wqkv.astype(jnp.bfloat16), "seq", scatter_dimension=1, tiled=True
        ).astype(jnp.float32),
        lax.psum_scatter(g_bqv.astype(jnp.bfloat16), "seq", scatter_dimension=1, tiled=True).astype(
            jnp.float32
        ),
        lax.psum_scatter(
            g_wout.astype(jnp.bfloat16), "seq", scatter_dimension=1, tiled=True
        ).astype(jnp.float32),
        lax.psum_scatter(
            g_bout.astype(jnp.bfloat16), "seq", scatter_dimension=1, tiled=True
        ).astype(jnp.float32),
        lax.psum_scatter(
            g_gain.astype(jnp.bfloat16), "seq", scatter_dimension=2, tiled=True
        ).astype(jnp.float32),
        lax.psum_scatter(
            g_shift.astype(jnp.bfloat16), "seq", scatter_dimension=2, tiled=True
        ).astype(jnp.float32),
        lax.psum_scatter(g_wup.astype(jnp.bfloat16), "seq", scatter_dimension=1, tiled=True).astype(
            jnp.float32
        ),
        lax.psum_scatter(g_bup.astype(jnp.bfloat16), "seq", scatter_dimension=1, tiled=True).astype(
            jnp.float32
        ),
        lax.psum_scatter(
            g_wdown.astype(jnp.bfloat16), "seq", scatter_dimension=1, tiled=True
        ).astype(jnp.float32),
        lax.psum_scatter(
            g_bdown.astype(jnp.bfloat16), "seq", scatter_dimension=1, tiled=True
        ).astype(jnp.float32),
    )
    s_wqkv, s_bqv, s_wout, s_bout, s_gain, s_shift, s_wup, s_bup, s_wdown, s_bdown = shares
    totals = (
        lax.psum(s_wqkv.astype(jnp.bfloat16), "bucket").astype(jnp.float32),
        lax.psum(s_bqv.astype(jnp.bfloat16), "bucket").astype(jnp.float32),
        lax.psum(s_wout.astype(jnp.bfloat16), "bucket").astype(jnp.float32),
        lax.psum(s_bout.astype(jnp.bfloat16), "bucket").astype(jnp.float32),
        lax.psum(s_gain.astype(jnp.bfloat16), "bucket").astype(jnp.float32),
        lax.psum(s_shift.astype(jnp.bfloat16), "bucket").astype(jnp.float32),
        lax.psum(s_wup.astype(jnp.bfloat16), "bucket").astype(jnp.float32),
        lax.psum(s_bup.astype(jnp.bfloat16), "bucket").astype(jnp.float32),
        lax.psum(s_wdown.astype(jnp.bfloat16), "bucket").astype(jnp.float32),
        lax.psum(s_bdown.astype(jnp.bfloat16), "bucket").astype(jnp.float32),
    )
    return (
        activations,
        grad_hidden[None],
        totals[0],
        totals[1],
        totals[2],
        totals[3],
        totals[4],
        totals[5],
        totals[6],
        totals[7],
        totals[8],
        totals[9],
    )


def solution(mesh):
    placed = (
        P("bucket", "seq", None),
        P(),
        P(),
        P(),
        P(),
        P(),
        P(),
        P(),
        P(),
        P(),
        P(),
        P("bucket", "seq", None),
        P("bucket", None),
        P("bucket", None),
    )
    chips_2x2 = mesh.shape["seq"] == 8 and mesh.shape["bucket"] == 4
    return jax.shard_map(
        fast_local if chips_2x2 else local,
        mesh=mesh,
        in_specs=placed,
        out_specs=(
            P("bucket", "seq", None),
            P("bucket", "seq", None),
            P(None, "seq", None),
            P(None, "seq"),
            P(None, "seq", None),
            P(None, "seq"),
            P(None, None, "seq"),
            P(None, None, "seq"),
            P(None, "seq", None),
            P(None, "seq"),
            P(None, "seq", None),
            P(None, "seq"),
        ),
        check_vma=False,
    )
```
